32 devices in a mesh: exp: 8 (over y, x, core), imp: 4 (over z).
Axes of the slice: x: 2, y: 2, z: 4, core: 2. Of those that a mesh axis runs over, the one named last changes fastest.
Arguments:
- flows: bfloat16 [128, 256, 256], P(('exp', 'imp')), may hold values from 0 to 8, as said below
- routing: int32 [32, 4, 1], P(('exp', 'imp')), may hold values from -1 to 3, as said below
- tile_block: int32 [128], P(('exp', 'imp')), may hold values from 0 to 7, as said below
- exp_country: int32 [4096], P('exp'), may hold values from 0 to 127, never falling along the last dimension, each value on 1 to 64 neighbouring positions
- imp_country: int32 [4096], P('imp'), may hold values from 0 to 127, never falling along the last dimension, each value on 1 to 64 neighbouring positions
Outputs:
- exporter_effects: float32 [4096], P('exp')
- importer_effects: float32 [4096], P('imp')
- pair_effects: float32 [128, 128], replicated
The draws below stay inside these ranges and needn't reach their ends.
Inputs may be any that keep to these rules, and one draw needn't show every extreme that they name: `routing`: entry [d, t, s] names a slot of device d routed to imp index t, or is -1. Each slot is named at most once. The devices of one exp index route at most 3 named slots to each imp index in all, and exactly 3 to some imp index of every exp index; each entry names at most one slot, and some entry of some device does name one; in every exp index some device names all 4 of its slots. `tile_block`: r * 4 + c for the slot's local exporter block r and local importer block c; distinct within a device. `exp_country`: never falls along the exporter-years; every country has 1 to 64 of them. `imp_country`: never falls along the importer-years; every country has 1 to 64 of them. Positive flows.
All inputs are finite; a program needn't handle non-finite values.
Results may differ from the reference program's by a relative error of at most 0.0003.
Values may be sent and summed in bfloat16 or wider, within the bound.
No kernel may reach another device: no remote copies, remote signals or barrier semaphores. Data moves between devices by JAX's collectives and lax.ppermute only.
A program may use at most 64 MiB of HBM per device.

```python
import math
import jax
import jax.numpy as jnp
import numpy as np

BS = 256
RB_DEV = 2
TS = 4
NCE = 128
NCI = 128
NEWTON = 2
CG = 2
CB_DEV = 4
TR = 3
SB = 1
TILES = 128
NA = 4096
NB = 4096
N_EXP = 8
N_IMP = 4


def route_group(group_key):
    key_extra, key_heavy, key_pick, key_slots, key_turn = jax.random.split(group_key, 5)
    extra_total = jax.random.randint(key_extra, (), 0, N_IMP)
    group_total = N_IMP * (TR - 1) + 1 + extra_total
    heavy_member = jax.random.randint(key_heavy, (), 0, N_IMP)
    spare_units = group_total - TS - (N_IMP - 1)
    places = (N_IMP - 1) * (TS - 1)
    shuffle = jax.random.permutation(key_pick, places)
    chosen = (shuffle < spare_units).astype(jnp.int32).reshape(N_IMP - 1, TS - 1)
    others = 1 + jnp.sum(chosen, axis=1)
    member = jnp.arange(N_IMP, dtype=jnp.int32)
    other_index = jnp.clip(member - (member > heavy_member).astype(jnp.int32), 0, N_IMP - 2)
    counts = jnp.where(member == heavy_member, TS, others[other_index])
    starts = jnp.cumsum(counts) - counts
    slot_keys = jax.random.split(key_slots, N_IMP)
    slot_order = jax.vmap(lambda sub_key: jax.random.permutation(sub_key, TS))(slot_keys).astype(jnp.int32)
    start_turn = jax.random.randint(key_turn, (), 0, N_IMP)
    within = jnp.arange(TS, dtype=jnp.int32)
    target = (starts[:, None] + within[None, :] + start_turn) % N_IMP
    slot_place = jnp.broadcast_to((within // N_IMP)[None, :], (N_IMP, TS))
    slot_value = jnp.where(within[None, :] < counts[:, None], slot_order, -1).astype(jnp.int32)
    sender = jnp.broadcast_to(member[:, None], (N_IMP, TS))
    send_table = jnp.full((N_IMP, N_IMP, SB), -1, jnp.int32)
    return send_table.at[sender, target, slot_place].set(slot_value)


def draw_routing(key, part):
    group_keys = jax.random.split(jax.random.fold_in(key, 11), N_EXP)
    return jax.vmap(route_group)(group_keys).reshape(N_EXP * N_IMP, N_IMP, SB)


def draw_tile_block(key, part):
    device_keys = jax.random.split(jax.random.fold_in(key, 23), N_EXP * N_IMP)
    picked = jax.vmap(lambda sub_key: jax.random.permutation(sub_key, RB_DEV * CB_DEV)[:TS])(device_keys)
    return picked.reshape(-1).astype(jnp.int32)


def draw_flows(key, part):
    key_rows, key_cols, key_cells = jax.random.split(jax.random.fold_in(key, 37), 3)
    col_scale = jnp.exp(jax.random.uniform(key_cols, (TILES, 1, BS), jnp.float32, math.log(0.5), math.log(2.0)))
    row_scale = jnp.exp(jax.random.uniform(key_rows, (TILES, BS, 1), jnp.float32, math.log(0.5), math.log(2.0)))
    cell_part = jax.random.uniform(key_cells, (TILES, BS, BS), jnp.float32, 0.5, 1.5)
    return (row_scale * col_scale * cell_part).astype(jnp.bfloat16)


def split_up(count, total, bound, slope):
    weights = [(1 << 20) // math.isqrt(rank ** slope) + 1 for rank in range(2, count + 1)]
    spare, given = total - bound - (count - 1), [1] * (count - 1)
    while spare > 0:
        candidates = [i for i in range(count - 1) if given[i] < bound]
        mass, budget = sum([weights[i] for i in candidates]), spare
        for i in candidates:
            more = min(bound - given[i], max(1, budget * weights[i] // mass), spare)
            given[i] = given[i] + more
            spare = spare - more
    return np.array([bound] + given)


def uneven_parts(rng, number_of, total, bound, slope):
    if number_of == 2:
        one = jax.random.randint(rng, (), max(1, total - bound), min(bound, total - 1) + 1)
        return jnp.stack([one, total - one])
    tallies = jnp.asarray(split_up(number_of, total, bound, slope), jnp.int32)
    couples = (number_of - 1) // 2
    source_of, taker = tallies[1:1 + 2 * couples:2], tallies[2:2 + 2 * couples:2]
    slack = jnp.minimum(source_of - 1, bound - taker)
    moved = jax.random.randint(jax.random.fold_in(rng, 1), (couples,), 0, 1 << 20) % (slack + 1)
    tallies = tallies.at[1:1 + 2 * couples:2].set(source_of - moved).at[2:2 + 2 * couples:2].set(taker + moved)
    return tallies[jax.random.permutation(jax.random.fold_in(rng, 2), number_of)]


def setup_inputs(seed: int = 0) -> dict:
    arg_keys = jax.random.split(jax.random.key(seed), 6)
    flows = draw_flows(jax.random.fold_in(arg_keys[5], 71), 0)
    routing = draw_routing(jax.random.fold_in(arg_keys[5], 71), 0)
    tile_block = draw_tile_block(jax.random.fold_in(arg_keys[5], 71), 0)
    exp_country = jnp.searchsorted(jnp.cumsum(uneven_parts(arg_keys[3], NCE, NA, 2 * NA // NCE, 1)), jnp.arange(NA), side="right").astype(jnp.int32)
    imp_country = jnp.searchsorted(jnp.cumsum(uneven_parts(arg_keys[4], NCI, NB, 2 * NB // NCI, 1)), jnp.arange(NB), side="right").astype(jnp.int32)
    return dict(flows=flows, routing=routing, tile_block=tile_block, exp_country=exp_country, imp_country=imp_country)


ridge_weight = 64.0


def combine(anchor, factor, change):
    return tuple(current + factor * addend for current, addend in zip(anchor, change))


def inner_product(left_vec, right_vec):
    return jnp.sum(left_vec[0] * right_vec[0]) + jnp.sum(left_vec[1] * right_vec[1]) + jnp.sum(left_vec[2] * right_vec[2])


def reference(flows, routing, tile_block, exp_country, imp_country):
    tile_index = jnp.arange(TILES, dtype=jnp.int32)
    device = tile_index // TS
    slot_number = tile_index % TS
    is_live = jnp.any(routing[device] == slot_number[:, None, None], axis=(1, 2))
    row_block = (device // N_IMP) * RB_DEV + tile_block // CB_DEV
    col_block = (device % N_IMP) * CB_DEV + tile_block % CB_DEV
    within = jnp.arange(BS, dtype=jnp.int32)
    row_ids = (row_block[:, None] * BS + within[None, :]).astype(jnp.int32)
    col_ids = (col_block[:, None] * BS + within[None, :]).astype(jnp.int32)
    pair_ids = (exp_country[row_ids][:, :, None] * NCI + imp_country[col_ids][:, None, :]).astype(jnp.int32)
    live_mask = is_live[:, None, None]
    observed = flows.astype(jnp.float32)

    def expand(effects):
        return effects[0][row_ids][:, :, None] + effects[1][col_ids][:, None, :] + effects[2].reshape(-1)[pair_ids]

    def collect(weighted):
        part_rows = jax.ops.segment_sum(jnp.sum(weighted, axis=2).reshape(-1), row_ids.reshape(-1), num_segments=NA)
        part_cols = jax.ops.segment_sum(jnp.sum(weighted, axis=1).reshape(-1), col_ids.reshape(-1), num_segments=NB)
        part_pairs = jax.ops.segment_sum(weighted.reshape(-1), pair_ids.reshape(-1), num_segments=NCE * NCI)
        return (part_rows, part_cols, part_pairs.reshape(NCE, NCI))

    effects = (jnp.zeros((NA,), jnp.float32), jnp.zeros((NB,), jnp.float32), jnp.zeros((NCE, NCI), jnp.float32))
    for newton in range(NEWTON):
        mean_rate = jnp.where(live_mask, jnp.exp(expand(effects)), 0.0)
        gradient = collect(jnp.where(live_mask, observed - mean_rate, 0.0))
        residual = combine(gradient, -ridge_weight, effects)
        update = tuple(jnp.zeros_like(current) for current in effects)
        direction = residual
        norm_now = inner_product(residual, residual)
        for cg_sweep in range(CG):
            image_vec = combine(collect(mean_rate * expand(direction)), ridge_weight, direction)
            step_size = norm_now / inner_product(direction, image_vec)
            update = combine(update, step_size, direction)
            residual = combine(residual, -step_size, image_vec)
            norm_next = inner_product(residual, residual)
            direction = combine(residual, norm_next / norm_now, direction)
            norm_now = norm_next
        effects = combine(effects, 1.0, update)
    return (effects[0], effects[1], effects[2])
```

```python
import functools

import jax
import jax.numpy as jnp
from jax import lax
from jax.experimental import pallas as pl
from jax.experimental.pallas import tpu as pltpu
from jax.sharding import PartitionSpec as P

NCE = 128
NCI = 128
NEWTON = 2
CG = 2
LANES = 128
RIDGE = 64.0
VMEM_BYTES = 48 * 1024 * 1024

f32 = jnp.float32
bf16 = jnp.bfloat16
i32 = jnp.int32


def iota(shape, dim):
    return lax.broadcasted_iota(i32, shape, dim)


def split(x):
    hi = x.astype(bf16).astype(f32)
    rest = x - hi
    mid = rest.astype(bf16).astype(f32)
    return hi, mid, rest - mid


def dot(x, y, cx, cy, precision=None):
    return lax.dot_general(
        x, y, (((cx,), (cy,)), ((), ())), precision=precision, preferred_element_type=f32
    )


def exact(x, y, cx, cy):
    return dot(x, y, cx, cy, lax.Precision.HIGHEST)


class Layout:
    def __init__(self, na, nb, side):
        self.na, self.nb, self.side = na, nb, side
        self.rows_at = NCE
        self.cols_at = self.rows_at + na // LANES
        self.cnt_at = self.cols_at + nb // LANES
        self.live_at = self.cnt_at + 8
        self.blocks_a, self.blocks_b = na // side, nb // side
        self.total = self.live_at + -(-self.blocks_a // 8) * 8


def local_kernel(lay, slots, where, routing, tile_block, flows, ec, ic, out):
    side = lay.side
    row_blocks = ec.shape[0]
    col_local = ic.shape[0]
    exp_place, imp_place = where[0], where[1]
    out[...] = jnp.zeros_like(out)
    per = side // LANES
    country = iota((NCE, side), 0)
    ones = jnp.ones((8, side), bf16)
    pairs = jnp.zeros((NCE, NCI), f32)
    for k in range(slots):
        r = tile_block[k] // col_local
        c = tile_block[k] % col_local
        live = routing[0, 0, 0] == k
        for t in range(routing.shape[1]):
            for s in range(routing.shape[2]):
                live = live | (routing[0, t, s] == k)
        keep = live.astype(f32)
        hot_r = (country == ec[r]).astype(f32).astype(bf16)
        hot_c = (country == ic[c]).astype(f32).astype(bf16)
        tile = flows[k] * keep.astype(bf16)
        half = dot(hot_r, tile, 1, 0)
        col_sum = jnp.sum(half, axis=0, keepdims=True)
        row_sum = dot(ones, tile, 1, 1)[0:1]
        for piece in split(half):
            pairs = pairs + dot(piece.astype(bf16), hot_c, 1, 1)
        row_at = lay.rows_at + (exp_place * row_blocks + r) * per
        col_at = lay.cols_at + (imp_place * col_local + c) * per
        for h in range(per):
            cut = slice(h * LANES, (h + 1) * LANES)
            out[pl.ds(row_at + h, 1), :] += row_sum[:, cut]
            out[pl.ds(col_at + h, 1), :] += col_sum[:, cut]
        live_row = lay.live_at + exp_place * row_blocks + r
        here = iota((1, LANES), 1) == imp_place * col_local + c
        out[pl.ds(live_row, 1), :] += jnp.where(here, keep, 0.0)
    out[0:NCE, :] = pairs
    cnt_a = jnp.zeros((8, LANES), f32)
    for r in range(row_blocks):
        cnt_a += dot(ones, (country == ec[r]).astype(f32).astype(bf16), 1, 1)
    cnt_b = jnp.zeros((8, LANES), f32)
    for c in range(col_local):
        cnt_b += dot(ones, (country == ic[c]).astype(f32).astype(bf16), 1, 1)
    cnt_a = cnt_a[0:1] * (imp_place == 0).astype(f32)
    cnt_b = cnt_b[0:1] * (exp_place == 0).astype(f32)
    out[lay.cnt_at : lay.cnt_at + 1, :] = cnt_a
    out[lay.cnt_at + 1 : lay.cnt_at + 2, :] = cnt_b


class Side:
    def __init__(self, count, n, block, hot):
        before = (iota((LANES, LANES), 0) < iota((LANES, LANES), 1)).astype(f32).astype(bf16)
        start = dot(jnp.broadcast_to(count, (8, LANES)).astype(bf16), before, 1, 0)[0:1]
        start = start.astype(i32)
        end = start + count.astype(i32)
        first = start // block
        middle = jnp.minimum(end, (first + 1) * block)
        self.lo = jnp.concatenate([start, middle], axis=1)
        self.hi = jnp.concatenate([middle, end], axis=1)
        self.block_of = jnp.concatenate([first, first + 1], axis=1)
        self.block_of = jnp.where(self.hi > self.lo, self.block_of, -1)
        self.count = (self.hi - self.lo).astype(f32)
        self.n, self.hot = n, hot
        step = block
        for j in range(n // step):
            pos = iota((step, 2 * LANES), 0) + j * step
            inside = (pos >= self.lo) & (pos < self.hi)
            hot[j * step : (j + 1) * step, :] = inside.astype(f32).astype(bf16)

    def sums(self, values):
        pieces = jnp.concatenate(split(values), axis=0).astype(bf16)
        got = dot(pieces, self.hot[...], 1, 0)
        return got[0:1] + got[1:2] + got[2:3]

    def expand(self, table):
        pieces = jnp.concatenate(split(table), axis=0).astype(bf16)
        got = dot(pieces, self.hot[...], 1, 1)
        return got[0:1] + got[1:2] + got[2:3]

    def maxima(self, values):
        lo, hi = column(self.lo.astype(f32)).astype(i32), column(self.hi.astype(f32)).astype(i32)
        best = jnp.full((2 * LANES, LANES), -jnp.inf, f32)
        for j in range(self.n // LANES):
            pos = iota((2 * LANES, LANES), 1) + j * LANES
            inside = (pos >= lo) & (pos < hi)
            best = jnp.maximum(best, jnp.where(inside, values[:, j * LANES : (j + 1) * LANES], -jnp.inf))
        best = jnp.max(best, axis=1, keepdims=True)
        best = jnp.where(hi > lo, best, 0.0)
        return best


def column(row):
    return jnp.transpose(jnp.broadcast_to(row, (8, row.shape[1])))[:, 0:1]


def as_row(col):
    return jnp.transpose(jnp.broadcast_to(col, (col.shape[0], LANES)))[0:1, :]


def fold(x):
    return (x[:NCE, :NCI] + x[:NCE, NCI:]) + (x[NCE:, :NCI] + x[NCE:, NCI:])


def tile2(x):
    wide = jnp.concatenate([x, x], axis=1)
    return jnp.concatenate([wide, wide], axis=0)


def total(x):
    return jnp.sum(jnp.sum(x, axis=0, keepdims=True), axis=1, keepdims=True)


def inner(u, v):
    return total(u[0] * v[0]) + total(u[1] * v[1]) + total(u[2] * v[2])


def lane_row(ref, at, rows):
    return jnp.concatenate([ref[at + j : at + j + 1, :] for j in range(rows)], axis=1)


def solve_kernel(lay, shared, out_a, out_b, out_g, hot_a, hot_b):
    flow = (
        lane_row(shared, lay.rows_at, lay.na // LANES),
        lane_row(shared, lay.cols_at, lay.nb // LANES),
        shared[0:NCE, :],
    )
    sa = Side(shared[lay.cnt_at : lay.cnt_at + 1, :], lay.na, lay.side, hot_a)
    sb = Side(shared[lay.cnt_at + 1 : lay.cnt_at + 2, :], lay.nb, lay.side, hot_b)
    live = shared[lay.live_at : lay.total, :].astype(bf16)
    pick_a = (iota((lay.total - lay.live_at, 2 * LANES), 0) == sa.block_of).astype(f32)
    pick_b = (iota((LANES, 2 * LANES), 0) == sb.block_of).astype(f32).astype(bf16)
    wide = dot(jnp.transpose(pick_a).astype(bf16), live, 1, 0)
    mask = dot(wide.astype(bf16), pick_b, 1, 0) > 0.5

    a = jnp.zeros((1, lay.na), f32)
    b = jnp.zeros((1, lay.nb), f32)
    g = jnp.zeros((NCE, NCI), f32)
    for newton in range(NEWTON):
        if newton == 0:
            rate = mask.astype(f32)
            pa = jnp.ones((1, lay.na), f32)
            pb = jnp.ones((1, lay.nb), f32)
            wa, wb = sa.count, sb.count
        else:
            top_a, top_b = sa.maxima(a), sb.maxima(b)
            row_a, row_b = as_row(top_a), as_row(top_b)
            rate = jnp.where(mask, jnp.exp(tile2(g) + top_a + row_b), 0.0)
            pa = jnp.exp(a - sa.expand(row_a))
            pb = jnp.exp(b - sb.expand(row_b))
            wa, wb = sa.sums(pa), sb.sums(pb)
        col_wa = column(wa)
        da = pa * sa.expand(exact(wb, rate, 1, 1))
        db = pb * sb.expand(exact(wa, rate, 1, 0))
        dg = fold(rate * (col_wa * wb))
        res = (flow[0] - da - RIDGE * a, flow[1] - db - RIDGE * b, flow[2] - dg - RIDGE * g)
        way = res
        norm = inner(res, res)
        for sweep in range(CG):
            va, vb = sa.sums(pa * way[0]), sb.sums(pb * way[1])
            bent = rate * tile2(way[2])
            ua = exact(vb, rate, 1, 1) + exact(wb, bent, 1, 1)
            ub = exact(va, rate, 1, 0) + exact(wa, bent, 1, 0)
            image = (
                (da + RIDGE) * way[0] + pa * sa.expand(ua),
                (db + RIDGE) * way[1] + pb * sb.expand(ub),
                (dg + RIDGE) * way[2] + fold(rate * (column(va) * wb + col_wa * vb)),
            )
            step = norm / inner(way, image)
            a, b, g = a + step * way[0], b + step * way[1], g + step * way[2]
            if sweep + 1 < CG:
                res = tuple(x - step * y for x, y in zip(res, image))
                fresh = inner(res, res)
                ratio = fresh / norm
                way = tuple(x + ratio * y for x, y in zip(res, way))
                norm = fresh
    out_a[...] = a
    out_b[...] = b
    out_g[...] = g


def per_device(mesh_shape, flows, routing, tile_block, exp_country, imp_country):
    slots, side = flows.shape[0], flows.shape[1]
    n_exp, n_imp = mesh_shape
    rows, cols = exp_country.shape[0], imp_country.shape[0]
    lay = Layout(rows * n_exp, cols * n_imp, side)
    exp_place = lax.axis_index("exp")
    imp_place = lax.axis_index("imp")
    where = jnp.stack([exp_place, imp_place]).astype(i32)
    smem = pl.BlockSpec(memory_space=pltpu.SMEM)
    vmem = pl.BlockSpec(memory_space=pltpu.VMEM)
    shared = pl.pallas_call(
        functools.partial(local_kernel, lay, slots),
        out_shape=jax.ShapeDtypeStruct((lay.total, LANES), f32),
        in_specs=[smem, smem, smem, vmem, vmem, vmem],
        out_specs=vmem,
        compiler_params=pltpu.CompilerParams(vmem_limit_bytes=VMEM_BYTES),
        name="local_sums",
    )(
        where,
        routing,
        tile_block,
        flows,
        exp_country.reshape(-1, 1, side),
        imp_country.reshape(-1, 1, side),
    )
    shared = lax.psum(lax.psum(shared, "imp"), "exp")
    a, b, g = pl.pallas_call(
        functools.partial(solve_kernel, lay),
        out_shape=(
            jax.ShapeDtypeStruct((1, lay.na), f32),
            jax.ShapeDtypeStruct((1, lay.nb), f32),
            jax.ShapeDtypeStruct((NCE, NCI), f32),
        ),
        in_specs=[vmem],
        out_specs=(vmem, vmem, vmem),
        scratch_shapes=[
            pltpu.VMEM((lay.na, 2 * LANES), bf16),
            pltpu.VMEM((lay.nb, 2 * LANES), bf16),
        ],
        compiler_params=pltpu.CompilerParams(vmem_limit_bytes=VMEM_BYTES),
        name="solve",
    )(shared)
    a = lax.dynamic_slice(a.reshape(-1), (exp_place * rows,), (rows,))
    b = lax.dynamic_slice(b.reshape(-1), (imp_place * cols,), (cols,))
    return a, b, g


def solution(mesh):
    placed = (
        P(("exp", "imp"), None, None),
        P(("exp", "imp"), None, None),
        P(("exp", "imp")),
        P("exp"),
        P("imp"),
    )
    return jax.shard_map(
        functools.partial(per_device, (mesh.shape["exp"], mesh.shape["imp"])),
        mesh=mesh,
        in_specs=placed,
        out_specs=(P("exp"), P("imp"), P()),
        check_vma=False,
    )
```

```python
import functools

import jax
import jax.numpy as jnp
from jax import lax
from jax.experimental import pallas as pl
from jax.experimental.pallas import tpu as pltpu
from jax.sharding import PartitionSpec as P

NCE = 128
NCI = 128
NEWTON = 2
CG = 2
LANES = 128
RIDGE = 64.0
VMEM_BYTES = 48 * 1024 * 1024

f32 = jnp.float32
bf16 = jnp.bfloat16
i32 = jnp.int32


def iota(shape, dim):
    return lax.broadcasted_iota(i32, shape, dim)


def split(x):
    hi = x.astype(bf16).astype(f32)
    rest = x - hi
    mid = rest.astype(bf16).astype(f32)
    return hi, mid, rest - mid


def dot(x, y, cx, cy, precision=None):
    return lax.dot_general(
        x, y, (((cx,), (cy,)), ((), ())), precision=precision, preferred_element_type=f32
    )


def exact(x, y, cx, cy):
    return dot(x, y, cx, cy, lax.Precision.HIGHEST)


class Layout:
    def __init__(self, na, nb, side):
        self.na, self.nb, self.side = na, nb, side
        self.rows_at = NCE
        self.cols_at = self.rows_at + na // LANES
        self.cnt_at = self.cols_at + nb // LANES
        self.live_at = self.cnt_at + 8
        self.blocks_a, self.blocks_b = na // side, nb // side
        self.total = self.live_at + -(-self.blocks_a // 8) * 8


def local_kernel(lay, slots, where, routing, tile_block, flows, ec, ic, out):
    side = lay.side
    row_blocks = ec.shape[0]
    col_local = ic.shape[0]
    exp_place, imp_place = where[0], where[1]
    out[...] = jnp.zeros_like(out)
    per = side // LANES
    country = iota((NCE, side), 0)
    ones = jnp.ones((8, side), bf16)
    pairs = jnp.zeros((NCE, NCI), f32)
    for k in range(slots):
        r = tile_block[k] // col_local
        c = tile_block[k] % col_local
        live = routing[0, 0, 0] == k
        for t in range(routing.shape[1]):
            for s in range(routing.shape[2]):
                live = live | (routing[0, t, s] == k)
        keep = live.astype(f32)
        hot_r = (country == ec[r]).astype(f32).astype(bf16)
        hot_c = (country == ic[c]).astype(f32).astype(bf16)
        tile = flows[k] * keep.astype(bf16)
        half = dot(hot_r, tile, 1, 0)
        col_sum = jnp.sum(half, axis=0, keepdims=True)
        row_sum = dot(ones, tile, 1, 1)[0:1]
        for piece in split(half):
            pairs = pairs + dot(piece.astype(bf16), hot_c, 1, 1)
        row_at = lay.rows_at + (exp_place * row_blocks + r) * per
        col_at = lay.cols_at + (imp_place * col_local + c) * per
        for h in range(per):
            cut = slice(h * LANES, (h + 1) * LANES)
            out[pl.ds(row_at + h, 1), :] += row_sum[:, cut]
            out[pl.ds(col_at + h, 1), :] += col_sum[:, cut]
        live_row = lay.live_at + exp_place * row_blocks + r
        here = iota((1, LANES), 1) == imp_place * col_local + c
        out[pl.ds(live_row, 1), :] += jnp.where(here, keep, 0.0)
    out[0:NCE, :] = pairs
    cnt_a = jnp.zeros((8, LANES), f32)
    for r in range(row_blocks):
        cnt_a += dot(ones, (country == ec[r]).astype(f32).astype(bf16), 1, 1)
    cnt_b = jnp.zeros((8, LANES), f32)
    for c in range(col_local):
        cnt_b += dot(ones, (country == ic[c]).astype(f32).astype(bf16), 1, 1)
    cnt_a = cnt_a[0:1] * (imp_place == 0).astype(f32)
    cnt_b = cnt_b[0:1] * (exp_place == 0).astype(f32)
    out[lay.cnt_at : lay.cnt_at + 1, :] = cnt_a
    out[lay.cnt_at + 1 : lay.cnt_at + 2, :] = cnt_b


class Side:
    def __init__(self, count, n, block, hot):
        before = (iota((LANES, LANES), 0) < iota((LANES, LANES), 1)).astype(f32).astype(bf16)
        start = dot(jnp.broadcast_to(count, (8, LANES)).astype(bf16), before, 1, 0)[0:1]
        start = start.astype(i32)
        end = start + count.astype(i32)
        first = start // block
        middle = jnp.minimum(end, (first + 1) * block)
        self.lo = jnp.concatenate([start, middle], axis=1)
        self.hi = jnp.concatenate([middle, end], axis=1)
        self.block_of = jnp.concatenate([first, first + 1], axis=1)
        self.block_of = jnp.where(self.hi > self.lo, self.block_of, -1)
        self.count = (self.hi - self.lo).astype(f32)
        self.n, self.hot = n, hot
        step = block
        for j in range(n // step):
            pos = iota((step, 2 * LANES), 0) + j * step
            inside = (pos >= self.lo) & (pos < self.hi)
            hot[j * step : (j + 1) * step, :] = inside.astype(f32).astype(bf16)

    def sums(self, values):
        pieces = jnp.concatenate(split(values), axis=0).astype(bf16)
        got = dot(pieces, self.hot[...], 1, 0)
        return got[0:1] + got[1:2] + got[2:3]

    def expand(self, table):
        pieces = jnp.concatenate(split(table), axis=0).astype(bf16)
        got = dot(pieces, self.hot[...], 1, 1)
        return got[0:1] + got[1:2] + got[2:3]

    def maxima(self, values):
        lo, hi = column(self.lo.astype(f32)).astype(i32), column(self.hi.astype(f32)).astype(i32)
        best = jnp.full((2 * LANES, LANES), -jnp.inf, f32)
        for j in range(self.n // LANES):
            pos = iota((2 * LANES, LANES), 1) + j * LANES
            inside = (pos >= lo) & (pos < hi)
            best = jnp.maximum(best, jnp.where(inside, values[:, j * LANES : (j + 1) * LANES], -jnp.inf))
        best = jnp.max(best, axis=1, keepdims=True)
        best = jnp.where(hi > lo, best, 0.0)
        return best


def column(row):
    return jnp.transpose(jnp.broadcast_to(row, (8, row.shape[1])))[:, 0:1]


def as_row(col):
    return jnp.transpose(jnp.broadcast_to(col, (col.shape[0], LANES)))[0:1, :]


def fold(x):
    return (x[:NCE, :NCI] + x[:NCE, NCI:]) + (x[NCE:, :NCI] + x[NCE:, NCI:])


def tile2(x):
    wide = jnp.concatenate([x, x], axis=1)
    return jnp.concatenate([wide, wide], axis=0)


def total(x):
    return jnp.sum(jnp.sum(x, axis=0, keepdims=True), axis=1, keepdims=True)


def inner(u, v):
    return total(u[0] * v[0]) + total(u[1] * v[1]) + total(u[2] * v[2])


def lane_row(ref, at, rows):
    return jnp.concatenate([ref[at + j : at + j + 1, :] for j in range(rows)], axis=1)


def solve_kernel(lay, shared, out_a, out_b, out_g, hot_a, hot_b):
    flow = (
        lane_row(shared, lay.rows_at, lay.na // LANES),
        lane_row(shared, lay.cols_at, lay.nb // LANES),
        shared[0:NCE, :],
    )
    sa = Side(shared[lay.cnt_at : lay.cnt_at + 1, :], lay.na, lay.side, hot_a)
    sb = Side(shared[lay.cnt_at + 1 : lay.cnt_at + 2, :], lay.nb, lay.side, hot_b)
    live = shared[lay.live_at : lay.total, :].astype(bf16)
    pick_a = (iota((lay.total - lay.live_at, 2 * LANES), 0) == sa.block_of).astype(f32)
    pick_b = (iota((LANES, 2 * LANES), 0) == sb.block_of).astype(f32).astype(bf16)
    wide = dot(jnp.transpose(pick_a).astype(bf16), live, 1, 0)
    mask = dot(wide.astype(bf16), pick_b, 1, 0) > 0.5

    a = jnp.zeros((1, lay.na), f32)
    b = jnp.zeros((1, lay.nb), f32)
    g = jnp.zeros((NCE, NCI), f32)
    for newton in range(NEWTON):
        if newton == 0:
            rate = mask.astype(f32)
            pa = jnp.ones((1, lay.na), f32)
            pb = jnp.ones((1, lay.nb), f32)
            wa, wb = sa.count, sb.count
        else:
            top_a, top_b = sa.maxima(a), sb.maxima(b)
            row_a, row_b = as_row(top_a), as_row(top_b)
            rate = jnp.where(mask, jnp.exp(tile2(g) + top_a + row_b), 0.0)
            pa = jnp.exp(a - sa.expand(row_a))
            pb = jnp.exp(b - sb.expand(row_b))
            wa, wb = sa.sums(pa), sb.sums(pb)
        col_wa = column(wa)
        da = pa * sa.expand(exact(wb, rate, 1, 1))
        db = pb * sb.expand(exact(wa, rate, 1, 0))
        dg = fold(rate * (col_wa * wb))
        res = (flow[0] - da - RIDGE * a, flow[1] - db - RIDGE * b, flow[2] - dg - RIDGE * g)
        way = res
        norm = inner(res, res)
        for sweep in range(CG):
            va, vb = sa.sums(pa * way[0]), sb.sums(pb * way[1])
            bent = rate * tile2(way[2])
            ua = exact(vb, rate, 1, 1) + exact(wb, bent, 1, 1)
            ub = exact(va, rate, 1, 0) + exact(wa, bent, 1, 0)
            image = (
                (da + RIDGE) * way[0] + pa * sa.expand(ua),
                (db + RIDGE) * way[1] + pb * sb.expand(ub),
                (dg + RIDGE) * way[2] + fold(rate * (column(va) * wb + col_wa * vb)),
            )
            step = norm / inner(way, image)
            a, b, g = a + step * way[0], b + step * way[1], g + step * way[2]
            if sweep + 1 < CG:
                res = tuple(x - step * y for x, y in zip(res, image))
                fresh = inner(res, res)
                ratio = fresh / norm
                way = tuple(x + ratio * y for x, y in zip(res, way))
                norm = fresh
    out_a[...] = a
    out_b[...] = b
    out_g[...] = g


def add_over(x, axis, size):
    bit = 1
    while bit < size:
        x = x + lax.ppermute(x, axis, [(d, d ^ bit) for d in range(size)])
        bit *= 2
    return x


def per_device(mesh_shape, flows, routing, tile_block, exp_country, imp_country):
    slots, side = flows.shape[0], flows.shape[1]
    n_exp, n_imp = mesh_shape
    rows, cols = exp_country.shape[0], imp_country.shape[0]
    lay = Layout(rows * n_exp, cols * n_imp, side)
    exp_place = lax.axis_index("exp")
    imp_place = lax.axis_index("imp")
    where = jnp.stack([exp_place, imp_place]).astype(i32)
    smem = pl.BlockSpec(memory_space=pltpu.SMEM)
    vmem = pl.BlockSpec(memory_space=pltpu.VMEM)
    shared = pl.pallas_call(
        functools.partial(local_kernel, lay, slots),
        out_shape=jax.ShapeDtypeStruct((lay.total, LANES), f32),
        in_specs=[smem, smem, smem, vmem, vmem, vmem],
        out_specs=vmem,
        compiler_params=pltpu.CompilerParams(vmem_limit_bytes=VMEM_BYTES),
        name="local_sums",
    )(
        where,
        routing,
        tile_block,
        flows,
        exp_country.reshape(-1, 1, side),
        imp_country.reshape(-1, 1, side),
    )
    shared = add_over(add_over(shared, "exp", n_exp), "imp", n_imp)
    a, b, g = pl.pallas_call(
        functools.partial(solve_kernel, lay),
        out_shape=(
            jax.ShapeDtypeStruct((1, lay.na), f32),
            jax.ShapeDtypeStruct((1, lay.nb), f32),
            jax.ShapeDtypeStruct((NCE, NCI), f32),
        ),
        in_specs=[vmem],
        out_specs=(vmem, vmem, vmem),
        scratch_shapes=[
            pltpu.VMEM((lay.na, 2 * LANES), bf16),
            pltpu.VMEM((lay.nb, 2 * LANES), bf16),
        ],
        compiler_params=pltpu.CompilerParams(vmem_limit_bytes=VMEM_BYTES),
        name="solve",
    )(shared)
    a = lax.dynamic_slice(a.reshape(-1), (exp_place * rows,), (rows,))
    b = lax.dynamic_slice(b.reshape(-1), (imp_place * cols,), (cols,))
    return a, b, g


def solution(mesh):
    placed = (
        P(("exp", "imp"), None, None),
        P(("exp", "imp"), None, None),
        P(("exp", "imp")),
        P("exp"),
        P("imp"),
    )
    return jax.shard_map(
        functools.partial(per_device, (mesh.shape["exp"], mesh.shape["imp"])),
        mesh=mesh,
        in_specs=placed,
        out_specs=(P("exp"), P("imp"), P()),
        check_vma=False,
    )
```

```python
import functools

import jax
import jax.numpy as jnp
from jax import lax
from jax.experimental import pallas as pl
from jax.experimental.pallas import tpu as pltpu
from jax.sharding import PartitionSpec as P

NCE = 128
NCI = 128
NEWTON = 2
CG = 2
LANES = 128
RIDGE = 64.0
VMEM_BYTES = 48 * 1024 * 1024

f32 = jnp.float32
bf16 = jnp.bfloat16
i32 = jnp.int32


def iota(shape, dim):
    return lax.broadcasted_iota(i32, shape, dim)


def split(x):
    hi = x.astype(bf16).astype(f32)
    rest = x - hi
    mid = rest.astype(bf16).astype(f32)
    return hi, mid, rest - mid


def dot(x, y, cx, cy, precision=None):
    return lax.dot_general(
        x, y, (((cx,), (cy,)), ((), ())), precision=precision, preferred_element_type=f32
    )


class Layout:
    def __init__(self, na, nb, side):
        self.na, self.nb, self.side = na, nb, side
        self.rows_at = NCE
        self.cols_at = self.rows_at + na // LANES
        self.cnt_at = self.cols_at + nb // LANES
        self.live_at = self.cnt_at + 8
        self.blocks_a, self.blocks_b = na // side, nb // side
        self.total = self.live_at + -(-self.blocks_a // 8) * 8


def local_kernel(lay, slots, where, routing, tile_block, flows, ec, ic, out):
    side = lay.side
    row_blocks = ec.shape[0]
    col_local = ic.shape[0]
    exp_place, imp_place = where[0], where[1]
    out[...] = jnp.zeros_like(out)
    per = side // LANES
    country = iota((NCE, side), 0)
    ones = jnp.ones((8, side), bf16)
    pairs = jnp.zeros((NCE, NCI), f32)
    for k in range(slots):
        r = tile_block[k] // col_local
        c = tile_block[k] % col_local
        live = routing[0, 0, 0] == k
        for t in range(routing.shape[1]):
            for s in range(routing.shape[2]):
                live = live | (routing[0, t, s] == k)
        keep = live.astype(f32)
        hot_r = (country == ec[r]).astype(f32).astype(bf16)
        hot_c = (country == ic[c]).astype(f32).astype(bf16)
        tile = flows[k] * keep.astype(bf16)
        half = dot(hot_r, tile, 1, 0)
        col_sum = jnp.sum(half, axis=0, keepdims=True)
        row_sum = dot(ones, tile, 1, 1)[0:1]
        for piece in split(half):
            pairs = pairs + dot(piece.astype(bf16), hot_c, 1, 1)
        row_at = lay.rows_at + (exp_place * row_blocks + r) * per
        col_at = lay.cols_at + (imp_place * col_local + c) * per
        for h in range(per):
            cut = slice(h * LANES, (h + 1) * LANES)
            out[pl.ds(row_at + h, 1), :] += row_sum[:, cut]
            out[pl.ds(col_at + h, 1), :] += col_sum[:, cut]
        live_row = lay.live_at + exp_place * row_blocks + r
        here = iota((1, LANES), 1) == imp_place * col_local + c
        out[pl.ds(live_row, 1), :] += jnp.where(here, keep, 0.0)
    out[0:NCE, :] = pairs
    cnt_a = jnp.zeros((8, LANES), f32)
    for r in range(row_blocks):
        cnt_a += dot(ones, (country == ec[r]).astype(f32).astype(bf16), 1, 1)
    cnt_b = jnp.zeros((8, LANES), f32)
    for c in range(col_local):
        cnt_b += dot(ones, (country == ic[c]).astype(f32).astype(bf16), 1, 1)
    cnt_a = cnt_a[0:1] * (imp_place == 0).astype(f32)
    cnt_b = cnt_b[0:1] * (exp_place == 0).astype(f32)
    out[lay.cnt_at : lay.cnt_at + 1, :] = cnt_a
    out[lay.cnt_at + 1 : lay.cnt_at + 2, :] = cnt_b


def lookup(row, index):
    return jnp.take_along_axis(
        jnp.broadcast_to(row, index.shape), index, axis=1, mode="promise_in_bounds"
    )


def down(row):
    return jnp.transpose(jnp.broadcast_to(row, (LANES, LANES)))


def across(x):
    return jnp.sum(jnp.transpose(x), axis=0, keepdims=True)


def below(x):
    return jnp.sum(x, axis=0, keepdims=True)


def eights(x):
    return functools.reduce(lambda u, v: u + v, [x[j : j + 8] for j in range(0, x.shape[0], 8)])


def inner(u, v):
    partial = eights(u[0] * v[0]) + eights(u[1] * v[1]) + eights(u[2] * v[2])
    return jnp.sum(below(partial), axis=1, keepdims=True)


class Side:
    def __init__(self, n, block, start, middle, end, hot, stage):
        self.n, self.block, self.hot, self.stage = n, block, hot, stage
        self.chunks = n // LANES
        shape = (self.chunks, LANES)
        place = (iota(shape, 0) * LANES + iota(shape, 1)).astype(f32)
        country = jnp.zeros(shape, i32)
        jump = LANES // 2
        while jump:
            passed = lookup(end, country + (jump - 1)) <= place
            country = jnp.where(passed, country + jump, country)
            jump //= 2
        self.country = country
        self.second = place >= lookup(middle, country)
        for j in range(n // block):
            at = (iota((block, LANES), 0) + j * block).astype(f32)
            inside = (at >= start) & (at < end)
            hot[j * block : (j + 1) * block, :] = jnp.where(inside, 1.0, 0.0).astype(bf16)

    def expand(self, first, second):
        return jnp.where(self.second, lookup(second, self.country), lookup(first, self.country))

    def sums(self, vectors):
        chunks, stage = self.chunks, self.stage
        for k, v in enumerate(vectors):
            stage[2 * k * chunks : (2 * k + 1) * chunks, :] = jnp.where(self.second, 0.0, v)
            stage[(2 * k + 1) * chunks : (2 * k + 2) * chunks, :] = jnp.where(self.second, v, 0.0)
        high = -(-2 * len(vectors) // 8) * 8
        for k in range(2 * len(vectors), high):
            stage[k * chunks : (k + 1) * chunks, :] = jnp.zeros((chunks, LANES), f32)
        got = jnp.zeros((3 * high, LANES), f32)
        per = self.block // LANES
        for j in range(chunks // per):
            left = jnp.concatenate(
                [stage[pl.ds(j * per + h, high, stride=chunks), :] for h in range(per)], axis=1
            )
            pieces = jnp.concatenate(split(left), axis=0).astype(bf16)
            got += dot(pieces, self.hot[j * self.block : (j + 1) * self.block, :], 1, 0)
        return got[:high] + got[high : 2 * high] + got[2 * high :]

    def maxima(self, values_ref, low, high):
        low, high = down(low), down(high)

        def body(j, best):
            at = (iota((LANES, LANES), 1) + j * LANES).astype(f32)
            inside = (at >= low) & (at < high)
            return jnp.maximum(best, jnp.where(inside, values_ref[pl.ds(j, 1), :], -jnp.inf))

        best = lax.fori_loop(0, self.chunks, body, jnp.full((LANES, LANES), -jnp.inf, f32))
        best = jnp.max(jnp.transpose(best), axis=0, keepdims=True)
        return jnp.where(best > -jnp.inf, best, 0.0)


def solve_kernel(lay, where, shared, out_a, out_b, out_g, hot_a, hot_b, stage_a, stage_b, val_a, val_b, shift_ref):
    flow = (
        shared[lay.rows_at : lay.cols_at, :],
        shared[lay.cols_at : lay.cnt_at, :],
        shared[0:NCE, :],
    )
    side = lay.side
    tally = shared[lay.cnt_at : lay.cnt_at + 8, :]
    before = jnp.where(iota((LANES, LANES), 0) < iota((LANES, LANES), 1), 1.0, 0.0).astype(bf16)
    start = dot(tally.astype(bf16), before, 1, 0)
    end = start + tally
    first = jnp.floor((start + 0.5) * (1.0 / side))
    middle = jnp.minimum(end, (first + 1.0) * side)

    def table(x, y):
        return jnp.concatenate([x[0:1], y[0:1], x[1:2], y[1:2]], axis=0)

    low, high = table(start, middle), table(middle, end)
    count = high - low
    full = count > 0.5
    inv_count = jnp.where(full, 1.0 / jnp.maximum(count, 1.0), 0.0)
    block_of = jnp.where(full, table(first, first + 1.0), -1.0)
    sa = Side(lay.na, side, start[0:1], middle[0:1], end[0:1], hot_a, stage_a)
    sb = Side(lay.nb, side, start[1:2], middle[1:2], end[1:2], hot_b, stage_b)

    live = shared[lay.live_at : lay.total, :].astype(bf16)
    height = lay.total - lay.live_at
    number = iota((LANES, LANES), 1).astype(f32)
    pick_a = [jnp.where(down(block_of[p : p + 1]) == number, 1.0, 0.0).astype(bf16) for p in (0, 1)]
    number = iota((LANES, LANES), 0).astype(f32)
    pick_b = [jnp.where(block_of[q : q + 1] == number, 1.0, 0.0).astype(bf16) for q in (2, 3)]
    wide = [dot(pick[:, :height], live, 1, 0).astype(bf16) for pick in pick_a]
    mask = [[dot(wide[p], pick_b[q], 1, 0) for q in (0, 1)] for p in (0, 1)]

    a = jnp.zeros((lay.na // LANES, LANES), f32)
    b = jnp.zeros((lay.nb // LANES, LANES), f32)
    g = jnp.zeros((NCE, NCI), f32)
    mean = jnp.zeros((4, LANES), f32)
    for newton in range(NEWTON):
        if newton == 0:
            left = flow
            weight, inv, rate = count, inv_count, mask
            sum_a, sum_b = sa.sums([flow[0]]), sb.sums([flow[1]])
            part_a, part_b = sa.expand(inv[0:1], inv[1:2]), sb.expand(inv[2:3], inv[3:4])
            m2, m3 = inv, inv * inv
            f1 = jnp.concatenate([sum_a[0:2], sum_b[0:2]], axis=0) * inv
            f2 = f1 * inv
        else:
            left = (flow[0] - RIDGE * a, flow[1] - RIDGE * b, flow[2] - RIDGE * g)
            shift_ref[0:4, :] = mean
            off_a = a - sa.expand(mean[0:1], mean[1:2])
            off_b = b - sb.expand(mean[2:3], mean[3:4])
            worst = jnp.maximum(jnp.max(off_a), jnp.max(off_b))
            val_a[...] = a
            val_b[...] = b

            @pl.when(worst > 20.0)
            def _():
                shift_ref[0:1, :] = sa.maxima(val_a, low[0:1], high[0:1])
                shift_ref[1:2, :] = sa.maxima(val_a, low[1:2], high[1:2])
                shift_ref[2:3, :] = sb.maxima(val_b, low[2:3], high[2:3])
                shift_ref[3:4, :] = sb.maxima(val_b, low[3:4], high[3:4])

            shift = shift_ref[0:4, :]
            size_a = jnp.exp(a - sa.expand(shift[0:1], shift[1:2]))
            size_b = jnp.exp(b - sb.expand(shift[2:3], shift[3:4]))

            def moments(s, x, f):
                return s.sums([x, x * x, x * x * x, x * f, x * x * f])

            sum_a, sum_b = moments(sa, size_a, left[0]), moments(sb, size_b, left[1])
            got = [jnp.concatenate([sum_a[2 * k : 2 * k + 2], sum_b[2 * k : 2 * k + 2]], axis=0) for k in range(5)]
            weight = got[0]
            inv = jnp.where(full, 1.0 / jnp.where(full, weight, 1.0), 0.0)
            part_a = size_a * sa.expand(inv[0:1], inv[1:2])
            part_b = size_b * sb.expand(inv[2:3], inv[3:4])
            inv2 = inv * inv
            m2, m3 = got[1] * inv2, got[2] * (inv2 * inv)
            f1, f2 = got[3] * inv, got[4] * inv2
            lift = [g + down(shift[p : p + 1]) for p in (0, 1)]
            rate = [
                [jnp.where(mask[p][q] > 0.5, jnp.exp(lift[p] + shift[2 + q : 3 + q]), 0.0) for q in (0, 1)]
                for p in (0, 1)
            ]
        tall = [down(weight[p : p + 1]) for p in (0, 1)]
        mu = [[rate[p][q] * (tall[p] * weight[2 + q : 3 + q]) for q in (0, 1)] for p in (0, 1)]
        mu_a = [mu[p][0] + mu[p][1] for p in (0, 1)]
        mu_b = [mu[0][q] + mu[1][q] for q in (0, 1)]
        whole = jnp.concatenate([across(mu_a[0]), across(mu_a[1]), below(mu_b[0]), below(mu_b[1])], axis=0)
        da = part_a * sa.expand(whole[0:1], whole[1:2])
        db = part_b * sb.expand(whole[2:3], whole[3:4])
        res = (left[0] - da, left[1] - db, left[2] - (mu_a[0] + mu_a[1]))
        way = res
        norm = inner(res, res)
        v = f1 - whole * m2
        w = f2 - whole * m3
        for sweep in range(CG):
            tall = [down(v[p : p + 1]) for p in (0, 1)]
            flat = [v[2 + q : 3 + q] for q in (0, 1)]
            ga = [mu[p][0] * flat[0] + mu[p][1] * flat[1] + way[2] * mu_a[p] for p in (0, 1)]
            gb = [mu[0][q] * tall[0] + mu[1][q] * tall[1] + way[2] * mu_b[q] for q in (0, 1)]
            u = jnp.concatenate([across(ga[0]), across(ga[1]), below(gb[0]), below(gb[1])], axis=0)
            image = (
                (da + RIDGE) * way[0] + part_a * sa.expand(u[0:1], u[1:2]),
                (db + RIDGE) * way[1] + part_b * sb.expand(u[2:3], u[3:4]),
                RIDGE * way[2] + (ga[0] + ga[1]) + (tall[0] * mu_a[0] + tall[1] * mu_a[1]),
            )
            step = norm / inner(way, image)
            a, b, g = a + step * way[0], b + step * way[1], g + step * way[2]
            if newton + 1 < NEWTON:
                mean = mean + step * v
            if sweep + 1 < CG:
                res = tuple(x - step * y for x, y in zip(res, image))
                fresh = inner(res, res)
                ratio = fresh / norm
                way = tuple(x + ratio * y for x, y in zip(res, way))
                norm = fresh
                v = v - step * (whole * w + RIDGE * v + u * m2) + ratio * v
    out_g[...] = g
    val_a[...] = a
    val_b[...] = b
    for out, val, at in ((out_a, val_a, where[0]), (out_b, val_b, where[1])):
        rows = out.shape[0] // LANES
        for j in range(rows):
            out[j * LANES : (j + 1) * LANES] = val[pl.ds(at * rows + j, 1), :].reshape(LANES)


def add_over(x, axis, size):
    bit = 1
    while bit < size:
        x = x + lax.ppermute(x, axis, [(d, d ^ bit) for d in range(size)])
        bit *= 2
    return x


def per_device(mesh_shape, flows, routing, tile_block, exp_country, imp_country):
    slots, side = flows.shape[0], flows.shape[1]
    n_exp, n_imp = mesh_shape
    rows, cols = exp_country.shape[0], imp_country.shape[0]
    lay = Layout(rows * n_exp, cols * n_imp, side)
    exp_place = lax.axis_index("exp")
    imp_place = lax.axis_index("imp")
    where = jnp.stack([exp_place, imp_place]).astype(i32)
    smem = pl.BlockSpec(memory_space=pltpu.SMEM)
    vmem = pl.BlockSpec(memory_space=pltpu.VMEM)
    shared = pl.pallas_call(
        functools.partial(local_kernel, lay, slots),
        out_shape=jax.ShapeDtypeStruct((lay.total, LANES), f32),
        in_specs=[smem, smem, smem, vmem, vmem, vmem],
        out_specs=vmem,
        compiler_params=pltpu.CompilerParams(vmem_limit_bytes=VMEM_BYTES),
        name="local_sums",
    )(
        where,
        routing,
        tile_block,
        flows,
        exp_country.reshape(-1, 1, side),
        imp_country.reshape(-1, 1, side),
    )
    shared = add_over(add_over(shared, "exp", n_exp), "imp", n_imp)
    high = 16
    a, b, g = pl.pallas_call(
        functools.partial(solve_kernel, lay),
        out_shape=(
            jax.ShapeDtypeStruct((rows,), f32),
            jax.ShapeDtypeStruct((cols,), f32),
            jax.ShapeDtypeStruct((NCE, NCI), f32),
        ),
        in_specs=[smem, vmem],
        out_specs=(vmem, vmem, vmem),
        scratch_shapes=[
            pltpu.VMEM((lay.na, LANES), bf16),
            pltpu.VMEM((lay.nb, LANES), bf16),
            pltpu.VMEM((high * lay.na // LANES, LANES), f32),
            pltpu.VMEM((high * lay.nb // LANES, LANES), f32),
            pltpu.VMEM((lay.na // LANES, LANES), f32),
            pltpu.VMEM((lay.nb // LANES, LANES), f32),
            pltpu.VMEM((8, LANES), f32),
        ],
        compiler_params=pltpu.CompilerParams(vmem_limit_bytes=VMEM_BYTES),
        name="solve",
    )(where, shared)
    return a, b, g


def solution(mesh):
    placed = (
        P(("exp", "imp"), None, None),
        P(("exp", "imp"), None, None),
        P(("exp", "imp")),
        P("exp"),
        P("imp"),
    )
    return jax.shard_map(
        functools.partial(per_device, (mesh.shape["exp"], mesh.shape["imp"])),
        mesh=mesh,
        in_specs=placed,
        out_specs=(P("exp"), P("imp"), P()),
        check_vma=False,
    )
```

```python
import functools

import jax
import jax.numpy as jnp
from jax import lax
from jax.experimental import pallas as pl
from jax.experimental.pallas import tpu as pltpu
from jax.sharding import PartitionSpec as P

NCE = 128
NCI = 128
NEWTON = 2
CG = 2
LANES = 128
RIDGE = 64.0
VMEM_BYTES = 48 * 1024 * 1024

f32 = jnp.float32
bf16 = jnp.bfloat16
i32 = jnp.int32


def iota(shape, dim):
    return lax.broadcasted_iota(i32, shape, dim)


def split(x):
    hi = x.astype(bf16).astype(f32)
    rest = x - hi
    mid = rest.astype(bf16).astype(f32)
    return hi, mid, rest - mid


def dot(x, y, cx, cy, precision=None):
    return lax.dot_general(
        x, y, (((cx,), (cy,)), ((), ())), precision=precision, preferred_element_type=f32
    )


class Layout:
    def __init__(self, na, nb, side, shares):
        self.na, self.nb, self.side, self.shares = na, nb, side, shares
        self.rows_at = NCE
        self.cols_at = self.rows_at + na // LANES
        self.cnt_at = self.cols_at + nb // LANES
        self.live_at = self.cnt_at + 8
        self.blocks_a, self.blocks_b = na // side, nb // side
        self.total = self.live_at + -(-self.blocks_a // 8) * 8
        self.share = -(-self.total // (8 * shares)) * 8
        self.padded = self.share * shares


def local_kernel(lay, slots, where, routing, tile_block, flows, ec, ic, *rest):
    outs, out = rest[:-1], rest[-1]
    side = lay.side
    row_blocks = ec.shape[0]
    col_local = ic.shape[0]
    exp_place, imp_place = where[0], where[1]
    out[...] = jnp.zeros_like(out)
    per = side // LANES
    country = iota((NCE, side), 0)
    ones = jnp.ones((8, side), bf16)
    pairs = jnp.zeros((NCE, NCI), f32)
    for k in range(slots):
        r = tile_block[k] // col_local
        c = tile_block[k] % col_local
        live = routing[0, 0, 0] == k
        for t in range(routing.shape[1]):
            for s in range(routing.shape[2]):
                live = live | (routing[0, t, s] == k)
        keep = live.astype(f32)
        hot_r = (country == ec[r]).astype(f32).astype(bf16)
        hot_c = (country == ic[c]).astype(f32).astype(bf16)
        tile = flows[k] * keep.astype(bf16)
        half = dot(hot_r, tile, 1, 0)
        col_sum = jnp.sum(half, axis=0, keepdims=True)
        row_sum = dot(ones, tile, 1, 1)[0:1]
        for piece in split(half):
            pairs = pairs + dot(piece.astype(bf16), hot_c, 1, 1)
        row_at = lay.rows_at + (exp_place * row_blocks + r) * per
        col_at = lay.cols_at + (imp_place * col_local + c) * per
        for h in range(per):
            cut = slice(h * LANES, (h + 1) * LANES)
            out[pl.ds(row_at + h, 1), :] += row_sum[:, cut]
            out[pl.ds(col_at + h, 1), :] += col_sum[:, cut]
        live_row = lay.live_at + exp_place * row_blocks + r
        here = iota((1, LANES), 1) == imp_place * col_local + c
        out[pl.ds(live_row, 1), :] += jnp.where(here, keep, 0.0)
    out[0:NCE, :] = pairs
    cnt_a = jnp.zeros((8, LANES), f32)
    for r in range(row_blocks):
        cnt_a += dot(ones, (country == ec[r]).astype(f32).astype(bf16), 1, 1)
    cnt_b = jnp.zeros((8, LANES), f32)
    for c in range(col_local):
        cnt_b += dot(ones, (country == ic[c]).astype(f32).astype(bf16), 1, 1)
    cnt_a = cnt_a[0:1] * (imp_place == 0).astype(f32)
    cnt_b = cnt_b[0:1] * (exp_place == 0).astype(f32)
    out[lay.cnt_at : lay.cnt_at + 1, :] = cnt_a
    out[lay.cnt_at + 1 : lay.cnt_at + 2, :] = cnt_b
    for k, part in enumerate(outs):
        part[...] = out[pl.ds(pl.multiple_of((exp_place ^ k) * lay.share, 8), lay.share), :]


def lookup(row, index):
    return jnp.take_along_axis(
        jnp.broadcast_to(row, index.shape), index, axis=1, mode="promise_in_bounds"
    )


def down(row):
    return jnp.transpose(jnp.broadcast_to(row, (LANES, LANES)))


def across(x):
    return jnp.sum(jnp.transpose(x), axis=0, keepdims=True)


def below(x):
    return jnp.sum(x, axis=0, keepdims=True)


def eights(x):
    return functools.reduce(lambda u, v: u + v, [x[j : j + 8] for j in range(0, x.shape[0], 8)])


def inner(u, v):
    partial = eights(u[0] * v[0]) + eights(u[1] * v[1]) + eights(u[2] * v[2])
    return jnp.sum(below(partial), axis=1, keepdims=True)


class Side:
    def __init__(self, n, block, start, middle, end, hot, stage):
        self.n, self.block, self.hot, self.stage = n, block, hot, stage
        self.chunks = n // LANES
        shape = (self.chunks, LANES)
        place = (iota(shape, 0) * LANES + iota(shape, 1)).astype(f32)
        country = jnp.zeros(shape, i32)
        jump = LANES // 2
        while jump:
            passed = lookup(end, country + (jump - 1)) <= place
            country = jnp.where(passed, country + jump, country)
            jump //= 2
        self.country = country
        self.second = place >= lookup(middle, country)
        for j in range(n // block):
            at = (iota((block, LANES), 0) + j * block).astype(f32)
            inside = (at >= start) & (at < end)
            hot[j * block : (j + 1) * block, :] = jnp.where(inside, 1.0, 0.0).astype(bf16)

    def expand(self, first, second):
        return jnp.where(self.second, lookup(second, self.country), lookup(first, self.country))

    def sums(self, vectors):
        chunks, stage = self.chunks, self.stage
        for k, v in enumerate(vectors):
            stage[2 * k * chunks : (2 * k + 1) * chunks, :] = jnp.where(self.second, 0.0, v)
            stage[(2 * k + 1) * chunks : (2 * k + 2) * chunks, :] = jnp.where(self.second, v, 0.0)
        high = -(-2 * len(vectors) // 8) * 8
        for k in range(2 * len(vectors), high):
            stage[k * chunks : (k + 1) * chunks, :] = jnp.zeros((chunks, LANES), f32)
        got = jnp.zeros((3 * high, LANES), f32)
        per = self.block // LANES
        for j in range(chunks // per):
            left = jnp.concatenate(
                [stage[pl.ds(j * per + h, high, stride=chunks), :] for h in range(per)], axis=1
            )
            pieces = jnp.concatenate(split(left), axis=0).astype(bf16)
            got += dot(pieces, self.hot[j * self.block : (j + 1) * self.block, :], 1, 0)
        return got[:high] + got[high : 2 * high] + got[2 * high :]

    def maxima(self, values_ref, low, high):
        low, high = down(low), down(high)

        def body(j, best):
            at = (iota((LANES, LANES), 1) + j * LANES).astype(f32)
            inside = (at >= low) & (at < high)
            return jnp.maximum(best, jnp.where(inside, values_ref[pl.ds(j, 1), :], -jnp.inf))

        best = lax.fori_loop(0, self.chunks, body, jnp.full((LANES, LANES), -jnp.inf, f32))
        best = jnp.max(jnp.transpose(best), axis=0, keepdims=True)
        return jnp.where(best > -jnp.inf, best, 0.0)


def solve_kernel(lay, where, *refs):
    shares, refs = refs[: lay.shares], refs[lay.shares :]
    out_a, out_b, out_g, shared, hot_a, hot_b, stage_a, stage_b, val_a, val_b, shift_ref = refs
    for k, part in enumerate(shares):
        shared[pl.ds(pl.multiple_of((where[0] ^ k) * lay.share, 8), lay.share), :] = part[...]
    flow = (
        shared[lay.rows_at : lay.cols_at, :],
        shared[lay.cols_at : lay.cnt_at, :],
        shared[0:NCE, :],
    )
    side = lay.side
    tally = shared[lay.cnt_at : lay.cnt_at + 8, :]
    before = jnp.where(iota((LANES, LANES), 0) < iota((LANES, LANES), 1), 1.0, 0.0).astype(bf16)
    start = dot(tally.astype(bf16), before, 1, 0)
    end = start + tally
    first = jnp.floor((start + 0.5) * (1.0 / side))
    middle = jnp.minimum(end, (first + 1.0) * side)

    def table(x, y):
        return jnp.concatenate([x[0:1], y[0:1], x[1:2], y[1:2]], axis=0)

    low, high = table(start, middle), table(middle, end)
    count = high - low
    full = count > 0.5
    inv_count = jnp.where(full, 1.0 / jnp.maximum(count, 1.0), 0.0)
    block_of = jnp.where(full, table(first, first + 1.0), -1.0)
    sa = Side(lay.na, side, start[0:1], middle[0:1], end[0:1], hot_a, stage_a)
    sb = Side(lay.nb, side, start[1:2], middle[1:2], end[1:2], hot_b, stage_b)

    live = shared[lay.live_at : lay.total, :].astype(bf16)
    height = lay.total - lay.live_at
    number = iota((LANES, LANES), 1).astype(f32)
    pick_a = [jnp.where(down(block_of[p : p + 1]) == number, 1.0, 0.0).astype(bf16) for p in (0, 1)]
    number = iota((LANES, LANES), 0).astype(f32)
    pick_b = [jnp.where(block_of[q : q + 1] == number, 1.0, 0.0).astype(bf16) for q in (2, 3)]
    wide = [dot(pick[:, :height], live, 1, 0).astype(bf16) for pick in pick_a]
    mask = [[dot(wide[p], pick_b[q], 1, 0) for q in (0, 1)] for p in (0, 1)]

    a = jnp.zeros((lay.na // LANES, LANES), f32)
    b = jnp.zeros((lay.nb // LANES, LANES), f32)
    g = jnp.zeros((NCE, NCI), f32)
    mean = jnp.zeros((4, LANES), f32)
    for newton in range(NEWTON):
        if newton == 0:
            left = flow
            weight, inv, rate = count, inv_count, mask
            sum_a, sum_b = sa.sums([flow[0]]), sb.sums([flow[1]])
            part_a, part_b = sa.expand(inv[0:1], inv[1:2]), sb.expand(inv[2:3], inv[3:4])
            m2, m3 = inv, inv * inv
            f1 = jnp.concatenate([sum_a[0:2], sum_b[0:2]], axis=0) * inv
            f2 = f1 * inv
        else:
            left = (flow[0] - RIDGE * a, flow[1] - RIDGE * b, flow[2] - RIDGE * g)
            shift_ref[0:4, :] = mean
            off_a = a - sa.expand(mean[0:1], mean[1:2])
            off_b = b - sb.expand(mean[2:3], mean[3:4])
            worst = jnp.maximum(jnp.max(off_a), jnp.max(off_b))
            val_a[...] = a
            val_b[...] = b

            @pl.when(worst > 20.0)
            def _():
                shift_ref[0:1, :] = sa.maxima(val_a, low[0:1], high[0:1])
                shift_ref[1:2, :] = sa.maxima(val_a, low[1:2], high[1:2])
                shift_ref[2:3, :] = sb.maxima(val_b, low[2:3], high[2:3])
                shift_ref[3:4, :] = sb.maxima(val_b, low[3:4], high[3:4])

            shift = shift_ref[0:4, :]
            size_a = jnp.exp(a - sa.expand(shift[0:1], shift[1:2]))
            size_b = jnp.exp(b - sb.expand(shift[2:3], shift[3:4]))

            def moments(s, x, f):
                return s.sums([x, x * x, x * x * x, x * f, x * x * f])

            sum_a, sum_b = moments(sa, size_a, left[0]), moments(sb, size_b, left[1])
            got = [jnp.concatenate([sum_a[2 * k : 2 * k + 2], sum_b[2 * k : 2 * k + 2]], axis=0) for k in range(5)]
            weight = got[0]
            inv = jnp.where(full, 1.0 / jnp.where(full, weight, 1.0), 0.0)
            part_a = size_a * sa.expand(inv[0:1], inv[1:2])
            part_b = size_b * sb.expand(inv[2:3], inv[3:4])
            inv2 = inv * inv
            m2, m3 = got[1] * inv2, got[2] * (inv2 * inv)
            f1, f2 = got[3] * inv, got[4] * inv2
            lift = [g + down(shift[p : p + 1]) for p in (0, 1)]
            rate = [
                [jnp.where(mask[p][q] > 0.5, jnp.exp(lift[p] + shift[2 + q : 3 + q]), 0.0) for q in (0, 1)]
                for p in (0, 1)
            ]
        tall = [down(weight[p : p + 1]) for p in (0, 1)]
        mu = [[rate[p][q] * (tall[p] * weight[2 + q : 3 + q]) for q in (0, 1)] for p in (0, 1)]
        mu_a = [mu[p][0] + mu[p][1] for p in (0, 1)]
        mu_b = [mu[0][q] + mu[1][q] for q in (0, 1)]
        whole = jnp.concatenate([across(mu_a[0]), across(mu_a[1]), below(mu_b[0]), below(mu_b[1])], axis=0)
        da = part_a * sa.expand(whole[0:1], whole[1:2])
        db = part_b * sb.expand(whole[2:3], whole[3:4])
        res = (left[0] - da, left[1] - db, left[2] - (mu_a[0] + mu_a[1]))
        way = res
        norm = inner(res, res)
        v = f1 - whole * m2
        w = f2 - whole * m3
        for sweep in range(CG):
            tall = [down(v[p : p + 1]) for p in (0, 1)]
            flat = [v[2 + q : 3 + q] for q in (0, 1)]
            ga = [mu[p][0] * flat[0] + mu[p][1] * flat[1] + way[2] * mu_a[p] for p in (0, 1)]
            gb = [mu[0][q] * tall[0] + mu[1][q] * tall[1] + way[2] * mu_b[q] for q in (0, 1)]
            u = jnp.concatenate([across(ga[0]), across(ga[1]), below(gb[0]), below(gb[1])], axis=0)
            image = (
                (da + RIDGE) * way[0] + part_a * sa.expand(u[0:1], u[1:2]),
                (db + RIDGE) * way[1] + part_b * sb.expand(u[2:3], u[3:4]),
                RIDGE * way[2] + (ga[0] + ga[1]) + (tall[0] * mu_a[0] + tall[1] * mu_a[1]),
            )
            step = norm / inner(way, image)
            a, b, g = a + step * way[0], b + step * way[1], g + step * way[2]
            if newton + 1 < NEWTON:
                mean = mean + step * v
            if sweep + 1 < CG:
                res = tuple(x - step * y for x, y in zip(res, image))
                fresh = inner(res, res)
                ratio = fresh / norm
                way = tuple(x + ratio * y for x, y in zip(res, way))
                norm = fresh
                v = v - step * (whole * w + RIDGE * v + u * m2) + ratio * v
    out_g[...] = g
    val_a[...] = a
    val_b[...] = b
    for out, val, at in ((out_a, val_a, where[0]), (out_b, val_b, where[1])):
        rows = out.shape[0] // LANES
        for j in range(rows):
            out[j * LANES : (j + 1) * LANES] = val[pl.ds(at * rows + j, 1), :].reshape(LANES)


def swap(x, axis, size, bits):
    return lax.ppermute(x, axis, [(d, d ^ bits) for d in range(size)])


def add_all(xs):
    return functools.reduce(lambda u, v: u + v, xs)


def per_device(mesh_shape, flows, routing, tile_block, exp_country, imp_country):
    slots, side = flows.shape[0], flows.shape[1]
    n_exp, n_imp = mesh_shape
    rows, cols = exp_country.shape[0], imp_country.shape[0]
    lay = Layout(rows * n_exp, cols * n_imp, side, n_exp)
    exp_place = lax.axis_index("exp")
    imp_place = lax.axis_index("imp")
    where = jnp.stack([exp_place, imp_place]).astype(i32)
    smem = pl.BlockSpec(memory_space=pltpu.SMEM)
    vmem = pl.BlockSpec(memory_space=pltpu.VMEM)
    parts = pl.pallas_call(
        functools.partial(local_kernel, lay, slots),
        out_shape=[jax.ShapeDtypeStruct((lay.share, LANES), f32)] * n_exp,
        in_specs=[smem, smem, smem, vmem, vmem, vmem],
        out_specs=[vmem] * n_exp,
        scratch_shapes=[pltpu.VMEM((lay.padded, LANES), f32)],
        compiler_params=pltpu.CompilerParams(vmem_limit_bytes=VMEM_BYTES),
        name="local_sums",
    )(
        where,
        routing,
        tile_block,
        flows,
        exp_country.reshape(-1, 1, side),
        imp_country.reshape(-1, 1, side),
    )
    mine = add_all([parts[0]] + [swap(parts[k], "exp", n_exp, k) for k in range(1, n_exp)])
    mine = add_all([mine] + [swap(mine, "imp", n_imp, k) for k in range(1, n_imp)])
    shares = [mine] + [swap(mine, "exp", n_exp, k) for k in range(1, n_exp)]
    high = 16
    a, b, g = pl.pallas_call(
        functools.partial(solve_kernel, lay),
        out_shape=(
            jax.ShapeDtypeStruct((rows,), f32),
            jax.ShapeDtypeStruct((cols,), f32),
            jax.ShapeDtypeStruct((NCE, NCI), f32),
        ),
        in_specs=[smem] + [vmem] * n_exp,
        out_specs=(vmem, vmem, vmem),
        scratch_shapes=[
            pltpu.VMEM((lay.padded, LANES), f32),
            pltpu.VMEM((lay.na, LANES), bf16),
            pltpu.VMEM((lay.nb, LANES), bf16),
            pltpu.VMEM((high * lay.na // LANES, LANES), f32),
            pltpu.VMEM((high * lay.nb // LANES, LANES), f32),
            pltpu.VMEM((lay.na // LANES, LANES), f32),
            pltpu.VMEM((lay.nb // LANES, LANES), f32),
            pltpu.VMEM((8, LANES), f32),
        ],
        compiler_params=pltpu.CompilerParams(vmem_limit_bytes=VMEM_BYTES),
        name="solve",
    )(where, *shares)
    return a, b, g


def solution(mesh):
    placed = (
        P(("exp", "imp"), None, None),
        P(("exp", "imp"), None, None),
        P(("exp", "imp")),
        P("exp"),
        P("imp"),
    )
    return jax.shard_map(
        functools.partial(per_device, (mesh.shape["exp"], mesh.shape["imp"])),
        mesh=mesh,
        in_specs=placed,
        out_specs=(P("exp"), P("imp"), P()),
        check_vma=False,
    )
```

```python
import functools

import jax
import jax.numpy as jnp
from jax import lax
from jax.experimental import pallas as pl
from jax.experimental.pallas import tpu as pltpu
from jax.sharding import PartitionSpec as P

NCE = 128
NCI = 128
NEWTON = 2
CG = 2
LANES = 128
RIDGE = 64.0
VMEM_BYTES = 48 * 1024 * 1024

f32 = jnp.float32
bf16 = jnp.bfloat16
i32 = jnp.int32


def iota(shape, dim):
    return lax.broadcasted_iota(i32, shape, dim)


def split(x):
    hi = x.astype(bf16).astype(f32)
    rest = x - hi
    mid = rest.astype(bf16).astype(f32)
    return hi, mid, rest - mid


def dot(x, y, cx, cy, precision=None):
    return lax.dot_general(
        x, y, (((cx,), (cy,)), ((), ())), precision=precision, preferred_element_type=f32
    )


class Layout:
    def __init__(self, na, nb, side, shares):
        self.na, self.nb, self.side, self.shares = na, nb, side, shares
        self.rows_at = NCE
        self.cols_at = self.rows_at + na // LANES
        self.cnt_at = self.cols_at + nb // LANES
        self.live_at = self.cnt_at + 8
        self.blocks_a, self.blocks_b = na // side, nb // side
        self.total = self.live_at + -(-self.blocks_a // 8) * 8
        self.share = -(-self.total // (8 * shares)) * 8
        self.padded = self.share * shares


def local_kernel(lay, slots, *refs):
    sources, outs, out, homes, sems = refs[:5], refs[5:7], refs[7], refs[8:13], refs[13]
    copies = [pltpu.make_async_copy(x, y, sems.at[j]) for j, (x, y) in enumerate(zip(sources, homes))]
    for copy in copies:
        copy.start()
    flows, routing, tile_block, ec, ic = homes
    exp_place, imp_place = lax.axis_index("exp"), lax.axis_index("imp")
    side = lay.side
    row_blocks = ec.shape[0]
    col_local = ic.shape[0]
    out[...] = jnp.zeros_like(out)
    per = side // LANES
    country = iota((NCE, side), 0)
    ones = jnp.ones((8, side), bf16)
    for copy in copies:
        copy.wait()
    pairs = jnp.zeros((NCE, NCI), f32)
    for k in range(slots):
        r = tile_block[k] // col_local
        c = tile_block[k] % col_local
        live = routing[0] == k
        for t in range(1, routing.shape[0]):
            live = live | (routing[t] == k)
        keep = live.astype(f32)
        hot_r = (country == ec[r]).astype(f32).astype(bf16)
        hot_c = (country == ic[c]).astype(f32).astype(bf16)
        tile = flows[k] * keep.astype(bf16)
        half = dot(hot_r, tile, 1, 0)
        col_sum = jnp.sum(half, axis=0, keepdims=True)
        row_sum = dot(ones, tile, 1, 1)[0:1]
        for piece in split(half):
            pairs = pairs + dot(piece.astype(bf16), hot_c, 1, 1)
        row_at = lay.rows_at + (exp_place * row_blocks + r) * per
        col_at = lay.cols_at + (imp_place * col_local + c) * per
        for h in range(per):
            cut = slice(h * LANES, (h + 1) * LANES)
            out[pl.ds(row_at + h, 1), :] += row_sum[:, cut]
            out[pl.ds(col_at + h, 1), :] += col_sum[:, cut]
        live_row = lay.live_at + exp_place * row_blocks + r
        here = iota((1, LANES), 1) == imp_place * col_local + c
        out[pl.ds(live_row, 1), :] += jnp.where(here, keep, 0.0)
    out[0:NCE, :] = pairs
    cnt_a = jnp.zeros((8, LANES), f32)
    for r in range(row_blocks):
        cnt_a += dot(ones, (country == ec[r]).astype(f32).astype(bf16), 1, 1)
    cnt_b = jnp.zeros((8, LANES), f32)
    for c in range(col_local):
        cnt_b += dot(ones, (country == ic[c]).astype(f32).astype(bf16), 1, 1)
    cnt_a = cnt_a[0:1] * (imp_place == 0).astype(f32)
    cnt_b = cnt_b[0:1] * (exp_place == 0).astype(f32)
    out[lay.cnt_at : lay.cnt_at + 1, :] = cnt_a
    out[lay.cnt_at + 1 : lay.cnt_at + 2, :] = cnt_b
    for k, part in enumerate(outs):
        part[...] = out[pl.ds(pl.multiple_of(((exp_place & 1) ^ k) * lay.share, 8), lay.share), :]


def lookup(row, index):
    return jnp.take_along_axis(
        jnp.broadcast_to(row, index.shape), index, axis=1, mode="promise_in_bounds"
    )


def down(row):
    return jnp.transpose(jnp.broadcast_to(row, (LANES, LANES)))


def across(x):
    return jnp.sum(jnp.transpose(x), axis=0, keepdims=True)


def below(x):
    return jnp.sum(x, axis=0, keepdims=True)


def eights(x):
    return functools.reduce(lambda u, v: u + v, [x[j : j + 8] for j in range(0, x.shape[0], 8)])


def inner(u, v):
    partial = eights(u[0] * v[0]) + eights(u[1] * v[1]) + eights(u[2] * v[2])
    return jnp.sum(below(partial), axis=1, keepdims=True)


class Side:
    def __init__(self, n, block, start, middle, end, hot, stage):
        self.n, self.block, self.hot, self.stage = n, block, hot, stage
        self.chunks = n // LANES
        shape = (self.chunks, LANES)
        place = (iota(shape, 0) * LANES + iota(shape, 1)).astype(f32)
        country = jnp.zeros(shape, i32)
        jump = LANES // 2
        while jump:
            passed = lookup(end, country + (jump - 1)) <= place
            country = jnp.where(passed, country + jump, country)
            jump //= 2
        self.country = country
        self.second = place >= lookup(middle, country)
        for j in range(n // block):
            at = (iota((block, LANES), 0) + j * block).astype(f32)
            inside = (at >= start) & (at < end)
            hot[j * block : (j + 1) * block, :] = jnp.where(inside, 1.0, 0.0).astype(bf16)

    def expand(self, first, second):
        return jnp.where(self.second, lookup(second, self.country), lookup(first, self.country))

    def sums(self, vectors):
        chunks, stage = self.chunks, self.stage
        for k, v in enumerate(vectors):
            stage[2 * k * chunks : (2 * k + 1) * chunks, :] = jnp.where(self.second, 0.0, v)
            stage[(2 * k + 1) * chunks : (2 * k + 2) * chunks, :] = jnp.where(self.second, v, 0.0)
        high = -(-2 * len(vectors) // 8) * 8
        for k in range(2 * len(vectors), high):
            stage[k * chunks : (k + 1) * chunks, :] = jnp.zeros((chunks, LANES), f32)
        got = jnp.zeros((3 * high, LANES), f32)
        per = self.block // LANES
        for j in range(chunks // per):
            left = jnp.concatenate(
                [stage[pl.ds(j * per + h, high, stride=chunks), :] for h in range(per)], axis=1
            )
            pieces = jnp.concatenate(split(left), axis=0).astype(bf16)
            got += dot(pieces, self.hot[j * self.block : (j + 1) * self.block, :], 1, 0)
        return got[:high] + got[high : 2 * high] + got[2 * high :]

    def maxima(self, values_ref, low, high):
        low, high = down(low), down(high)

        def body(j, best):
            at = (iota((LANES, LANES), 1) + j * LANES).astype(f32)
            inside = (at >= low) & (at < high)
            return jnp.maximum(best, jnp.where(inside, values_ref[pl.ds(j, 1), :], -jnp.inf))

        best = lax.fori_loop(0, self.chunks, body, jnp.full((LANES, LANES), -jnp.inf, f32))
        best = jnp.max(jnp.transpose(best), axis=0, keepdims=True)
        return jnp.where(best > -jnp.inf, best, 0.0)


def solve_kernel(lay, *refs):
    where = lax.axis_index("exp"), lax.axis_index("imp")
    shares, refs = refs[: lay.shares], refs[lay.shares :]
    out_a, out_b, out_g, shared, hot_a, hot_b, stage_a, stage_b, val_a, val_b, shift_ref = refs
    for k, part in enumerate(shares):
        shared[pl.ds(pl.multiple_of(((where[0] & 1) ^ k) * lay.share, 8), lay.share), :] = part[...]
    flow = (
        shared[lay.rows_at : lay.cols_at, :],
        shared[lay.cols_at : lay.cnt_at, :],
        shared[0:NCE, :],
    )
    side = lay.side
    tally = shared[lay.cnt_at : lay.cnt_at + 8, :]
    before = jnp.where(iota((LANES, LANES), 0) < iota((LANES, LANES), 1), 1.0, 0.0).astype(bf16)
    start = dot(tally.astype(bf16), before, 1, 0)
    end = start + tally
    first = jnp.floor((start + 0.5) * (1.0 / side))
    middle = jnp.minimum(end, (first + 1.0) * side)

    def table(x, y):
        return jnp.concatenate([x[0:1], y[0:1], x[1:2], y[1:2]], axis=0)

    low, high = table(start, middle), table(middle, end)
    count = high - low
    full = count > 0.5
    inv_count = jnp.where(full, 1.0 / jnp.maximum(count, 1.0), 0.0)
    block_of = jnp.where(full, table(first, first + 1.0), -1.0)
    sa = Side(lay.na, side, start[0:1], middle[0:1], end[0:1], hot_a, stage_a)
    sb = Side(lay.nb, side, start[1:2], middle[1:2], end[1:2], hot_b, stage_b)

    live = shared[lay.live_at : lay.total, :].astype(bf16)
    height = lay.total - lay.live_at
    number = iota((LANES, LANES), 1).astype(f32)
    pick_a = [jnp.where(down(block_of[p : p + 1]) == number, 1.0, 0.0).astype(bf16) for p in (0, 1)]
    number = iota((LANES, LANES), 0).astype(f32)
    pick_b = [jnp.where(block_of[q : q + 1] == number, 1.0, 0.0).astype(bf16) for q in (2, 3)]
    wide = [dot(pick[:, :height], live, 1, 0).astype(bf16) for pick in pick_a]
    mask = [[dot(wide[p], pick_b[q], 1, 0) for q in (0, 1)] for p in (0, 1)]

    a = jnp.zeros((lay.na // LANES, LANES), f32)
    b = jnp.zeros((lay.nb // LANES, LANES), f32)
    g = jnp.zeros((NCE, NCI), f32)
    mean = jnp.zeros((4, LANES), f32)
    for newton in range(NEWTON):
        if newton == 0:
            left = flow
            weight, inv, rate = count, inv_count, mask
            sum_a, sum_b = sa.sums([flow[0]]), sb.sums([flow[1]])
            part_a, part_b = sa.expand(inv[0:1], inv[1:2]), sb.expand(inv[2:3], inv[3:4])
            m2, m3 = inv, inv * inv
            f1 = jnp.concatenate([sum_a[0:2], sum_b[0:2]], axis=0) * inv
            f2 = f1 * inv
        else:
            left = (flow[0] - RIDGE * a, flow[1] - RIDGE * b, flow[2] - RIDGE * g)
            shift_ref[0:4, :] = mean
            off_a = a - sa.expand(mean[0:1], mean[1:2])
            off_b = b - sb.expand(mean[2:3], mean[3:4])
            worst = jnp.maximum(jnp.max(off_a), jnp.max(off_b))
            val_a[...] = a
            val_b[...] = b

            @pl.when(worst > 20.0)
            def _():
                shift_ref[0:1, :] = sa.maxima(val_a, low[0:1], high[0:1])
                shift_ref[1:2, :] = sa.maxima(val_a, low[1:2], high[1:2])
                shift_ref[2:3, :] = sb.maxima(val_b, low[2:3], high[2:3])
                shift_ref[3:4, :] = sb.maxima(val_b, low[3:4], high[3:4])

            shift = shift_ref[0:4, :]
            size_a = jnp.exp(a - sa.expand(shift[0:1], shift[1:2]))
            size_b = jnp.exp(b - sb.expand(shift[2:3], shift[3:4]))

            def moments(s, x, f):
                return s.sums([x, x * x, x * x * x, x * f, x * x * f])

            sum_a, sum_b = moments(sa, size_a, left[0]), moments(sb, size_b, left[1])
            got = [jnp.concatenate([sum_a[2 * k : 2 * k + 2], sum_b[2 * k : 2 * k + 2]], axis=0) for k in range(5)]
            weight = got[0]
            inv = jnp.where(full, 1.0 / jnp.where(full, weight, 1.0), 0.0)
            part_a = size_a * sa.expand(inv[0:1], inv[1:2])
            part_b = size_b * sb.expand(inv[2:3], inv[3:4])
            inv2 = inv * inv
            m2, m3 = got[1] * inv2, got[2] * (inv2 * inv)
            f1, f2 = got[3] * inv, got[4] * inv2
            lift = [g + down(shift[p : p + 1]) for p in (0, 1)]
            rate = [
                [jnp.where(mask[p][q] > 0.5, jnp.exp(lift[p] + shift[2 + q : 3 + q]), 0.0) for q in (0, 1)]
                for p in (0, 1)
            ]
        tall = [down(weight[p : p + 1]) for p in (0, 1)]
        mu = [[rate[p][q] * (tall[p] * weight[2 + q : 3 + q]) for q in (0, 1)] for p in (0, 1)]
        mu_a = [mu[p][0] + mu[p][1] for p in (0, 1)]
        mu_b = [mu[0][q] + mu[1][q] for q in (0, 1)]
        whole = jnp.concatenate([across(mu_a[0]), across(mu_a[1]), below(mu_b[0]), below(mu_b[1])], axis=0)
        da = part_a * sa.expand(whole[0:1], whole[1:2])
        db = part_b * sb.expand(whole[2:3], whole[3:4])
        res = (left[0] - da, left[1] - db, left[2] - (mu_a[0] + mu_a[1]))
        way = res
        norm = inner(res, res)
        v = f1 - whole * m2
        w = f2 - whole * m3
        for sweep in range(CG):
            tall = [down(v[p : p + 1]) for p in (0, 1)]
            flat = [v[2 + q : 3 + q] for q in (0, 1)]
            ga = [mu[p][0] * flat[0] + mu[p][1] * flat[1] + way[2] * mu_a[p] for p in (0, 1)]
            gb = [mu[0][q] * tall[0] + mu[1][q] * tall[1] + way[2] * mu_b[q] for q in (0, 1)]
            u = jnp.concatenate([across(ga[0]), across(ga[1]), below(gb[0]), below(gb[1])], axis=0)
            image = (
                (da + RIDGE) * way[0] + part_a * sa.expand(u[0:1], u[1:2]),
                (db + RIDGE) * way[1] + part_b * sb.expand(u[2:3], u[3:4]),
                RIDGE * way[2] + (ga[0] + ga[1]) + (tall[0] * mu_a[0] + tall[1] * mu_a[1]),
            )
            step = norm / inner(way, image)
            a, b, g = a + step * way[0], b + step * way[1], g + step * way[2]
            if newton + 1 < NEWTON:
                mean = mean + step * v
            if sweep + 1 < CG:
                res = tuple(x - step * y for x, y in zip(res, image))
                fresh = inner(res, res)
                ratio = fresh / norm
                way = tuple(x + ratio * y for x, y in zip(res, way))
                norm = fresh
                v = v - step * (whole * w + RIDGE * v + u * m2) + ratio * v
    out_g[...] = g
    val_a[...] = a
    val_b[...] = b
    for out, val, at in ((out_a, val_a, where[0]), (out_b, val_b, where[1])):
        rows = out.shape[0] // LANES
        for j in range(rows):
            out[j * LANES : (j + 1) * LANES] = val[pl.ds(at * rows + j, 1), :].reshape(LANES)


def swap(x, axis, size, bits):
    return lax.ppermute(x, axis, [(d, d ^ bits) for d in range(size)])


def per_device(mesh_shape, flows, routing, tile_block, exp_country, imp_country):
    slots, side = flows.shape[0], flows.shape[1]
    n_exp, n_imp = mesh_shape
    rows, cols = exp_country.shape[0], imp_country.shape[0]
    lay = Layout(rows * n_exp, cols * n_imp, side, 2)
    vmem = pl.BlockSpec(memory_space=pltpu.VMEM)
    inputs = (
        flows,
        routing.reshape(-1),
        tile_block,
        exp_country.reshape(-1, 1, side),
        imp_country.reshape(-1, 1, side),
    )
    homes = [pltpu.VMEM, pltpu.SMEM, pltpu.SMEM, pltpu.VMEM, pltpu.VMEM]
    parts = pl.pallas_call(
        functools.partial(local_kernel, lay, slots),
        out_shape=[jax.ShapeDtypeStruct((lay.share, LANES), f32)] * 2,
        in_specs=[pl.BlockSpec(memory_space=pltpu.HBM)] * 5,
        out_specs=[vmem] * 2,
        scratch_shapes=[pltpu.VMEM((lay.padded, LANES), f32)]
        + [space(x.shape, x.dtype) for space, x in zip(homes, inputs)]
        + [pltpu.SemaphoreType.DMA((5,))],
        compiler_params=pltpu.CompilerParams(vmem_limit_bytes=VMEM_BYTES),
        name="local_sums",
    )(*inputs)
    mine = parts[0] + swap(parts[1], "exp", n_exp, 1)
    for axis, size, bit in (("exp", n_exp, 2), ("imp", n_imp, 1)):
        while bit < size:
            mine = mine + swap(mine, axis, size, bit)
            bit *= 2
    shares = (mine, swap(mine, "exp", n_exp, 1))
    high = 16
    a, b, g = pl.pallas_call(
        functools.partial(solve_kernel, lay),
        out_shape=(
            jax.ShapeDtypeStruct((rows,), f32),
            jax.ShapeDtypeStruct((cols,), f32),
            jax.ShapeDtypeStruct((NCE, NCI), f32),
        ),
        in_specs=[vmem] * 2,
        out_specs=(vmem, vmem, vmem),
        scratch_shapes=[
            pltpu.VMEM((lay.padded, LANES), f32),
            pltpu.VMEM((lay.na, LANES), bf16),
            pltpu.VMEM((lay.nb, LANES), bf16),
            pltpu.VMEM((high * lay.na // LANES, LANES), f32),
            pltpu.VMEM((high * lay.nb // LANES, LANES), f32),
            pltpu.VMEM((lay.na // LANES, LANES), f32),
            pltpu.VMEM((lay.nb // LANES, LANES), f32),
            pltpu.VMEM((8, LANES), f32),
        ],
        compiler_params=pltpu.CompilerParams(vmem_limit_bytes=VMEM_BYTES),
        name="solve",
    )(*shares)
    return a, b, g


def solution(mesh):
    placed = (
        P(("exp", "imp"), None, None),
        P(("exp", "imp"), None, None),
        P(("exp", "imp")),
        P("exp"),
        P("imp"),
    )
    return jax.shard_map(
        functools.partial(per_device, (mesh.shape["exp"], mesh.shape["imp"])),
        mesh=mesh,
        in_specs=placed,
        out_specs=(P("exp"), P("imp"), P()),
        check_vma=False,
    )
```

```python
import functools

import jax
import jax.numpy as jnp
from jax import lax
from jax.experimental import pallas as pl
from jax.experimental.pallas import tpu as pltpu
from jax.sharding import PartitionSpec as P

NCE = 128
NCI = 128
NEWTON = 2
CG = 2
LANES = 128
RIDGE = 64.0
VMEM_BYTES = 48 * 1024 * 1024

f32 = jnp.float32
bf16 = jnp.bfloat16
i32 = jnp.int32


def iota(shape, dim):
    return lax.broadcasted_iota(i32, shape, dim)


def split(x):
    hi = x.astype(bf16).astype(f32)
    rest = x - hi
    mid = rest.astype(bf16).astype(f32)
    return hi, mid, rest - mid


def dot(x, y, cx, cy, precision=None):
    return lax.dot_general(
        x, y, (((cx,), (cy,)), ((), ())), precision=precision, preferred_element_type=f32
    )


class Layout:
    def __init__(self, na, nb, side, shares):
        self.na, self.nb, self.side, self.shares = na, nb, side, shares
        self.rows_at = NCE
        self.cols_at = self.rows_at + na // LANES
        self.cnt_at = self.cols_at + nb // LANES
        self.live_at = self.cnt_at + 8
        self.blocks_a, self.blocks_b = na // side, nb // side
        self.total = self.live_at + -(-self.blocks_a // 8) * 8
        self.share = -(-self.total // (8 * shares)) * 8
        self.padded = self.share * shares


def local_kernel(lay, slots, *refs):
    sources, out, homes, sems = refs[:5], refs[5], refs[6:11], refs[11]
    copies = [pltpu.make_async_copy(x, y, sems.at[j]) for j, (x, y) in enumerate(zip(sources, homes))]
    for copy in copies:
        copy.start()
    flows, routing, tile_block, ec, ic = homes
    exp_place, imp_place = lax.axis_index("exp"), lax.axis_index("imp")
    side = lay.side
    row_blocks = ec.shape[0]
    col_local = ic.shape[0]
    out[...] = jnp.zeros_like(out)
    per = side // LANES
    country = iota((NCE, side), 0)
    ones = jnp.ones((8, side), bf16)
    for copy in copies:
        copy.wait()
    pairs = jnp.zeros((NCE, NCI), f32)
    for k in range(slots):
        r = tile_block[k] // col_local
        c = tile_block[k] % col_local
        live = routing[0] == k
        for t in range(1, routing.shape[0]):
            live = live | (routing[t] == k)
        keep = live.astype(f32)
        hot_r = (country == ec[r]).astype(f32).astype(bf16)
        hot_c = (country == ic[c]).astype(f32).astype(bf16)
        tile = flows[k] * keep.astype(bf16)
        half = dot(hot_r, tile, 1, 0)
        col_sum = jnp.sum(half, axis=0, keepdims=True)
        row_sum = dot(ones, tile, 1, 1)[0:1]
        for piece in split(half):
            pairs = pairs + dot(piece.astype(bf16), hot_c, 1, 1)
        row_at = lay.rows_at + (exp_place * row_blocks + r) * per
        col_at = lay.cols_at + (imp_place * col_local + c) * per
        for h in range(per):
            cut = slice(h * LANES, (h + 1) * LANES)
            out[pl.ds(row_at + h, 1), :] += row_sum[:, cut]
            out[pl.ds(col_at + h, 1), :] += col_sum[:, cut]
        live_row = lay.live_at + exp_place * row_blocks + r
        here = iota((1, LANES), 1) == imp_place * col_local + c
        out[pl.ds(live_row, 1), :] += jnp.where(here, keep, 0.0)
    out[0:NCE, :] = pairs
    cnt_a = jnp.zeros((8, LANES), f32)
    for r in range(row_blocks):
        cnt_a += dot(ones, (country == ec[r]).astype(f32).astype(bf16), 1, 1)
    cnt_b = jnp.zeros((8, LANES), f32)
    for c in range(col_local):
        cnt_b += dot(ones, (country == ic[c]).astype(f32).astype(bf16), 1, 1)
    cnt_a = cnt_a[0:1] * (imp_place == 0).astype(f32)
    cnt_b = cnt_b[0:1] * (exp_place == 0).astype(f32)
    out[lay.cnt_at : lay.cnt_at + 1, :] = cnt_a
    out[lay.cnt_at + 1 : lay.cnt_at + 2, :] = cnt_b


def lookup(row, index):
    return jnp.take_along_axis(
        jnp.broadcast_to(row, index.shape), index, axis=1, mode="promise_in_bounds"
    )


def down(row):
    return jnp.transpose(jnp.broadcast_to(row, (LANES, LANES)))


def across(x):
    return jnp.sum(jnp.transpose(x), axis=0, keepdims=True)


def below(x):
    return jnp.sum(x, axis=0, keepdims=True)


def eights(x):
    return functools.reduce(lambda u, v: u + v, [x[j : j + 8] for j in range(0, x.shape[0], 8)])


def inner(u, v):
    partial = eights(u[0] * v[0]) + eights(u[1] * v[1]) + eights(u[2] * v[2])
    return jnp.sum(below(partial), axis=1, keepdims=True)


class Side:
    def __init__(self, n, block, start, middle, end, hot, stage):
        self.n, self.block, self.hot, self.stage = n, block, hot, stage
        self.chunks = n // LANES
        shape = (self.chunks, LANES)
        place = (iota(shape, 0) * LANES + iota(shape, 1)).astype(f32)
        country = jnp.zeros(shape, i32)
        jump = LANES // 2
        while jump:
            passed = lookup(end, country + (jump - 1)) <= place
            country = jnp.where(passed, country + jump, country)
            jump //= 2
        self.country = country
        self.second = place >= lookup(middle, country)
        for j in range(n // block):
            at = (iota((block, LANES), 0) + j * block).astype(f32)
            inside = (at >= start) & (at < end)
            hot[j * block : (j + 1) * block, :] = jnp.where(inside, 1.0, 0.0).astype(bf16)

    def expand(self, first, second):
        return jnp.where(self.second, lookup(second, self.country), lookup(first, self.country))

    def sums(self, vectors):
        chunks, stage = self.chunks, self.stage
        for k, v in enumerate(vectors):
            stage[2 * k * chunks : (2 * k + 1) * chunks, :] = jnp.where(self.second, 0.0, v)
            stage[(2 * k + 1) * chunks : (2 * k + 2) * chunks, :] = jnp.where(self.second, v, 0.0)
        high = -(-2 * len(vectors) // 8) * 8
        for k in range(2 * len(vectors), high):
            stage[k * chunks : (k + 1) * chunks, :] = jnp.zeros((chunks, LANES), f32)
        got = jnp.zeros((3 * high, LANES), f32)
        per = self.block // LANES
        for j in range(chunks // per):
            left = jnp.concatenate(
                [stage[pl.ds(j * per + h, high, stride=chunks), :] for h in range(per)], axis=1
            )
            pieces = jnp.concatenate(split(left), axis=0).astype(bf16)
            got += dot(pieces, self.hot[j * self.block : (j + 1) * self.block, :], 1, 0)
        return got[:high] + got[high : 2 * high] + got[2 * high :]

    def maxima(self, values_ref, low, high):
        low, high = down(low), down(high)

        def body(j, best):
            at = (iota((LANES, LANES), 1) + j * LANES).astype(f32)
            inside = (at >= low) & (at < high)
            return jnp.maximum(best, jnp.where(inside, values_ref[pl.ds(j, 1), :], -jnp.inf))

        best = lax.fori_loop(0, self.chunks, body, jnp.full((LANES, LANES), -jnp.inf, f32))
        best = jnp.max(jnp.transpose(best), axis=0, keepdims=True)
        return jnp.where(best > -jnp.inf, best, 0.0)


def solve_kernel(lay, *refs):
    where = lax.axis_index("exp"), lax.axis_index("imp")
    shared, out_a, out_b, out_g, hot_a, hot_b, stage_a, stage_b, val_a, val_b, shift_ref = refs
    flow = (
        shared[lay.rows_at : lay.cols_at, :],
        shared[lay.cols_at : lay.cnt_at, :],
        shared[0:NCE, :],
    )
    side = lay.side
    tally = shared[lay.cnt_at : lay.cnt_at + 8, :]
    before = jnp.where(iota((LANES, LANES), 0) < iota((LANES, LANES), 1), 1.0, 0.0).astype(bf16)
    start = dot(tally.astype(bf16), before, 1, 0)
    end = start + tally
    first = jnp.floor((start + 0.5) * (1.0 / side))
    middle = jnp.minimum(end, (first + 1.0) * side)

    def table(x, y):
        return jnp.concatenate([x[0:1], y[0:1], x[1:2], y[1:2]], axis=0)

    low, high = table(start, middle), table(middle, end)
    count = high - low
    full = count > 0.5
    inv_count = jnp.where(full, 1.0 / jnp.maximum(count, 1.0), 0.0)
    block_of = jnp.where(full, table(first, first + 1.0), -1.0)
    sa = Side(lay.na, side, start[0:1], middle[0:1], end[0:1], hot_a, stage_a)
    sb = Side(lay.nb, side, start[1:2], middle[1:2], end[1:2], hot_b, stage_b)

    live = shared[lay.live_at : lay.total, :].astype(bf16)
    height = lay.total - lay.live_at
    number = iota((LANES, LANES), 1).astype(f32)
    pick_a = [jnp.where(down(block_of[p : p + 1]) == number, 1.0, 0.0).astype(bf16) for p in (0, 1)]
    number = iota((LANES, LANES), 0).astype(f32)
    pick_b = [jnp.where(block_of[q : q + 1] == number, 1.0, 0.0).astype(bf16) for q in (2, 3)]
    wide = [dot(pick[:, :height], live, 1, 0).astype(bf16) for pick in pick_a]
    mask = [[dot(wide[p], pick_b[q], 1, 0) for q in (0, 1)] for p in (0, 1)]

    a = jnp.zeros((lay.na // LANES, LANES), f32)
    b = jnp.zeros((lay.nb // LANES, LANES), f32)
    g = jnp.zeros((NCE, NCI), f32)
    mean = jnp.zeros((4, LANES), f32)
    for newton in range(NEWTON):
        if newton == 0:
            left = flow
            weight, inv, rate = count, inv_count, mask
            sum_a, sum_b = sa.sums([flow[0]]), sb.sums([flow[1]])
            part_a, part_b = sa.expand(inv[0:1], inv[1:2]), sb.expand(inv[2:3], inv[3:4])
            m2, m3 = inv, inv * inv
            f1 = jnp.concatenate([sum_a[0:2], sum_b[0:2]], axis=0) * inv
            f2 = f1 * inv
        else:
            left = (flow[0] - RIDGE * a, flow[1] - RIDGE * b, flow[2] - RIDGE * g)
            shift_ref[0:4, :] = mean
            off_a = a - sa.expand(mean[0:1], mean[1:2])
            off_b = b - sb.expand(mean[2:3], mean[3:4])
            worst = jnp.maximum(jnp.max(off_a), jnp.max(off_b))
            val_a[...] = a
            val_b[...] = b

            @pl.when(worst > 20.0)
            def _():
                shift_ref[0:1, :] = sa.maxima(val_a, low[0:1], high[0:1])
                shift_ref[1:2, :] = sa.maxima(val_a, low[1:2], high[1:2])
                shift_ref[2:3, :] = sb.maxima(val_b, low[2:3], high[2:3])
                shift_ref[3:4, :] = sb.maxima(val_b, low[3:4], high[3:4])

            shift = shift_ref[0:4, :]
            size_a = jnp.exp(a - sa.expand(shift[0:1], shift[1:2]))
            size_b = jnp.exp(b - sb.expand(shift[2:3], shift[3:4]))

            def moments(s, x, f):
                return s.sums([x, x * x, x * x * x, x * f, x * x * f])

            sum_a, sum_b = moments(sa, size_a, left[0]), moments(sb, size_b, left[1])
            got = [jnp.concatenate([sum_a[2 * k : 2 * k + 2], sum_b[2 * k : 2 * k + 2]], axis=0) for k in range(5)]
            weight = got[0]
            inv = jnp.where(full, 1.0 / jnp.where(full, weight, 1.0), 0.0)
            part_a = size_a * sa.expand(inv[0:1], inv[1:2])
            part_b = size_b * sb.expand(inv[2:3], inv[3:4])
            inv2 = inv * inv
            m2, m3 = got[1] * inv2, got[2] * (inv2 * inv)
            f1, f2 = got[3] * inv, got[4] * inv2
            lift = [g + down(shift[p : p + 1]) for p in (0, 1)]
            rate = [
                [jnp.where(mask[p][q] > 0.5, jnp.exp(lift[p] + shift[2 + q : 3 + q]), 0.0) for q in (0, 1)]
                for p in (0, 1)
            ]
        tall = [down(weight[p : p + 1]) for p in (0, 1)]
        mu = [[rate[p][q] * (tall[p] * weight[2 + q : 3 + q]) for q in (0, 1)] for p in (0, 1)]
        mu_a = [mu[p][0] + mu[p][1] for p in (0, 1)]
        mu_b = [mu[0][q] + mu[1][q] for q in (0, 1)]
        whole = jnp.concatenate([across(mu_a[0]), across(mu_a[1]), below(mu_b[0]), below(mu_b[1])], axis=0)
        da = part_a * sa.expand(whole[0:1], whole[1:2])
        db = part_b * sb.expand(whole[2:3], whole[3:4])
        res = (left[0] - da, left[1] - db, left[2] - (mu_a[0] + mu_a[1]))
        way = res
        norm = inner(res, res)
        v = f1 - whole * m2
        w = f2 - whole * m3
        for sweep in range(CG):
            tall = [down(v[p : p + 1]) for p in (0, 1)]
            flat = [v[2 + q : 3 + q] for q in (0, 1)]
            ga = [mu[p][0] * flat[0] + mu[p][1] * flat[1] + way[2] * mu_a[p] for p in (0, 1)]
            gb = [mu[0][q] * tall[0] + mu[1][q] * tall[1] + way[2] * mu_b[q] for q in (0, 1)]
            u = jnp.concatenate([across(ga[0]), across(ga[1]), below(gb[0]), below(gb[1])], axis=0)
            image = (
                (da + RIDGE) * way[0] + part_a * sa.expand(u[0:1], u[1:2]),
                (db + RIDGE) * way[1] + part_b * sb.expand(u[2:3], u[3:4]),
                RIDGE * way[2] + (ga[0] + ga[1]) + (tall[0] * mu_a[0] + tall[1] * mu_a[1]),
            )
            step = norm / inner(way, image)
            a, b, g = a + step * way[0], b + step * way[1], g + step * way[2]
            if newton + 1 < NEWTON:
                mean = mean + step * v
            if sweep + 1 < CG:
                res = tuple(x - step * y for x, y in zip(res, image))
                fresh = inner(res, res)
                ratio = fresh / norm
                way = tuple(x + ratio * y for x, y in zip(res, way))
                norm = fresh
                v = v - step * (whole * w + RIDGE * v + u * m2) + ratio * v
    out_g[...] = g
    val_a[...] = a
    val_b[...] = b
    for out, val, at in ((out_a, val_a, where[0]), (out_b, val_b, where[1])):
        rows = out.shape[0] // LANES
        for j in range(rows):
            out[j * LANES : (j + 1) * LANES] = val[pl.ds(at * rows + j, 1), :].reshape(LANES)


def per_device(mesh_shape, flows, routing, tile_block, exp_country, imp_country):
    slots, side = flows.shape[0], flows.shape[1]
    n_exp, n_imp = mesh_shape
    rows, cols = exp_country.shape[0], imp_country.shape[0]
    lay = Layout(rows * n_exp, cols * n_imp, side, n_exp * n_imp)
    vmem = pl.BlockSpec(memory_space=pltpu.VMEM)
    inputs = (
        flows,
        routing.reshape(-1),
        tile_block,
        exp_country.reshape(-1, 1, side),
        imp_country.reshape(-1, 1, side),
    )
    homes = [pltpu.VMEM, pltpu.SMEM, pltpu.SMEM, pltpu.VMEM, pltpu.VMEM]
    shared = pl.pallas_call(
        functools.partial(local_kernel, lay, slots),
        out_shape=jax.ShapeDtypeStruct((lay.padded, LANES), f32),
        in_specs=[pl.BlockSpec(memory_space=pltpu.HBM)] * 5,
        out_specs=vmem,
        scratch_shapes=[space(x.shape, x.dtype) for space, x in zip(homes, inputs)]
        + [pltpu.SemaphoreType.DMA((5,))],
        compiler_params=pltpu.CompilerParams(vmem_limit_bytes=VMEM_BYTES),
        name="local_sums",
    )(*inputs)
    every = n_exp * n_imp
    got = lax.all_to_all(shared, ("exp", "imp"), 0, 0, tiled=True)
    mine = jnp.sum(got.reshape(every, lay.share, LANES), axis=0)
    mine = jnp.broadcast_to(mine[None], (every, lay.share, LANES)).reshape(lay.padded, LANES)
    shared = lax.all_to_all(mine, ("exp", "imp"), 0, 0, tiled=True)
    high = 16
    a, b, g = pl.pallas_call(
        functools.partial(solve_kernel, lay),
        out_shape=(
            jax.ShapeDtypeStruct((rows,), f32),
            jax.ShapeDtypeStruct((cols,), f32),
            jax.ShapeDtypeStruct((NCE, NCI), f32),
        ),
        in_specs=[vmem],
        out_specs=(vmem, vmem, vmem),
        scratch_shapes=[
            pltpu.VMEM((lay.na, LANES), bf16),
            pltpu.VMEM((lay.nb, LANES), bf16),
            pltpu.VMEM((high * lay.na // LANES, LANES), f32),
            pltpu.VMEM((high * lay.nb // LANES, LANES), f32),
            pltpu.VMEM((lay.na // LANES, LANES), f32),
            pltpu.VMEM((lay.nb // LANES, LANES), f32),
            pltpu.VMEM((8, LANES), f32),
        ],
        compiler_params=pltpu.CompilerParams(vmem_limit_bytes=VMEM_BYTES),
        name="solve",
    )(shared)
    return a, b, g


def solution(mesh):
    placed = (
        P(("exp", "imp"), None, None),
        P(("exp", "imp"), None, None),
        P(("exp", "imp")),
        P("exp"),
        P("imp"),
    )
    return jax.shard_map(
        functools.partial(per_device, (mesh.shape["exp"], mesh.shape["imp"])),
        mesh=mesh,
        in_specs=placed,
        out_specs=(P("exp"), P("imp"), P()),
        check_vma=False,
    )
```

```python
import functools

import jax
import jax.numpy as jnp
from jax import lax
from jax.experimental import pallas as pl
from jax.experimental.pallas import tpu as pltpu
from jax.sharding import PartitionSpec as P

NCE = 128
NCI = 128
NEWTON = 2
CG = 2
LANES = 128
RIDGE = 64.0
VMEM_BYTES = 48 * 1024 * 1024

f32 = jnp.float32
bf16 = jnp.bfloat16
i32 = jnp.int32


def iota(shape, dim):
    return lax.broadcasted_iota(i32, shape, dim)


def split(x):
    hi = x.astype(bf16).astype(f32)
    rest = x - hi
    mid = rest.astype(bf16).astype(f32)
    return hi, mid, rest - mid


def dot(x, y, cx, cy, precision=None):
    return lax.dot_general(
        x, y, (((cx,), (cy,)), ((), ())), precision=precision, preferred_element_type=f32
    )


class Layout:
    def __init__(self, na, nb, side, shares):
        self.na, self.nb, self.side, self.shares = na, nb, side, shares
        self.rows_at = NCE
        self.cols_at = self.rows_at + na // LANES
        self.cnt_at = self.cols_at + nb // LANES
        self.live_at = self.cnt_at + 8
        self.blocks_a, self.blocks_b = na // side, nb // side
        self.total = self.live_at + -(-self.blocks_a // 8) * 8
        self.share = -(-self.total // (8 * shares)) * 8
        self.padded = self.share * shares


def local_kernel(lay, slots, *refs):
    sources, out, homes, sems = refs[:5], refs[5], refs[6:11], refs[11]
    copies = [pltpu.make_async_copy(x, y, sems.at[j]) for j, (x, y) in enumerate(zip(sources, homes))]
    for copy in copies:
        copy.start()
    flows, routing, tile_block, ec, ic = homes
    exp_place, imp_place = lax.axis_index("exp"), lax.axis_index("imp")
    side = lay.side
    row_blocks = ec.shape[0]
    col_local = ic.shape[0]
    out[...] = jnp.zeros_like(out)
    per = side // LANES
    country = iota((NCE, side), 0)
    ones = jnp.ones((8, side), bf16)
    for copy in copies:
        copy.wait()
    pairs = jnp.zeros((NCE, NCI), f32)
    for k in range(slots):
        r = tile_block[k] // col_local
        c = tile_block[k] % col_local
        live = routing[0] == k
        for t in range(1, routing.shape[0]):
            live = live | (routing[t] == k)
        keep = live.astype(f32)
        hot_r = (country == ec[r]).astype(f32).astype(bf16)
        hot_c = (country == ic[c]).astype(f32).astype(bf16)
        tile = flows[k] * keep.astype(bf16)
        half = dot(hot_r, tile, 1, 0)
        col_sum = jnp.sum(half, axis=0, keepdims=True)
        row_sum = dot(ones, tile, 1, 1)[0:1]
        for piece in split(half):
            pairs = pairs + dot(piece.astype(bf16), hot_c, 1, 1)
        row_at = lay.rows_at + (exp_place * row_blocks + r) * per
        col_at = lay.cols_at + (imp_place * col_local + c) * per
        for h in range(per):
            cut = slice(h * LANES, (h + 1) * LANES)
            out[pl.ds(row_at + h, 1), :] += row_sum[:, cut]
            out[pl.ds(col_at + h, 1), :] += col_sum[:, cut]
        live_row = lay.live_at + exp_place * row_blocks + r
        here = iota((1, LANES), 1) == imp_place * col_local + c
        out[pl.ds(live_row, 1), :] += jnp.where(here, keep, 0.0)
    out[0:NCE, :] = pairs
    cnt_a = jnp.zeros((8, LANES), f32)
    for r in range(row_blocks):
        cnt_a += dot(ones, (country == ec[r]).astype(f32).astype(bf16), 1, 1)
    cnt_b = jnp.zeros((8, LANES), f32)
    for c in range(col_local):
        cnt_b += dot(ones, (country == ic[c]).astype(f32).astype(bf16), 1, 1)
    cnt_a = cnt_a[0:1] * (imp_place == 0).astype(f32)
    cnt_b = cnt_b[0:1] * (exp_place == 0).astype(f32)
    out[lay.cnt_at : lay.cnt_at + 1, :] = cnt_a
    out[lay.cnt_at + 1 : lay.cnt_at + 2, :] = cnt_b


def lookup(row, index):
    return jnp.take_along_axis(
        jnp.broadcast_to(row, index.shape), index, axis=1, mode="promise_in_bounds"
    )


def down(row):
    return jnp.transpose(jnp.broadcast_to(row, (LANES, LANES)))


def across(x):
    return jnp.sum(jnp.transpose(x), axis=0, keepdims=True)


def below(x):
    return jnp.sum(x, axis=0, keepdims=True)


def eights(x):
    return functools.reduce(lambda u, v: u + v, [x[j : j + 8] for j in range(0, x.shape[0], 8)])


def inner(u, v):
    partial = eights(u[0] * v[0]) + eights(u[1] * v[1]) + eights(u[2] * v[2])
    return jnp.sum(below(partial), axis=1, keepdims=True)


class Side:
    def __init__(self, n, block, start, middle, end, hot, stage):
        self.n, self.block, self.hot, self.stage = n, block, hot, stage
        self.chunks = n // LANES
        shape = (self.chunks, LANES)
        place = (iota(shape, 0) * LANES + iota(shape, 1)).astype(f32)
        country = jnp.zeros(shape, i32)
        jump = LANES // 2
        while jump:
            passed = lookup(end, country + (jump - 1)) <= place
            country = jnp.where(passed, country + jump, country)
            jump //= 2
        self.country = country
        self.second = place >= lookup(middle, country)
        for j in range(n // block):
            at = (iota((block, LANES), 0) + j * block).astype(f32)
            inside = (at >= start) & (at < end)
            hot[j * block : (j + 1) * block, :] = jnp.where(inside, 1.0, 0.0).astype(bf16)

    def expand(self, first, second):
        return jnp.where(self.second, lookup(second, self.country), lookup(first, self.country))

    def sums(self, vectors):
        chunks, stage = self.chunks, self.stage
        for k, v in enumerate(vectors):
            stage[2 * k * chunks : (2 * k + 1) * chunks, :] = jnp.where(self.second, 0.0, v)
            stage[(2 * k + 1) * chunks : (2 * k + 2) * chunks, :] = jnp.where(self.second, v, 0.0)
        high = -(-2 * len(vectors) // 8) * 8
        for k in range(2 * len(vectors), high):
            stage[k * chunks : (k + 1) * chunks, :] = jnp.zeros((chunks, LANES), f32)
        got = jnp.zeros((3 * high, LANES), f32)
        per = self.block // LANES
        for j in range(chunks // per):
            left = jnp.concatenate(
                [stage[pl.ds(j * per + h, high, stride=chunks), :] for h in range(per)], axis=1
            )
            pieces = jnp.concatenate(split(left), axis=0).astype(bf16)
            got += dot(pieces, self.hot[j * self.block : (j + 1) * self.block, :], 1, 0)
        return got[:high] + got[high : 2 * high] + got[2 * high :]

    def maxima(self, values_ref, low, high):
        low, high = down(low), down(high)

        def body(j, best):
            at = (iota((LANES, LANES), 1) + j * LANES).astype(f32)
            inside = (at >= low) & (at < high)
            return jnp.maximum(best, jnp.where(inside, values_ref[pl.ds(j, 1), :], -jnp.inf))

        best = lax.fori_loop(0, self.chunks, body, jnp.full((LANES, LANES), -jnp.inf, f32))
        best = jnp.max(jnp.transpose(best), axis=0, keepdims=True)
        return jnp.where(best > -jnp.inf, best, 0.0)


def solve_kernel(lay, *refs):
    where = lax.axis_index("exp"), lax.axis_index("imp")
    shared, out_a, out_b, out_g, hot_a, hot_b, stage_a, stage_b, val_a, val_b, shift_ref = refs
    flow = (
        shared[lay.rows_at : lay.cols_at, :],
        shared[lay.cols_at : lay.cnt_at, :],
        shared[0:NCE, :],
    )
    side = lay.side
    tally = shared[lay.cnt_at : lay.cnt_at + 8, :]
    before = jnp.where(iota((LANES, LANES), 0) < iota((LANES, LANES), 1), 1.0, 0.0).astype(bf16)
    start = dot(tally.astype(bf16), before, 1, 0)
    end = start + tally
    first = jnp.floor((start + 0.5) * (1.0 / side))
    middle = jnp.minimum(end, (first + 1.0) * side)

    def table(x, y):
        return jnp.concatenate([x[0:1], y[0:1], x[1:2], y[1:2]], axis=0)

    low, high = table(start, middle), table(middle, end)
    count = high - low
    full = count > 0.5
    inv_count = jnp.where(full, 1.0 / jnp.maximum(count, 1.0), 0.0)
    block_of = jnp.where(full, table(first, first + 1.0), -1.0)
    sa = Side(lay.na, side, start[0:1], middle[0:1], end[0:1], hot_a, stage_a)
    sb = Side(lay.nb, side, start[1:2], middle[1:2], end[1:2], hot_b, stage_b)

    live = shared[lay.live_at : lay.total, :].astype(bf16)
    height = lay.total - lay.live_at
    number = iota((LANES, LANES), 1).astype(f32)
    pick_a = [jnp.where(down(block_of[p : p + 1]) == number, 1.0, 0.0).astype(bf16) for p in (0, 1)]
    number = iota((LANES, LANES), 0).astype(f32)
    pick_b = [jnp.where(block_of[q : q + 1] == number, 1.0, 0.0).astype(bf16) for q in (2, 3)]
    wide = [dot(pick[:, :height], live, 1, 0).astype(bf16) for pick in pick_a]
    mask = [[dot(wide[p], pick_b[q], 1, 0) for q in (0, 1)] for p in (0, 1)]

    a = jnp.zeros((lay.na // LANES, LANES), f32)
    b = jnp.zeros((lay.nb // LANES, LANES), f32)
    g = jnp.zeros((NCE, NCI), f32)
    mean = jnp.zeros((4, LANES), f32)
    for newton in range(NEWTON):
        if newton == 0:
            left = flow
            weight, inv, rate = count, inv_count, mask
            sum_a, sum_b = sa.sums([flow[0]]), sb.sums([flow[1]])
            part_a, part_b = sa.expand(inv[0:1], inv[1:2]), sb.expand(inv[2:3], inv[3:4])
            m2, m3 = inv, inv * inv
            f1 = jnp.concatenate([sum_a[0:2], sum_b[0:2]], axis=0) * inv
            f2 = f1 * inv
        else:
            left = (flow[0] - RIDGE * a, flow[1] - RIDGE * b, flow[2] - RIDGE * g)
            shift_ref[0:4, :] = mean
            off_a = a - sa.expand(mean[0:1], mean[1:2])
            off_b = b - sb.expand(mean[2:3], mean[3:4])
            worst = jnp.maximum(jnp.max(off_a), jnp.max(off_b))
            val_a[...] = a
            val_b[...] = b

            @pl.when(worst > 20.0)
            def _():
                shift_ref[0:1, :] = sa.maxima(val_a, low[0:1], high[0:1])
                shift_ref[1:2, :] = sa.maxima(val_a, low[1:2], high[1:2])
                shift_ref[2:3, :] = sb.maxima(val_b, low[2:3], high[2:3])
                shift_ref[3:4, :] = sb.maxima(val_b, low[3:4], high[3:4])

            shift = shift_ref[0:4, :]
            size_a = jnp.exp(a - sa.expand(shift[0:1], shift[1:2]))
            size_b = jnp.exp(b - sb.expand(shift[2:3], shift[3:4]))

            def moments(s, x, f):
                return s.sums([x, x * x, x * x * x, x * f, x * x * f])

            sum_a, sum_b = moments(sa, size_a, left[0]), moments(sb, size_b, left[1])
            got = [jnp.concatenate([sum_a[2 * k : 2 * k + 2], sum_b[2 * k : 2 * k + 2]], axis=0) for k in range(5)]
            weight = got[0]
            inv = jnp.where(full, 1.0 / jnp.where(full, weight, 1.0), 0.0)
            part_a = size_a * sa.expand(inv[0:1], inv[1:2])
            part_b = size_b * sb.expand(inv[2:3], inv[3:4])
            inv2 = inv * inv
            m2, m3 = got[1] * inv2, got[2] * (inv2 * inv)
            f1, f2 = got[3] * inv, got[4] * inv2
            lift = [g + down(shift[p : p + 1]) for p in (0, 1)]
            rate = [
                [jnp.where(mask[p][q] > 0.5, jnp.exp(lift[p] + shift[2 + q : 3 + q]), 0.0) for q in (0, 1)]
                for p in (0, 1)
            ]
        tall = [down(weight[p : p + 1]) for p in (0, 1)]
        mu = [[rate[p][q] * (tall[p] * weight[2 + q : 3 + q]) for q in (0, 1)] for p in (0, 1)]
        mu_a = [mu[p][0] + mu[p][1] for p in (0, 1)]
        mu_b = [mu[0][q] + mu[1][q] for q in (0, 1)]
        whole = jnp.concatenate([across(mu_a[0]), across(mu_a[1]), below(mu_b[0]), below(mu_b[1])], axis=0)
        da = part_a * sa.expand(whole[0:1], whole[1:2])
        db = part_b * sb.expand(whole[2:3], whole[3:4])
        res = (left[0] - da, left[1] - db, left[2] - (mu_a[0] + mu_a[1]))
        way = res
        norm = inner(res, res)
        v = f1 - whole * m2
        w = f2 - whole * m3
        for sweep in range(CG):
            tall = [down(v[p : p + 1]) for p in (0, 1)]
            flat = [v[2 + q : 3 + q] for q in (0, 1)]
            ga = [mu[p][0] * flat[0] + mu[p][1] * flat[1] + way[2] * mu_a[p] for p in (0, 1)]
            gb = [mu[0][q] * tall[0] + mu[1][q] * tall[1] + way[2] * mu_b[q] for q in (0, 1)]
            u = jnp.concatenate([across(ga[0]), across(ga[1]), below(gb[0]), below(gb[1])], axis=0)
            image = (
                (da + RIDGE) * way[0] + part_a * sa.expand(u[0:1], u[1:2]),
                (db + RIDGE) * way[1] + part_b * sb.expand(u[2:3], u[3:4]),
                RIDGE * way[2] + (ga[0] + ga[1]) + (tall[0] * mu_a[0] + tall[1] * mu_a[1]),
            )
            step = norm / inner(way, image)
            a, b, g = a + step * way[0], b + step * way[1], g + step * way[2]
            if newton + 1 < NEWTON:
                mean = mean + step * v
            if sweep + 1 < CG:
                res = tuple(x - step * y for x, y in zip(res, image))
                fresh = inner(res, res)
                ratio = fresh / norm
                way = tuple(x + ratio * y for x, y in zip(res, way))
                norm = fresh
                v = v - step * (whole * w + RIDGE * v + u * m2) + ratio * v
    out_g[...] = g
    val_a[...] = a
    val_b[...] = b
    for out, val, at in ((out_a, val_a, where[0]), (out_b, val_b, where[1])):
        rows = out.shape[0] // LANES
        for j in range(rows):
            out[j * LANES : (j + 1) * LANES] = val[pl.ds(at * rows + j, 1), :].reshape(LANES)


def trade(x, axis):
    return lax.all_to_all(x, axis, 0, 0, tiled=True)


def add_up(x, number):
    return jnp.sum(x.reshape(number, -1, LANES), axis=0)


def copies_of(x, number):
    return jnp.broadcast_to(x[None], (number,) + x.shape).reshape(-1, LANES)


def per_device(mesh_shape, flows, routing, tile_block, exp_country, imp_country):
    slots, side = flows.shape[0], flows.shape[1]
    n_exp, n_imp = mesh_shape
    rows, cols = exp_country.shape[0], imp_country.shape[0]
    lay = Layout(rows * n_exp, cols * n_imp, side, n_exp)
    vmem = pl.BlockSpec(memory_space=pltpu.VMEM)
    inputs = (
        flows,
        routing.reshape(-1),
        tile_block,
        exp_country.reshape(-1, 1, side),
        imp_country.reshape(-1, 1, side),
    )
    homes = [pltpu.VMEM, pltpu.SMEM, pltpu.SMEM, pltpu.VMEM, pltpu.VMEM]
    shared = pl.pallas_call(
        functools.partial(local_kernel, lay, slots),
        out_shape=jax.ShapeDtypeStruct((lay.padded, LANES), f32),
        in_specs=[pl.BlockSpec(memory_space=pltpu.HBM)] * 5,
        out_specs=vmem,
        scratch_shapes=[space(x.shape, x.dtype) for space, x in zip(homes, inputs)]
        + [pltpu.SemaphoreType.DMA((5,))],
        compiler_params=pltpu.CompilerParams(vmem_limit_bytes=VMEM_BYTES),
        name="local_sums",
    )(*inputs)
    mine = add_up(trade(shared, "exp"), n_exp)
    mine = add_up(trade(copies_of(mine, n_imp), "imp"), n_imp)
    shared = trade(copies_of(mine, n_exp), "exp")
    high = 16
    a, b, g = pl.pallas_call(
        functools.partial(solve_kernel, lay),
        out_shape=(
            jax.ShapeDtypeStruct((rows,), f32),
            jax.ShapeDtypeStruct((cols,), f32),
            jax.ShapeDtypeStruct((NCE, NCI), f32),
        ),
        in_specs=[vmem],
        out_specs=(vmem, vmem, vmem),
        scratch_shapes=[
            pltpu.VMEM((lay.na, LANES), bf16),
            pltpu.VMEM((lay.nb, LANES), bf16),
            pltpu.VMEM((high * lay.na // LANES, LANES), f32),
            pltpu.VMEM((high * lay.nb // LANES, LANES), f32),
            pltpu.VMEM((lay.na // LANES, LANES), f32),
            pltpu.VMEM((lay.nb // LANES, LANES), f32),
            pltpu.VMEM((8, LANES), f32),
        ],
        compiler_params=pltpu.CompilerParams(vmem_limit_bytes=VMEM_BYTES),
        name="solve",
    )(shared)
    return a, b, g


def solution(mesh):
    placed = (
        P(("exp", "imp"), None, None),
        P(("exp", "imp"), None, None),
        P(("exp", "imp")),
        P("exp"),
        P("imp"),
    )
    return jax.shard_map(
        functools.partial(per_device, (mesh.shape["exp"], mesh.shape["imp"])),
        mesh=mesh,
        in_specs=placed,
        out_specs=(P("exp"), P("imp"), P()),
        check_vma=False,
    )
```

```python
import functools

import jax
import jax.numpy as jnp
from jax import lax
from jax.experimental import pallas as pl
from jax.experimental.pallas import tpu as pltpu
from jax.sharding import PartitionSpec as P

NCE = 128
NCI = 128
NEWTON = 2
CG = 2
LANES = 128
RIDGE = 64.0
VMEM_BYTES = 48 * 1024 * 1024

f32 = jnp.float32
bf16 = jnp.bfloat16
i32 = jnp.int32


def iota(shape, dim):
    return lax.broadcasted_iota(i32, shape, dim)


def split(x):
    hi = x.astype(bf16).astype(f32)
    rest = x - hi
    mid = rest.astype(bf16).astype(f32)
    return hi, mid, rest - mid


def dot(x, y, cx, cy, precision=None):
    return lax.dot_general(
        x, y, (((cx,), (cy,)), ((), ())), precision=precision, preferred_element_type=f32
    )


class Layout:
    def __init__(self, na, nb, side):
        self.na, self.nb, self.side = na, nb, side
        self.rows_at = NCE
        self.cols_at = self.rows_at + na // LANES
        self.cnt_at = self.cols_at + nb // LANES
        self.live_at = self.cnt_at + 2
        self.blocks_a, self.blocks_b = na // side, nb // side
        self.total = -(-(self.live_at - (-self.blocks_a * self.blocks_b // LANES)) // 8) * 8
        first = -(-self.total // 16) * 8
        self.chunks = ((0, first), (first, self.total))


def local_kernel(lay, slots, *refs):
    sources, outs, out, homes, sems = refs[:5], refs[5:7], refs[7], refs[8:13], refs[13]
    copies = [pltpu.make_async_copy(x, y, sems.at[j]) for j, (x, y) in enumerate(zip(sources, homes))]
    for copy in copies:
        copy.start()
    flows, routing, tile_block, ec, ic = homes
    exp_place, imp_place = lax.axis_index("exp"), lax.axis_index("imp")
    side = lay.side
    row_blocks = ec.shape[0]
    col_local = ic.shape[0]
    out[...] = jnp.zeros_like(out)
    per = side // LANES
    country = iota((NCE, side), 0)
    ones = jnp.ones((8, side), bf16)
    for copy in copies:
        copy.wait()
    pairs = jnp.zeros((NCE, NCI), f32)
    for k in range(slots):
        r = tile_block[k] // col_local
        c = tile_block[k] % col_local
        live = routing[0] == k
        for t in range(1, routing.shape[0]):
            live = live | (routing[t] == k)
        keep = live.astype(f32)
        hot_r = (country == ec[r]).astype(f32).astype(bf16)
        hot_c = (country == ic[c]).astype(f32).astype(bf16)
        tile = flows[k] * keep.astype(bf16)
        half = dot(hot_r, tile, 1, 0)
        col_sum = jnp.sum(half, axis=0, keepdims=True)
        row_sum = dot(ones, tile, 1, 1)[0:1]
        for piece in split(half):
            pairs = pairs + dot(piece.astype(bf16), hot_c, 1, 1)
        row_at = lay.rows_at + (exp_place * row_blocks + r) * per
        col_at = lay.cols_at + (imp_place * col_local + c) * per
        for h in range(per):
            cut = slice(h * LANES, (h + 1) * LANES)
            out[pl.ds(row_at + h, 1), :] += row_sum[:, cut]
            out[pl.ds(col_at + h, 1), :] += col_sum[:, cut]
        flat = (exp_place * row_blocks + r) * lay.blocks_b + imp_place * col_local + c
        here = iota((1, LANES), 1) == flat % LANES
        out[pl.ds(lay.live_at + flat // LANES, 1), :] += jnp.where(here, keep, 0.0)
    out[0:NCE, :] = pairs
    cnt_a = jnp.zeros((8, LANES), f32)
    for r in range(row_blocks):
        cnt_a += dot(ones, (country == ec[r]).astype(f32).astype(bf16), 1, 1)
    cnt_b = jnp.zeros((8, LANES), f32)
    for c in range(col_local):
        cnt_b += dot(ones, (country == ic[c]).astype(f32).astype(bf16), 1, 1)
    cnt_a = cnt_a[0:1] * (imp_place == 0).astype(f32)
    cnt_b = cnt_b[0:1] * (exp_place == 0).astype(f32)
    out[lay.cnt_at : lay.cnt_at + 1, :] = cnt_a
    out[lay.cnt_at + 1 : lay.cnt_at + 2, :] = cnt_b
    for part, (lo, hi) in zip(outs, lay.chunks):
        part[...] = out[lo:hi, :]


def lookup(row, index):
    return jnp.take_along_axis(
        jnp.broadcast_to(row, index.shape), index, axis=1, mode="promise_in_bounds"
    )


def down(row):
    return jnp.transpose(jnp.broadcast_to(row, (LANES, LANES)))


def across(x):
    return jnp.sum(jnp.transpose(x), axis=0, keepdims=True)


def below(x):
    return jnp.sum(x, axis=0, keepdims=True)


def eights(x):
    return functools.reduce(lambda u, v: u + v, [x[j : j + 8] for j in range(0, x.shape[0], 8)])


def inner(u, v):
    partial = eights(u[0] * v[0]) + eights(u[1] * v[1]) + eights(u[2] * v[2])
    return jnp.sum(below(partial), axis=1, keepdims=True)


class Side:
    def __init__(self, n, block, start, middle, end, hot, stage):
        self.n, self.block, self.hot, self.stage = n, block, hot, stage
        self.chunks = n // LANES
        shape = (self.chunks, LANES)
        place = (iota(shape, 0) * LANES + iota(shape, 1)).astype(f32)
        country = jnp.zeros(shape, i32)
        jump = LANES // 2
        while jump:
            passed = lookup(end, country + (jump - 1)) <= place
            country = jnp.where(passed, country + jump, country)
            jump //= 2
        self.country = country
        self.second = place >= lookup(middle, country)
        for j in range(n // block):
            at = (iota((block, LANES), 0) + j * block).astype(f32)
            inside = (at >= start) & (at < end)
            hot[j * block : (j + 1) * block, :] = jnp.where(inside, 1.0, 0.0).astype(bf16)

    def expand(self, first, second):
        return jnp.where(self.second, lookup(second, self.country), lookup(first, self.country))

    def sums(self, vectors):
        chunks, stage = self.chunks, self.stage
        for k, v in enumerate(vectors):
            stage[2 * k * chunks : (2 * k + 1) * chunks, :] = jnp.where(self.second, 0.0, v)
            stage[(2 * k + 1) * chunks : (2 * k + 2) * chunks, :] = jnp.where(self.second, v, 0.0)
        high = -(-2 * len(vectors) // 8) * 8
        for k in range(2 * len(vectors), high):
            stage[k * chunks : (k + 1) * chunks, :] = jnp.zeros((chunks, LANES), f32)
        got = jnp.zeros((3 * high, LANES), f32)
        per = self.block // LANES
        for j in range(chunks // per):
            left = jnp.concatenate(
                [stage[pl.ds(j * per + h, high, stride=chunks), :] for h in range(per)], axis=1
            )
            pieces = jnp.concatenate(split(left), axis=0).astype(bf16)
            got += dot(pieces, self.hot[j * self.block : (j + 1) * self.block, :], 1, 0)
        return got[:high] + got[high : 2 * high] + got[2 * high :]

    def maxima(self, values_ref, low, high):
        low, high = down(low), down(high)

        def body(j, best):
            at = (iota((LANES, LANES), 1) + j * LANES).astype(f32)
            inside = (at >= low) & (at < high)
            return jnp.maximum(best, jnp.where(inside, values_ref[pl.ds(j, 1), :], -jnp.inf))

        best = lax.fori_loop(0, self.chunks, body, jnp.full((LANES, LANES), -jnp.inf, f32))
        best = jnp.max(jnp.transpose(best), axis=0, keepdims=True)
        return jnp.where(best > -jnp.inf, best, 0.0)


def solve_kernel(lay, *refs):
    where = lax.axis_index("exp"), lax.axis_index("imp")
    own, given, refs = refs[:2], refs[2:4], refs[4:]
    out_a, out_b, out_g, shared, hot_a, hot_b, stage_a, stage_b, val_a, val_b, shift_ref = refs
    outer = where[0] % 2 == 1
    for x, y, (lo, hi) in zip(own, given, lay.chunks):
        shared[lo:hi, :] = jnp.where(outer, x[...], y[...])
    flow = (
        shared[lay.rows_at : lay.cols_at, :],
        shared[lay.cols_at : lay.cnt_at, :],
        shared[0:NCE, :],
    )
    side = lay.side
    tally = shared[lay.cnt_at : lay.cnt_at + 8, :]
    before = jnp.where(iota((LANES, LANES), 0) < iota((LANES, LANES), 1), 1.0, 0.0).astype(bf16)
    start = dot(tally.astype(bf16), before, 1, 0)
    end = start + tally
    first = jnp.floor((start + 0.5) * (1.0 / side))
    middle = jnp.minimum(end, (first + 1.0) * side)

    def table(x, y):
        return jnp.concatenate([x[0:1], y[0:1], x[1:2], y[1:2]], axis=0)

    low, high = table(start, middle), table(middle, end)
    count = high - low
    full = count > 0.5
    inv_count = jnp.where(full, 1.0 / jnp.maximum(count, 1.0), 0.0)
    block_of = jnp.where(full, table(first, first + 1.0), -1.0)
    sa = Side(lay.na, side, start[0:1], middle[0:1], end[0:1], hot_a, stage_a)
    sb = Side(lay.nb, side, start[1:2], middle[1:2], end[1:2], hot_b, stage_b)

    wide = lay.blocks_b
    spots = [(r * wide // LANES, r * wide % LANES) for r in range(lay.blocks_a)]
    live = jnp.concatenate(
        [shared[lay.live_at + row : lay.live_at + row + 1, at : at + wide] for row, at in spots], axis=0
    ).astype(bf16)
    number = iota((LANES, LANES), 1).astype(f32)
    pick_a = [jnp.where(down(block_of[p : p + 1]) == number, 1.0, 0.0).astype(bf16) for p in (0, 1)]
    number = iota((LANES, LANES), 0).astype(f32)
    pick_b = [jnp.where(block_of[q : q + 1] == number, 1.0, 0.0).astype(bf16) for q in (2, 3)]
    reach = [dot(pick[:, : lay.blocks_a], live, 1, 0).astype(bf16) for pick in pick_a]
    mask = [[dot(reach[p], pick_b[q][: lay.blocks_b], 1, 0) for q in (0, 1)] for p in (0, 1)]

    a = jnp.zeros((lay.na // LANES, LANES), f32)
    b = jnp.zeros((lay.nb // LANES, LANES), f32)
    g = jnp.zeros((NCE, NCI), f32)
    mean = jnp.zeros((4, LANES), f32)
    for newton in range(NEWTON):
        if newton == 0:
            left = flow
            weight, inv, rate = count, inv_count, mask
            sum_a, sum_b = sa.sums([flow[0]]), sb.sums([flow[1]])
            part_a, part_b = sa.expand(inv[0:1], inv[1:2]), sb.expand(inv[2:3], inv[3:4])
            m2, m3 = inv, inv * inv
            f1 = jnp.concatenate([sum_a[0:2], sum_b[0:2]], axis=0) * inv
            f2 = f1 * inv
        else:
            left = (flow[0] - RIDGE * a, flow[1] - RIDGE * b, flow[2] - RIDGE * g)
            shift_ref[0:4, :] = mean
            off_a = a - sa.expand(mean[0:1], mean[1:2])
            off_b = b - sb.expand(mean[2:3], mean[3:4])
            worst = jnp.maximum(jnp.max(off_a), jnp.max(off_b))
            val_a[...] = a
            val_b[...] = b

            @pl.when(worst > 20.0)
            def _():
                shift_ref[0:1, :] = sa.maxima(val_a, low[0:1], high[0:1])
                shift_ref[1:2, :] = sa.maxima(val_a, low[1:2], high[1:2])
                shift_ref[2:3, :] = sb.maxima(val_b, low[2:3], high[2:3])
                shift_ref[3:4, :] = sb.maxima(val_b, low[3:4], high[3:4])

            shift = shift_ref[0:4, :]
            size_a = jnp.exp(a - sa.expand(shift[0:1], shift[1:2]))
            size_b = jnp.exp(b - sb.expand(shift[2:3], shift[3:4]))

            def moments(s, x, f):
                return s.sums([x, x * x, x * x * x, x * f, x * x * f])

            sum_a, sum_b = moments(sa, size_a, left[0]), moments(sb, size_b, left[1])
            got = [jnp.concatenate([sum_a[2 * k : 2 * k + 2], sum_b[2 * k : 2 * k + 2]], axis=0) for k in range(5)]
            weight = got[0]
            inv = jnp.where(full, 1.0 / jnp.where(full, weight, 1.0), 0.0)
            part_a = size_a * sa.expand(inv[0:1], inv[1:2])
            part_b = size_b * sb.expand(inv[2:3], inv[3:4])
            inv2 = inv * inv
            m2, m3 = got[1] * inv2, got[2] * (inv2 * inv)
            f1, f2 = got[3] * inv, got[4] * inv2
            lift = [g + down(shift[p : p + 1]) for p in (0, 1)]
            rate = [
                [jnp.where(mask[p][q] > 0.5, jnp.exp(lift[p] + shift[2 + q : 3 + q]), 0.0) for q in (0, 1)]
                for p in (0, 1)
            ]
        tall = [down(weight[p : p + 1]) for p in (0, 1)]
        mu = [[rate[p][q] * (tall[p] * weight[2 + q : 3 + q]) for q in (0, 1)] for p in (0, 1)]
        mu_a = [mu[p][0] + mu[p][1] for p in (0, 1)]
        mu_b = [mu[0][q] + mu[1][q] for q in (0, 1)]
        whole = jnp.concatenate([across(mu_a[0]), across(mu_a[1]), below(mu_b[0]), below(mu_b[1])], axis=0)
        da = part_a * sa.expand(whole[0:1], whole[1:2])
        db = part_b * sb.expand(whole[2:3], whole[3:4])
        res = (left[0] - da, left[1] - db, left[2] - (mu_a[0] + mu_a[1]))
        way = res
        norm = inner(res, res)
        v = f1 - whole * m2
        w = f2 - whole * m3
        for sweep in range(CG):
            tall = [down(v[p : p + 1]) for p in (0, 1)]
            flat = [v[2 + q : 3 + q] for q in (0, 1)]
            ga = [mu[p][0] * flat[0] + mu[p][1] * flat[1] + way[2] * mu_a[p] for p in (0, 1)]
            gb = [mu[0][q] * tall[0] + mu[1][q] * tall[1] + way[2] * mu_b[q] for q in (0, 1)]
            u = jnp.concatenate([across(ga[0]), across(ga[1]), below(gb[0]), below(gb[1])], axis=0)
            image = (
                (da + RIDGE) * way[0] + part_a * sa.expand(u[0:1], u[1:2]),
                (db + RIDGE) * way[1] + part_b * sb.expand(u[2:3], u[3:4]),
                RIDGE * way[2] + (ga[0] + ga[1]) + (tall[0] * mu_a[0] + tall[1] * mu_a[1]),
            )
            step = norm / inner(way, image)
            a, b, g = a + step * way[0], b + step * way[1], g + step * way[2]
            if newton + 1 < NEWTON:
                mean = mean + step * v
            if sweep + 1 < CG:
                res = tuple(x - step * y for x, y in zip(res, image))
                fresh = inner(res, res)
                ratio = fresh / norm
                way = tuple(x + ratio * y for x, y in zip(res, way))
                norm = fresh
                v = v - step * (whole * w + RIDGE * v + u * m2) + ratio * v
    out_g[...] = g
    val_a[...] = a
    val_b[...] = b
    for out, val, at in ((out_a, val_a, where[0]), (out_b, val_b, where[1])):
        rows = out.shape[0] // LANES
        for j in range(rows):
            out[j * LANES : (j + 1) * LANES] = val[pl.ds(at * rows + j, 1), :].reshape(LANES)


def hand_over(x, n_exp, core):
    return lax.ppermute(x, "exp", [(d, d ^ 1) for d in range(n_exp) if d % 2 == core])


def swap(x, axis, n_exp, n_imp, bits):
    pairs = []
    for e in range(1, n_exp, 2):
        for m in range(n_imp):
            to = (e ^ bits, m) if axis == "exp" else (e, m ^ bits)
            pairs.append((e * n_imp + m, to[0] * n_imp + to[1]))
    return lax.ppermute(x, ("exp", "imp"), pairs)


def per_device(mesh_shape, flows, routing, tile_block, exp_country, imp_country):
    slots, side = flows.shape[0], flows.shape[1]
    n_exp, n_imp = mesh_shape
    rows, cols = exp_country.shape[0], imp_country.shape[0]
    lay = Layout(rows * n_exp, cols * n_imp, side)
    vmem = pl.BlockSpec(memory_space=pltpu.VMEM)
    inputs = (
        flows,
        routing.reshape(-1),
        tile_block,
        exp_country.reshape(-1, 1, side),
        imp_country.reshape(-1, 1, side),
    )
    homes = [pltpu.VMEM, pltpu.SMEM, pltpu.SMEM, pltpu.VMEM, pltpu.VMEM]
    parts = pl.pallas_call(
        functools.partial(local_kernel, lay, slots),
        out_shape=[jax.ShapeDtypeStruct((hi - lo, LANES), f32) for lo, hi in lay.chunks],
        in_specs=[pl.BlockSpec(memory_space=pltpu.HBM)] * 5,
        out_specs=[vmem] * 2,
        scratch_shapes=[pltpu.VMEM((lay.total, LANES), f32)]
        + [space(x.shape, x.dtype) for space, x in zip(homes, inputs)]
        + [pltpu.SemaphoreType.DMA((5,))],
        compiler_params=pltpu.CompilerParams(vmem_limit_bytes=VMEM_BYTES),
        name="local_sums",
    )(*inputs)
    own, given = [], []
    for x in parts:
        x = x + hand_over(x, n_exp, 0)
        for axis, size, bit in (("imp", n_imp, 1), ("exp", n_exp, 2)):
            while bit < size:
                x = x + swap(x, axis, n_exp, n_imp, bit)
                bit *= 2
        own.append(x)
        given.append(hand_over(x, n_exp, 1))
    high = 16
    a, b, g = pl.pallas_call(
        functools.partial(solve_kernel, lay),
        out_shape=(
            jax.ShapeDtypeStruct((rows,), f32),
            jax.ShapeDtypeStruct((cols,), f32),
            jax.ShapeDtypeStruct((NCE, NCI), f32),
        ),
        in_specs=[vmem] * 4,
        out_specs=(vmem, vmem, vmem),
        scratch_shapes=[
            pltpu.VMEM((lay.total, LANES), f32),
            pltpu.VMEM((lay.na, LANES), bf16),
            pltpu.VMEM((lay.nb, LANES), bf16),
            pltpu.VMEM((high * lay.na // LANES, LANES), f32),
            pltpu.VMEM((high * lay.nb // LANES, LANES), f32),
            pltpu.VMEM((lay.na // LANES, LANES), f32),
            pltpu.VMEM((lay.nb // LANES, LANES), f32),
            pltpu.VMEM((8, LANES), f32),
        ],
        compiler_params=pltpu.CompilerParams(vmem_limit_bytes=VMEM_BYTES),
        name="solve",
    )(*own, *given)
    return a, b, g


def solution(mesh):
    placed = (
        P(("exp", "imp"), None, None),
        P(("exp", "imp"), None, None),
        P(("exp", "imp")),
        P("exp"),
        P("imp"),
    )
    return jax.shard_map(
        functools.partial(per_device, (mesh.shape["exp"], mesh.shape["imp"])),
        mesh=mesh,
        in_specs=placed,
        out_specs=(P("exp"), P("imp"), P()),
        check_vma=False,
    )
```

```python
import functools

import jax
import jax.numpy as jnp
from jax import lax
from jax.experimental import pallas as pl
from jax.experimental.pallas import tpu as pltpu
from jax.sharding import PartitionSpec as P

NCE = 128
NCI = 128
NEWTON = 2
CG = 2
LANES = 128
RIDGE = 64.0
VMEM_BYTES = 48 * 1024 * 1024

f32 = jnp.float32
bf16 = jnp.bfloat16
i32 = jnp.int32


def iota(shape, dim):
    return lax.broadcasted_iota(i32, shape, dim)


def split(x):
    hi = x.astype(bf16).astype(f32)
    rest = x - hi
    mid = rest.astype(bf16).astype(f32)
    return hi, mid, rest - mid


def dot(x, y, cx, cy, precision=None):
    return lax.dot_general(
        x, y, (((cx,), (cy,)), ((), ())), precision=precision, preferred_element_type=f32
    )


class Layout:
    def __init__(self, na, nb, side):
        self.na, self.nb, self.side = na, nb, side
        self.rows_at = NCE
        self.cols_at = self.rows_at + na // LANES
        self.cnt_at = self.cols_at + nb // LANES
        self.live_at = self.cnt_at + 2
        self.blocks_a, self.blocks_b = na // side, nb // side
        self.total = -(-(self.live_at - (-self.blocks_a * self.blocks_b // LANES)) // 8) * 8
        first = -(-self.total // 16) * 8
        self.chunks = ((0, first), (first, self.total))


def local_kernel(lay, slots, *refs):
    sources, outs, out, homes, sems = refs[:5], refs[5:7], refs[7], refs[8:13], refs[13]
    copies = [pltpu.make_async_copy(x, y, sems.at[j]) for j, (x, y) in enumerate(zip(sources, homes))]
    for copy in copies:
        copy.start()
    flows, routing, tile_block, ec, ic = homes
    exp_place, imp_place = lax.axis_index("exp"), lax.axis_index("imp")
    side = lay.side
    row_blocks = ec.shape[0]
    col_local = ic.shape[0]
    out[...] = jnp.zeros_like(out)
    per = side // LANES
    country = iota((NCE, side), 0)
    ones = jnp.ones((8, side), bf16)
    for copy in copies:
        copy.wait()
    pairs = jnp.zeros((NCE, NCI), f32)
    for k in range(slots):
        r = tile_block[k] // col_local
        c = tile_block[k] % col_local
        live = routing[0] == k
        for t in range(1, routing.shape[0]):
            live = live | (routing[t] == k)
        keep = live.astype(f32)
        hot_r = (country == ec[r]).astype(f32).astype(bf16)
        hot_c = (country == ic[c]).astype(f32).astype(bf16)
        tile = flows[k] * keep.astype(bf16)
        half = dot(hot_r, tile, 1, 0)
        col_sum = jnp.sum(half, axis=0, keepdims=True)
        row_sum = dot(ones, tile, 1, 1)[0:1]
        for piece in split(half):
            pairs = pairs + dot(piece.astype(bf16), hot_c, 1, 1)
        row_at = lay.rows_at + (exp_place * row_blocks + r) * per
        col_at = lay.cols_at + (imp_place * col_local + c) * per
        for h in range(per):
            cut = slice(h * LANES, (h + 1) * LANES)
            out[pl.ds(row_at + h, 1), :] += row_sum[:, cut]
            out[pl.ds(col_at + h, 1), :] += col_sum[:, cut]
        flat = (exp_place * row_blocks + r) * lay.blocks_b + imp_place * col_local + c
        here = iota((1, LANES), 1) == flat % LANES
        out[pl.ds(lay.live_at + flat // LANES, 1), :] += jnp.where(here, keep, 0.0)
    out[0:NCE, :] = pairs
    cnt_a = jnp.zeros((8, LANES), f32)
    for r in range(row_blocks):
        cnt_a += dot(ones, (country == ec[r]).astype(f32).astype(bf16), 1, 1)
    cnt_b = jnp.zeros((8, LANES), f32)
    for c in range(col_local):
        cnt_b += dot(ones, (country == ic[c]).astype(f32).astype(bf16), 1, 1)
    cnt_a = cnt_a[0:1] * (imp_place == 0).astype(f32)
    cnt_b = cnt_b[0:1] * (exp_place == 0).astype(f32)
    out[lay.cnt_at : lay.cnt_at + 1, :] = cnt_a
    out[lay.cnt_at + 1 : lay.cnt_at + 2, :] = cnt_b
    for part, (lo, hi) in zip(outs, lay.chunks):
        part[...] = out[lo:hi, :]


def lookup(row, index):
    return jnp.take_along_axis(
        jnp.broadcast_to(row, index.shape), index, axis=1, mode="promise_in_bounds"
    )


def down(row):
    return jnp.transpose(jnp.broadcast_to(row, (LANES, LANES)))


def across(x):
    return jnp.sum(jnp.transpose(x), axis=0, keepdims=True)


def below(x):
    return jnp.sum(x, axis=0, keepdims=True)


def eights(x):
    return functools.reduce(lambda u, v: u + v, [x[j : j + 8] for j in range(0, x.shape[0], 8)])


def inner(u, v):
    partial = eights(u[0] * v[0]) + eights(u[1] * v[1]) + eights(u[2] * v[2])
    return jnp.sum(below(partial), axis=1, keepdims=True)


class Side:
    def __init__(self, n, block, start, middle, end, hot, stage):
        self.n, self.block, self.hot, self.stage = n, block, hot, stage
        self.chunks = n // LANES
        shape = (self.chunks, LANES)
        place = (iota(shape, 0) * LANES + iota(shape, 1)).astype(f32)
        country = jnp.zeros(shape, i32)
        jump = LANES // 2
        while jump:
            passed = lookup(end, country + (jump - 1)) <= place
            country = jnp.where(passed, country + jump, country)
            jump //= 2
        self.country = country
        self.second = place >= lookup(middle, country)
        for j in range(n // block):
            at = (iota((block, LANES), 0) + j * block).astype(f32)
            inside = (at >= start) & (at < end)
            hot[j * block : (j + 1) * block, :] = jnp.where(inside, 1.0, 0.0).astype(bf16)

    def expand(self, first, second):
        return jnp.where(self.second, lookup(second, self.country), lookup(first, self.country))

    def sums(self, vectors):
        chunks, stage = self.chunks, self.stage
        for k, v in enumerate(vectors):
            stage[2 * k * chunks : (2 * k + 1) * chunks, :] = jnp.where(self.second, 0.0, v)
            stage[(2 * k + 1) * chunks : (2 * k + 2) * chunks, :] = jnp.where(self.second, v, 0.0)
        high = -(-2 * len(vectors) // 8) * 8
        for k in range(2 * len(vectors), high):
            stage[k * chunks : (k + 1) * chunks, :] = jnp.zeros((chunks, LANES), f32)
        got = jnp.zeros((3 * high, LANES), f32)
        per = self.block // LANES
        for j in range(chunks // per):
            left = jnp.concatenate(
                [stage[pl.ds(j * per + h, high, stride=chunks), :] for h in range(per)], axis=1
            )
            pieces = jnp.concatenate(split(left), axis=0).astype(bf16)
            got += dot(pieces, self.hot[j * self.block : (j + 1) * self.block, :], 1, 0)
        return got[:high] + got[high : 2 * high] + got[2 * high :]

    def maxima(self, values_ref, low, high):
        low, high = down(low), down(high)

        def body(j, best):
            at = (iota((LANES, LANES), 1) + j * LANES).astype(f32)
            inside = (at >= low) & (at < high)
            return jnp.maximum(best, jnp.where(inside, values_ref[pl.ds(j, 1), :], -jnp.inf))

        best = lax.fori_loop(0, self.chunks, body, jnp.full((LANES, LANES), -jnp.inf, f32))
        best = jnp.max(jnp.transpose(best), axis=0, keepdims=True)
        return jnp.where(best > -jnp.inf, best, 0.0)


def solve_kernel(lay, *refs):
    where = lax.axis_index("exp"), lax.axis_index("imp")
    own, given, refs = refs[:2], refs[2:4], refs[4:]
    out_a, out_b, out_g, shared, hot_a, hot_b, stage_a, stage_b, val_a, val_b, shift_ref = refs
    outer = where[0] % 2 == 1
    for x, y, (lo, hi) in zip(own, given, lay.chunks):
        shared[lo:hi, :] = jnp.where(outer, x[...], y[...])
    flow = (
        shared[lay.rows_at : lay.cols_at, :],
        shared[lay.cols_at : lay.cnt_at, :],
        shared[0:NCE, :],
    )
    side = lay.side
    tally = shared[lay.cnt_at : lay.cnt_at + 8, :]
    before = jnp.where(iota((LANES, LANES), 0) < iota((LANES, LANES), 1), 1.0, 0.0).astype(bf16)
    start = dot(tally.astype(bf16), before, 1, 0)
    end = start + tally
    first = jnp.floor((start + 0.5) * (1.0 / side))
    middle = jnp.minimum(end, (first + 1.0) * side)

    def table(x, y):
        return jnp.concatenate([x[0:1], y[0:1], x[1:2], y[1:2]], axis=0)

    low, high = table(start, middle), table(middle, end)
    count = high - low
    full = count > 0.5
    inv_count = jnp.where(full, 1.0 / jnp.maximum(count, 1.0), 0.0)
    block_of = jnp.where(full, table(first, first + 1.0), -1.0)
    sa = Side(lay.na, side, start[0:1], middle[0:1], end[0:1], hot_a, stage_a)
    sb = Side(lay.nb, side, start[1:2], middle[1:2], end[1:2], hot_b, stage_b)

    wide = lay.blocks_b
    spots = [(r * wide // LANES, r * wide % LANES) for r in range(lay.blocks_a)]
    live = jnp.concatenate(
        [shared[lay.live_at + row : lay.live_at + row + 1, at : at + wide] for row, at in spots], axis=0
    ).astype(bf16)
    number = iota((LANES, LANES), 1).astype(f32)
    pick_a = [jnp.where(down(block_of[p : p + 1]) == number, 1.0, 0.0).astype(bf16) for p in (0, 1)]
    number = iota((LANES, LANES), 0).astype(f32)
    pick_b = [jnp.where(block_of[q : q + 1] == number, 1.0, 0.0).astype(bf16) for q in (2, 3)]
    reach = [dot(pick[:, : lay.blocks_a], live, 1, 0).astype(bf16) for pick in pick_a]
    mask = [[dot(reach[p], pick_b[q][: lay.blocks_b], 1, 0) for q in (0, 1)] for p in (0, 1)]

    a = jnp.zeros((lay.na // LANES, LANES), f32)
    b = jnp.zeros((lay.nb // LANES, LANES), f32)
    g = jnp.zeros((NCE, NCI), f32)
    mean = jnp.zeros((4, LANES), f32)
    for newton in range(NEWTON):
        if newton == 0:
            left = flow
            weight, inv, rate = count, inv_count, mask
            sum_a, sum_b = sa.sums([flow[0]]), sb.sums([flow[1]])
            part_a, part_b = sa.expand(inv[0:1], inv[1:2]), sb.expand(inv[2:3], inv[3:4])
            m2, m3 = inv, inv * inv
            f1 = jnp.concatenate([sum_a[0:2], sum_b[0:2]], axis=0) * inv
            f2 = f1 * inv
        else:
            left = (flow[0] - RIDGE * a, flow[1] - RIDGE * b, flow[2] - RIDGE * g)
            shift_ref[0:4, :] = mean
            off_a = a - sa.expand(mean[0:1], mean[1:2])
            off_b = b - sb.expand(mean[2:3], mean[3:4])
            worst = jnp.maximum(jnp.max(off_a), jnp.max(off_b))
            val_a[...] = a
            val_b[...] = b

            @pl.when(worst > 20.0)
            def _():
                shift_ref[0:1, :] = sa.maxima(val_a, low[0:1], high[0:1])
                shift_ref[1:2, :] = sa.maxima(val_a, low[1:2], high[1:2])
                shift_ref[2:3, :] = sb.maxima(val_b, low[2:3], high[2:3])
                shift_ref[3:4, :] = sb.maxima(val_b, low[3:4], high[3:4])

            shift = shift_ref[0:4, :]
            size_a = jnp.exp(a - sa.expand(shift[0:1], shift[1:2]))
            size_b = jnp.exp(b - sb.expand(shift[2:3], shift[3:4]))

            def moments(s, x, f):
                return s.sums([x, x * x, x * x * x, x * f, x * x * f])

            sum_a, sum_b = moments(sa, size_a, left[0]), moments(sb, size_b, left[1])
            got = [jnp.concatenate([sum_a[2 * k : 2 * k + 2], sum_b[2 * k : 2 * k + 2]], axis=0) for k in range(5)]
            weight = got[0]
            inv = jnp.where(full, 1.0 / jnp.where(full, weight, 1.0), 0.0)
            part_a = size_a * sa.expand(inv[0:1], inv[1:2])
            part_b = size_b * sb.expand(inv[2:3], inv[3:4])
            inv2 = inv * inv
            m2, m3 = got[1] * inv2, got[2] * (inv2 * inv)
            f1, f2 = got[3] * inv, got[4] * inv2
            lift = [g + down(shift[p : p + 1]) for p in (0, 1)]
            rate = [
                [jnp.where(mask[p][q] > 0.5, jnp.exp(lift[p] + shift[2 + q : 3 + q]), 0.0) for q in (0, 1)]
                for p in (0, 1)
            ]
        tall = [down(weight[p : p + 1]) for p in (0, 1)]
        mu = [[rate[p][q] * (tall[p] * weight[2 + q : 3 + q]) for q in (0, 1)] for p in (0, 1)]
        mu_a = [mu[p][0] + mu[p][1] for p in (0, 1)]
        mu_b = [mu[0][q] + mu[1][q] for q in (0, 1)]
        whole = jnp.concatenate([across(mu_a[0]), across(mu_a[1]), below(mu_b[0]), below(mu_b[1])], axis=0)
        da = part_a * sa.expand(whole[0:1], whole[1:2])
        db = part_b * sb.expand(whole[2:3], whole[3:4])
        res = (left[0] - da, left[1] - db, left[2] - (mu_a[0] + mu_a[1]))
        way = res
        norm = inner(res, res)
        v = f1 - whole * m2
        w = f2 - whole * m3
        for sweep in range(CG):
            tall = [down(v[p : p + 1]) for p in (0, 1)]
            flat = [v[2 + q : 3 + q] for q in (0, 1)]
            ga = [mu[p][0] * flat[0] + mu[p][1] * flat[1] + way[2] * mu_a[p] for p in (0, 1)]
            gb = [mu[0][q] * tall[0] + mu[1][q] * tall[1] + way[2] * mu_b[q] for q in (0, 1)]
            u = jnp.concatenate([across(ga[0]), across(ga[1]), below(gb[0]), below(gb[1])], axis=0)
            image = (
                (da + RIDGE) * way[0] + part_a * sa.expand(u[0:1], u[1:2]),
                (db + RIDGE) * way[1] + part_b * sb.expand(u[2:3], u[3:4]),
                RIDGE * way[2] + (ga[0] + ga[1]) + (tall[0] * mu_a[0] + tall[1] * mu_a[1]),
            )
            step = norm / inner(way, image)
            a, b, g = a + step * way[0], b + step * way[1], g + step * way[2]
            if newton + 1 < NEWTON:
                mean = mean + step * v
            if sweep + 1 < CG:
                res = tuple(x - step * y for x, y in zip(res, image))
                fresh = inner(res, res)
                ratio = fresh / norm
                way = tuple(x + ratio * y for x, y in zip(res, way))
                norm = fresh
                v = v - step * (whole * w + RIDGE * v + u * m2) + ratio * v
    out_g[...] = g
    val_a[...] = a
    val_b[...] = b
    for out, val, at in ((out_a, val_a, where[0]), (out_b, val_b, where[1])):
        rows = out.shape[0] // LANES
        for j in range(rows):
            out[j * LANES : (j + 1) * LANES] = val[pl.ds(at * rows + j, 1), :].reshape(LANES)


def hand_over(x, n_exp):
    return lax.ppermute(x, "exp", [(d, d ^ 1) for d in range(n_exp)])


def swap(x, axis, n_exp, n_imp, bits):
    pairs = []
    for e in range(n_exp):
        for m in range(n_imp):
            to = (e ^ bits, m) if axis == "exp" else (e, m ^ bits)
            to = to if e % 2 else (e, m)
            pairs.append((e * n_imp + m, to[0] * n_imp + to[1]))
    return lax.ppermute(x, ("exp", "imp"), pairs)


def per_device(mesh_shape, flows, routing, tile_block, exp_country, imp_country):
    slots, side = flows.shape[0], flows.shape[1]
    n_exp, n_imp = mesh_shape
    rows, cols = exp_country.shape[0], imp_country.shape[0]
    lay = Layout(rows * n_exp, cols * n_imp, side)
    vmem = pl.BlockSpec(memory_space=pltpu.VMEM)
    inputs = (
        flows,
        routing.reshape(-1),
        tile_block,
        exp_country.reshape(-1, 1, side),
        imp_country.reshape(-1, 1, side),
    )
    homes = [pltpu.VMEM, pltpu.SMEM, pltpu.SMEM, pltpu.VMEM, pltpu.VMEM]
    parts = pl.pallas_call(
        functools.partial(local_kernel, lay, slots),
        out_shape=[jax.ShapeDtypeStruct((hi - lo, LANES), f32) for lo, hi in lay.chunks],
        in_specs=[pl.BlockSpec(memory_space=pltpu.HBM)] * 5,
        out_specs=[vmem] * 2,
        scratch_shapes=[pltpu.VMEM((lay.total, LANES), f32)]
        + [space(x.shape, x.dtype) for space, x in zip(homes, inputs)]
        + [pltpu.SemaphoreType.DMA((5,))],
        compiler_params=pltpu.CompilerParams(vmem_limit_bytes=VMEM_BYTES),
        name="local_sums",
    )(*inputs)
    own, given = [], []
    for x in parts:
        x = x + hand_over(x, n_exp)
        for axis, size, bit in (("imp", n_imp, 1), ("exp", n_exp, 2)):
            while bit < size:
                x = x + swap(x, axis, n_exp, n_imp, bit)
                bit *= 2
        own.append(x)
        given.append(hand_over(x, n_exp))
    high = 16
    a, b, g = pl.pallas_call(
        functools.partial(solve_kernel, lay),
        out_shape=(
            jax.ShapeDtypeStruct((rows,), f32),
            jax.ShapeDtypeStruct((cols,), f32),
            jax.ShapeDtypeStruct((NCE, NCI), f32),
        ),
        in_specs=[vmem] * 4,
        out_specs=(vmem, vmem, vmem),
        scratch_shapes=[
            pltpu.VMEM((lay.total, LANES), f32),
            pltpu.VMEM((lay.na, LANES), bf16),
            pltpu.VMEM((lay.nb, LANES), bf16),
            pltpu.VMEM((high * lay.na // LANES, LANES), f32),
            pltpu.VMEM((high * lay.nb // LANES, LANES), f32),
            pltpu.VMEM((lay.na // LANES, LANES), f32),
            pltpu.VMEM((lay.nb // LANES, LANES), f32),
            pltpu.VMEM((8, LANES), f32),
        ],
        compiler_params=pltpu.CompilerParams(vmem_limit_bytes=VMEM_BYTES),
        name="solve",
    )(*own, *given)
    return a, b, g


def solution(mesh):
    placed = (
        P(("exp", "imp"), None, None),
        P(("exp", "imp"), None, None),
        P(("exp", "imp")),
        P("exp"),
        P("imp"),
    )
    return jax.shard_map(
        functools.partial(per_device, (mesh.shape["exp"], mesh.shape["imp"])),
        mesh=mesh,
        in_specs=placed,
        out_specs=(P("exp"), P("imp"), P()),
        check_vma=False,
    )
```

```python
import functools

import jax
import jax.numpy as jnp
from jax import lax
from jax.experimental import pallas as pl
from jax.experimental.pallas import tpu as pltpu
from jax.sharding import PartitionSpec as P

NCE = 128
NCI = 128
NEWTON = 2
CG = 2
LANES = 128
RIDGE = 64.0
VMEM_BYTES = 48 * 1024 * 1024
LOCAL_BYTES = 56 * 1024 * 1024

f32 = jnp.float32
bf16 = jnp.bfloat16
i32 = jnp.int32


def iota(shape, dim):
    return lax.broadcasted_iota(i32, shape, dim)


def split(x):
    hi = x.astype(bf16).astype(f32)
    rest = x - hi
    mid = rest.astype(bf16).astype(f32)
    return hi, mid, rest - mid


def dot(x, y, cx, cy, precision=None):
    return lax.dot_general(
        x, y, (((cx,), (cy,)), ((), ())), precision=precision, preferred_element_type=f32
    )


class Layout:
    def __init__(self, na, nb, side):
        self.na, self.nb, self.side = na, nb, side
        self.rows_at = NCE
        self.cols_at = self.rows_at + na // LANES
        self.cnt_at = self.cols_at + nb // LANES
        self.live_at = self.cnt_at + 2
        self.blocks_a, self.blocks_b = na // side, nb // side
        self.total = -(-(self.live_at - (-self.blocks_a * self.blocks_b // LANES)) // 8) * 8
        self.share = -(-self.total // 16) * 8


def half_of(exp_place, imp_place):
    bits = exp_place ^ imp_place
    for shift in (8, 4, 2, 1):
        bits = bits ^ (bits >> shift)
    return bits & 1


def local_kernel(lay, slots, *refs):
    sources, outs, out, homes, sems = refs[:5], refs[5:7], refs[7], refs[8:13], refs[13]
    copies = [pltpu.make_async_copy(x, y, sems.at[j]) for j, (x, y) in enumerate(zip(sources, homes))]
    for copy in copies:
        copy.start()
    flows, routing, tile_block, ec, ic = homes
    exp_place, imp_place = lax.axis_index("exp"), lax.axis_index("imp")
    side = lay.side
    row_blocks = ec.shape[0]
    col_local = ic.shape[0]
    out[...] = jnp.zeros_like(out)
    per = side // LANES
    country = iota((NCE, side), 0)
    ones = jnp.ones((8, side), bf16)
    for copy in copies:
        copy.wait()
    pairs = jnp.zeros((NCE, NCI), f32)
    for k in range(slots):
        r = tile_block[k] // col_local
        c = tile_block[k] % col_local
        live = routing[0] == k
        for t in range(1, routing.shape[0]):
            live = live | (routing[t] == k)
        keep = live.astype(f32)
        hot_r = (country == ec[r]).astype(f32).astype(bf16)
        hot_c = (country == ic[c]).astype(f32).astype(bf16)
        tile = flows[k] * keep.astype(bf16)
        half = dot(hot_r, tile, 1, 0)
        col_sum = jnp.sum(half, axis=0, keepdims=True)
        row_sum = dot(ones, tile, 1, 1)[0:1]
        for piece in split(half):
            pairs = pairs + dot(piece.astype(bf16), hot_c, 1, 1)
        row_at = lay.rows_at + (exp_place * row_blocks + r) * per
        col_at = lay.cols_at + (imp_place * col_local + c) * per
        for h in range(per):
            cut = slice(h * LANES, (h + 1) * LANES)
            out[pl.ds(row_at + h, 1), :] += row_sum[:, cut]
            out[pl.ds(col_at + h, 1), :] += col_sum[:, cut]
        flat = (exp_place * row_blocks + r) * lay.blocks_b + imp_place * col_local + c
        here = iota((1, LANES), 1) == flat % LANES
        out[pl.ds(lay.live_at + flat // LANES, 1), :] += jnp.where(here, keep, 0.0)
    out[0:NCE, :] = pairs
    cnt_a = jnp.zeros((8, LANES), f32)
    for r in range(row_blocks):
        cnt_a += dot(ones, (country == ec[r]).astype(f32).astype(bf16), 1, 1)
    cnt_b = jnp.zeros((8, LANES), f32)
    for c in range(col_local):
        cnt_b += dot(ones, (country == ic[c]).astype(f32).astype(bf16), 1, 1)
    cnt_a = cnt_a[0:1] * (imp_place == 0).astype(f32)
    cnt_b = cnt_b[0:1] * (exp_place == 0).astype(f32)
    out[lay.cnt_at : lay.cnt_at + 1, :] = cnt_a
    out[lay.cnt_at + 1 : lay.cnt_at + 2, :] = cnt_b
    mine = half_of(exp_place, imp_place)
    for k, part in enumerate(outs):
        part[...] = out[pl.ds(pl.multiple_of((mine ^ k) * lay.share, 8), lay.share), :]


def lookup(row, index):
    return jnp.take_along_axis(
        jnp.broadcast_to(row, index.shape), index, axis=1, mode="promise_in_bounds"
    )


def down(row):
    return jnp.transpose(jnp.broadcast_to(row, (LANES, LANES)))


def across(x):
    return jnp.sum(jnp.transpose(x), axis=0, keepdims=True)


def below(x):
    return jnp.sum(x, axis=0, keepdims=True)


def eights(x):
    return functools.reduce(lambda u, v: u + v, [x[j : j + 8] for j in range(0, x.shape[0], 8)])


def inner(u, v):
    partial = eights(u[0] * v[0]) + eights(u[1] * v[1]) + eights(u[2] * v[2])
    return jnp.sum(below(partial), axis=1, keepdims=True)


class Side:
    def __init__(self, n, block, start, middle, end, hot, stage):
        self.n, self.block, self.hot, self.stage = n, block, hot, stage
        self.chunks = n // LANES
        shape = (self.chunks, LANES)
        place = (iota(shape, 0) * LANES + iota(shape, 1)).astype(f32)
        country = jnp.zeros(shape, i32)
        jump = LANES // 2
        while jump:
            passed = lookup(end, country + (jump - 1)) <= place
            country = jnp.where(passed, country + jump, country)
            jump //= 2
        self.country = country
        self.second = place >= lookup(middle, country)
        for j in range(n // block):
            at = (iota((block, LANES), 0) + j * block).astype(f32)
            inside = (at >= start) & (at < end)
            hot[j * block : (j + 1) * block, :] = jnp.where(inside, 1.0, 0.0).astype(bf16)

    def expand(self, first, second):
        return jnp.where(self.second, lookup(second, self.country), lookup(first, self.country))

    def sums(self, vectors):
        chunks, stage = self.chunks, self.stage
        for k, v in enumerate(vectors):
            stage[2 * k * chunks : (2 * k + 1) * chunks, :] = jnp.where(self.second, 0.0, v)
            stage[(2 * k + 1) * chunks : (2 * k + 2) * chunks, :] = jnp.where(self.second, v, 0.0)
        high = -(-2 * len(vectors) // 8) * 8
        for k in range(2 * len(vectors), high):
            stage[k * chunks : (k + 1) * chunks, :] = jnp.zeros((chunks, LANES), f32)
        got = jnp.zeros((3 * high, LANES), f32)
        per = self.block // LANES
        for j in range(chunks // per):
            left = jnp.concatenate(
                [stage[pl.ds(j * per + h, high, stride=chunks), :] for h in range(per)], axis=1
            )
            pieces = jnp.concatenate(split(left), axis=0).astype(bf16)
            got += dot(pieces, self.hot[j * self.block : (j + 1) * self.block, :], 1, 0)
        return got[:high] + got[high : 2 * high] + got[2 * high :]

    def maxima(self, values_ref, low, high):
        low, high = down(low), down(high)

        def body(j, best):
            at = (iota((LANES, LANES), 1) + j * LANES).astype(f32)
            inside = (at >= low) & (at < high)
            return jnp.maximum(best, jnp.where(inside, values_ref[pl.ds(j, 1), :], -jnp.inf))

        best = lax.fori_loop(0, self.chunks, body, jnp.full((LANES, LANES), -jnp.inf, f32))
        best = jnp.max(jnp.transpose(best), axis=0, keepdims=True)
        return jnp.where(best > -jnp.inf, best, 0.0)


def solve_kernel(lay, *refs):
    where = lax.axis_index("exp"), lax.axis_index("imp")
    shares, refs = refs[:2], refs[2:]
    out_a, out_b, out_g, shared, hot_a, hot_b, stage_a, stage_b, val_a, val_b, shift_ref = refs
    mine = half_of(*where)
    for k, part in enumerate(shares):
        shared[pl.ds(pl.multiple_of((mine ^ k) * lay.share, 8), lay.share), :] = part[...]
    flow = (
        shared[lay.rows_at : lay.cols_at, :],
        shared[lay.cols_at : lay.cnt_at, :],
        shared[0:NCE, :],
    )
    side = lay.side
    tally = shared[lay.cnt_at : lay.cnt_at + 8, :]
    before = jnp.where(iota((LANES, LANES), 0) < iota((LANES, LANES), 1), 1.0, 0.0).astype(bf16)
    start = dot(tally.astype(bf16), before, 1, 0)
    end = start + tally
    first = jnp.floor((start + 0.5) * (1.0 / side))
    middle = jnp.minimum(end, (first + 1.0) * side)

    def table(x, y):
        return jnp.concatenate([x[0:1], y[0:1], x[1:2], y[1:2]], axis=0)

    low, high = table(start, middle), table(middle, end)
    count = high - low
    full = count > 0.5
    inv_count = jnp.where(full, 1.0 / jnp.maximum(count, 1.0), 0.0)
    block_of = jnp.where(full, table(first, first + 1.0), -1.0)
    sa = Side(lay.na, side, start[0:1], middle[0:1], end[0:1], hot_a, stage_a)
    sb = Side(lay.nb, side, start[1:2], middle[1:2], end[1:2], hot_b, stage_b)

    wide = lay.blocks_b
    spots = [(r * wide // LANES, r * wide % LANES) for r in range(lay.blocks_a)]
    live = jnp.concatenate(
        [shared[lay.live_at + row : lay.live_at + row + 1, at : at + wide] for row, at in spots], axis=0
    ).astype(bf16)
    number = iota((LANES, LANES), 1).astype(f32)
    pick_a = [jnp.where(down(block_of[p : p + 1]) == number, 1.0, 0.0).astype(bf16) for p in (0, 1)]
    number = iota((LANES, LANES), 0).astype(f32)
    pick_b = [jnp.where(block_of[q : q + 1] == number, 1.0, 0.0).astype(bf16) for q in (2, 3)]
    reach = [dot(pick[:, : lay.blocks_a], live, 1, 0).astype(bf16) for pick in pick_a]
    mask = [[dot(reach[p], pick_b[q][: lay.blocks_b], 1, 0) for q in (0, 1)] for p in (0, 1)]

    a = jnp.zeros((lay.na // LANES, LANES), f32)
    b = jnp.zeros((lay.nb // LANES, LANES), f32)
    g = jnp.zeros((NCE, NCI), f32)
    mean = jnp.zeros((4, LANES), f32)
    for newton in range(NEWTON):
        if newton == 0:
            left = flow
            weight, inv, rate = count, inv_count, mask
            sum_a, sum_b = sa.sums([flow[0]]), sb.sums([flow[1]])
            part_a, part_b = sa.expand(inv[0:1], inv[1:2]), sb.expand(inv[2:3], inv[3:4])
            m2, m3 = inv, inv * inv
            f1 = jnp.concatenate([sum_a[0:2], sum_b[0:2]], axis=0) * inv
            f2 = f1 * inv
        else:
            left = (flow[0] - RIDGE * a, flow[1] - RIDGE * b, flow[2] - RIDGE * g)
            shift_ref[0:4, :] = mean
            off_a = a - sa.expand(mean[0:1], mean[1:2])
            off_b = b - sb.expand(mean[2:3], mean[3:4])
            worst = jnp.maximum(jnp.max(off_a), jnp.max(off_b))
            val_a[...] = a
            val_b[...] = b

            @pl.when(worst > 20.0)
            def _():
                shift_ref[0:1, :] = sa.maxima(val_a, low[0:1], high[0:1])
                shift_ref[1:2, :] = sa.maxima(val_a, low[1:2], high[1:2])
                shift_ref[2:3, :] = sb.maxima(val_b, low[2:3], high[2:3])
                shift_ref[3:4, :] = sb.maxima(val_b, low[3:4], high[3:4])

            shift = shift_ref[0:4, :]
            size_a = jnp.exp(a - sa.expand(shift[0:1], shift[1:2]))
            size_b = jnp.exp(b - sb.expand(shift[2:3], shift[3:4]))

            def moments(s, x, f):
                return s.sums([x, x * x, x * x * x, x * f, x * x * f])

            sum_a, sum_b = moments(sa, size_a, left[0]), moments(sb, size_b, left[1])
            got = [jnp.concatenate([sum_a[2 * k : 2 * k + 2], sum_b[2 * k : 2 * k + 2]], axis=0) for k in range(5)]
            weight = got[0]
            inv = jnp.where(full, 1.0 / jnp.where(full, weight, 1.0), 0.0)
            part_a = size_a * sa.expand(inv[0:1], inv[1:2])
            part_b = size_b * sb.expand(inv[2:3], inv[3:4])
            inv2 = inv * inv
            m2, m3 = got[1] * inv2, got[2] * (inv2 * inv)
            f1, f2 = got[3] * inv, got[4] * inv2
            lift = [g + down(shift[p : p + 1]) for p in (0, 1)]
            rate = [
                [jnp.where(mask[p][q] > 0.5, jnp.exp(lift[p] + shift[2 + q : 3 + q]), 0.0) for q in (0, 1)]
                for p in (0, 1)
            ]
        tall = [down(weight[p : p + 1]) for p in (0, 1)]
        mu = [[rate[p][q] * (tall[p] * weight[2 + q : 3 + q]) for q in (0, 1)] for p in (0, 1)]
        mu_a = [mu[p][0] + mu[p][1] for p in (0, 1)]
        mu_b = [mu[0][q] + mu[1][q] for q in (0, 1)]
        whole = jnp.concatenate([across(mu_a[0]), across(mu_a[1]), below(mu_b[0]), below(mu_b[1])], axis=0)
        da = part_a * sa.expand(whole[0:1], whole[1:2])
        db = part_b * sb.expand(whole[2:3], whole[3:4])
        res = (left[0] - da, left[1] - db, left[2] - (mu_a[0] + mu_a[1]))
        way = res
        norm = inner(res, res)
        v = f1 - whole * m2
        w = f2 - whole * m3
        for sweep in range(CG):
            tall = [down(v[p : p + 1]) for p in (0, 1)]
            flat = [v[2 + q : 3 + q] for q in (0, 1)]
            ga = [mu[p][0] * flat[0] + mu[p][1] * flat[1] + way[2] * mu_a[p] for p in (0, 1)]
            gb = [mu[0][q] * tall[0] + mu[1][q] * tall[1] + way[2] * mu_b[q] for q in (0, 1)]
            u = jnp.concatenate([across(ga[0]), across(ga[1]), below(gb[0]), below(gb[1])], axis=0)
            image = (
                (da + RIDGE) * way[0] + part_a * sa.expand(u[0:1], u[1:2]),
                (db + RIDGE) * way[1] + part_b * sb.expand(u[2:3], u[3:4]),
                RIDGE * way[2] + (ga[0] + ga[1]) + (tall[0] * mu_a[0] + tall[1] * mu_a[1]),
            )
            step = norm / inner(way, image)
            a, b, g = a + step * way[0], b + step * way[1], g + step * way[2]
            if newton + 1 < NEWTON:
                mean = mean + step * v
            if sweep + 1 < CG:
                res = tuple(x - step * y for x, y in zip(res, image))
                fresh = inner(res, res)
                ratio = fresh / norm
                way = tuple(x + ratio * y for x, y in zip(res, way))
                norm = fresh
                v = v - step * (whole * w + RIDGE * v + u * m2) + ratio * v
    out_g[...] = g
    val_a[...] = a
    val_b[...] = b
    for out, val, at in ((out_a, val_a, where[0]), (out_b, val_b, where[1])):
        rows = out.shape[0] // LANES
        for j in range(rows):
            out[j * LANES : (j + 1) * LANES] = val[pl.ds(at * rows + j, 1), :].reshape(LANES)


def powers(first, limit):
    return [1 << k for k in range(16) if first <= 1 << k < limit]


def swap(x, n_exp, n_imp, exp_bits, imp_bits):
    pairs = [
        (e * n_imp + m, (e ^ exp_bits) * n_imp + (m ^ imp_bits)) for e in range(n_exp) for m in range(n_imp)
    ]
    return lax.ppermute(x, ("exp", "imp"), pairs)


def per_device(mesh_shape, flows, routing, tile_block, exp_country, imp_country):
    slots, side = flows.shape[0], flows.shape[1]
    n_exp, n_imp = mesh_shape
    rows, cols = exp_country.shape[0], imp_country.shape[0]
    lay = Layout(rows * n_exp, cols * n_imp, side)
    vmem = pl.BlockSpec(memory_space=pltpu.VMEM)
    inputs = (
        flows,
        routing.reshape(-1),
        tile_block,
        exp_country.reshape(-1, 1, side),
        imp_country.reshape(-1, 1, side),
    )
    homes = [pltpu.VMEM, pltpu.SMEM, pltpu.SMEM, pltpu.VMEM, pltpu.VMEM]
    parts = pl.pallas_call(
        functools.partial(local_kernel, lay, slots),
        out_shape=[jax.ShapeDtypeStruct((lay.share, LANES), f32)] * 2,
        in_specs=[pl.BlockSpec(memory_space=pltpu.HBM)] * 5,
        out_specs=[vmem] * 2,
        scratch_shapes=[pltpu.VMEM((2 * lay.share, LANES), f32)]
        + [space(x.shape, x.dtype) for space, x in zip(homes, inputs)]
        + [pltpu.SemaphoreType.DMA((5,))],
        compiler_params=pltpu.CompilerParams(vmem_limit_bytes=LOCAL_BYTES),
        name="local_sums",
    )(*inputs)
    mine = parts[0] + swap(parts[1], n_exp, n_imp, 1, 0)
    for bit in powers(2, n_exp):
        mine = mine + swap(mine, n_exp, n_imp, bit | 1, 0)
    for bit in powers(1, n_imp):
        mine = mine + swap(mine, n_exp, n_imp, 1, bit)
    shares = (mine, swap(mine, n_exp, n_imp, 1, 0))
    high = 16
    a, b, g = pl.pallas_call(
        functools.partial(solve_kernel, lay),
        out_shape=(
            jax.ShapeDtypeStruct((rows,), f32),
            jax.ShapeDtypeStruct((cols,), f32),
            jax.ShapeDtypeStruct((NCE, NCI), f32),
        ),
        in_specs=[vmem] * 2,
        out_specs=(vmem, vmem, vmem),
        scratch_shapes=[
            pltpu.VMEM((2 * lay.share, LANES), f32),
            pltpu.VMEM((lay.na, LANES), bf16),
            pltpu.VMEM((lay.nb, LANES), bf16),
            pltpu.VMEM((high * lay.na // LANES, LANES), f32),
            pltpu.VMEM((high * lay.nb // LANES, LANES), f32),
            pltpu.VMEM((lay.na // LANES, LANES), f32),
            pltpu.VMEM((lay.nb // LANES, LANES), f32),
            pltpu.VMEM((8, LANES), f32),
        ],
        compiler_params=pltpu.CompilerParams(vmem_limit_bytes=VMEM_BYTES),
        name="solve",
    )(*shares)
    return a, b, g


def solution(mesh):
    placed = (
        P(("exp", "imp"), None, None),
        P(("exp", "imp"), None, None),
        P(("exp", "imp")),
        P("exp"),
        P("imp"),
    )
    return jax.shard_map(
        functools.partial(per_device, (mesh.shape["exp"], mesh.shape["imp"])),
        mesh=mesh,
        in_specs=placed,
        out_specs=(P("exp"), P("imp"), P()),
        check_vma=False,
    )
```

```python
import functools

import jax
import jax.numpy as jnp
from jax import lax
from jax.experimental import pallas as pl
from jax.experimental.pallas import tpu as pltpu
from jax.sharding import PartitionSpec as P

NCE = 128
NCI = 128
NEWTON = 2
CG = 2
LANES = 128
RIDGE = 64.0
VMEM_BYTES = 48 * 1024 * 1024

f32 = jnp.float32
bf16 = jnp.bfloat16
i32 = jnp.int32


def iota(shape, dim):
    return lax.broadcasted_iota(i32, shape, dim)


def split(x):
    hi = x.astype(bf16).astype(f32)
    rest = x - hi
    mid = rest.astype(bf16).astype(f32)
    return hi, mid, rest - mid


def dot(x, y, cx, cy, precision=None):
    return lax.dot_general(
        x, y, (((cx,), (cy,)), ((), ())), precision=precision, preferred_element_type=f32
    )


class Layout:
    def __init__(self, na, nb, side):
        self.na, self.nb, self.side = na, nb, side
        self.rows_at = NCE
        self.cols_at = self.rows_at + na // LANES
        self.cnt_at = self.cols_at + nb // LANES
        self.live_at = self.cnt_at + 2
        self.blocks_a, self.blocks_b = na // side, nb // side
        self.total = -(-(self.live_at - (-self.blocks_a * self.blocks_b // LANES)) // 8) * 8
        self.share = -(-self.total // 16) * 8


def half_of(exp_place, imp_place):
    bits = exp_place ^ (imp_place & 1)
    for shift in (8, 4, 2, 1):
        bits = bits ^ (bits >> shift)
    return bits & 1


def local_kernel(lay, slots, *refs):
    sources, outs, out, homes, sems = refs[:5], refs[5:7], refs[7], refs[8:13], refs[13]
    small = [pltpu.make_async_copy(sources[j], homes[j], sems.at[j]) for j in range(1, 5)]
    tiles = [
        pltpu.make_async_copy(sources[0].at[k], homes[0].at[k], sems.at[5 + k]) for k in range(slots)
    ]
    for copy in small + tiles:
        copy.start()
    flows, routing, tile_block, ec, ic = homes
    exp_place, imp_place = lax.axis_index("exp"), lax.axis_index("imp")
    side = lay.side
    row_blocks = ec.shape[0]
    col_local = ic.shape[0]
    out[...] = jnp.zeros_like(out)
    per = side // LANES
    country = iota((NCE, side), 0)
    ones = jnp.ones((8, side), bf16)
    for copy in small:
        copy.wait()
    cnt_a = jnp.zeros((8, LANES), f32)
    for r in range(row_blocks):
        cnt_a += dot(ones, (country == ec[r]).astype(f32).astype(bf16), 1, 1)
    cnt_b = jnp.zeros((8, LANES), f32)
    for c in range(col_local):
        cnt_b += dot(ones, (country == ic[c]).astype(f32).astype(bf16), 1, 1)
    cnt_a = cnt_a[0:1] * (imp_place == 0).astype(f32)
    cnt_b = cnt_b[0:1] * (exp_place == 0).astype(f32)
    out[lay.cnt_at : lay.cnt_at + 1, :] = cnt_a
    out[lay.cnt_at + 1 : lay.cnt_at + 2, :] = cnt_b
    pairs = jnp.zeros((NCE, NCI), f32)
    for k in range(slots):
        r = tile_block[k] // col_local
        c = tile_block[k] % col_local
        live = routing[0] == k
        for t in range(1, routing.shape[0]):
            live = live | (routing[t] == k)
        keep = live.astype(f32)
        hot_r = (country == ec[r]).astype(f32).astype(bf16)
        hot_c = (country == ic[c]).astype(f32).astype(bf16)
        tiles[k].wait()
        tile = flows[k] * keep.astype(bf16)
        half = dot(hot_r, tile, 1, 0)
        col_sum = jnp.sum(half, axis=0, keepdims=True)
        row_sum = dot(ones, tile, 1, 1)[0:1]
        top = half.astype(bf16)
        rest = (half - top.astype(f32)).astype(bf16)
        both = dot(jnp.concatenate([top, rest], axis=0), hot_c, 1, 1)
        pairs = pairs + (both[:NCE] + both[NCE:])
        row_at = lay.rows_at + (exp_place * row_blocks + r) * per
        col_at = lay.cols_at + (imp_place * col_local + c) * per
        for h in range(per):
            cut = slice(h * LANES, (h + 1) * LANES)
            out[pl.ds(row_at + h, 1), :] += row_sum[:, cut]
            out[pl.ds(col_at + h, 1), :] += col_sum[:, cut]
        flat = (exp_place * row_blocks + r) * lay.blocks_b + imp_place * col_local + c
        here = iota((1, LANES), 1) == flat % LANES
        out[pl.ds(lay.live_at + flat // LANES, 1), :] += jnp.where(here, keep, 0.0)
    out[0:NCE, :] = pairs
    mine = half_of(exp_place, imp_place)
    for k, part in enumerate(outs):
        part[...] = out[pl.ds(pl.multiple_of((mine ^ k) * lay.share, 8), lay.share), :]


def lookup(row, index):
    return jnp.take_along_axis(
        jnp.broadcast_to(row, index.shape), index, axis=1, mode="promise_in_bounds"
    )


def down(row):
    return jnp.transpose(jnp.broadcast_to(row, (LANES, LANES)))


def across(x):
    return jnp.sum(jnp.transpose(x), axis=0, keepdims=True)


def below(x):
    return jnp.sum(x, axis=0, keepdims=True)


def eights(x):
    return functools.reduce(lambda u, v: u + v, [x[j : j + 8] for j in range(0, x.shape[0], 8)])


def inner(u, v):
    partial = eights(u[0] * v[0]) + eights(u[1] * v[1]) + eights(u[2] * v[2])
    return jnp.sum(below(partial), axis=1, keepdims=True)


class Side:
    def __init__(self, n, block, start, middle, end, hot, stage):
        self.n, self.block, self.hot, self.stage = n, block, hot, stage
        self.chunks = n // LANES
        shape = (self.chunks, LANES)
        place = (iota(shape, 0) * LANES + iota(shape, 1)).astype(f32)
        country = jnp.zeros(shape, i32)
        jump = LANES // 2
        while jump:
            passed = lookup(end, country + (jump - 1)) <= place
            country = jnp.where(passed, country + jump, country)
            jump //= 2
        self.country = country
        self.second = place >= lookup(middle, country)
        for j in range(n // block):
            at = (iota((block, LANES), 0) + j * block).astype(f32)
            inside = (at >= start) & (at < end)
            hot[j * block : (j + 1) * block, :] = jnp.where(inside, 1.0, 0.0).astype(bf16)

    def expand(self, first, second):
        return jnp.where(self.second, lookup(second, self.country), lookup(first, self.country))

    def sums(self, vectors):
        chunks, stage = self.chunks, self.stage
        for k, v in enumerate(vectors):
            stage[2 * k * chunks : (2 * k + 1) * chunks, :] = jnp.where(self.second, 0.0, v)
            stage[(2 * k + 1) * chunks : (2 * k + 2) * chunks, :] = jnp.where(self.second, v, 0.0)
        high = -(-2 * len(vectors) // 8) * 8
        for k in range(2 * len(vectors), high):
            stage[k * chunks : (k + 1) * chunks, :] = jnp.zeros((chunks, LANES), f32)
        got = jnp.zeros((3 * high, LANES), f32)
        per = self.block // LANES
        for j in range(chunks // per):
            left = jnp.concatenate(
                [stage[pl.ds(j * per + h, high, stride=chunks), :] for h in range(per)], axis=1
            )
            pieces = jnp.concatenate(split(left), axis=0).astype(bf16)
            got += dot(pieces, self.hot[j * self.block : (j + 1) * self.block, :], 1, 0)
        return got[:high] + got[high : 2 * high] + got[2 * high :]

    def maxima(self, values_ref, low, high):
        low, high = down(low), down(high)

        def body(j, best):
            at = (iota((LANES, LANES), 1) + j * LANES).astype(f32)
            inside = (at >= low) & (at < high)
            return jnp.maximum(best, jnp.where(inside, values_ref[pl.ds(j, 1), :], -jnp.inf))

        best = lax.fori_loop(0, self.chunks, body, jnp.full((LANES, LANES), -jnp.inf, f32))
        best = jnp.max(jnp.transpose(best), axis=0, keepdims=True)
        return jnp.where(best > -jnp.inf, best, 0.0)


def solve_kernel(lay, *refs):
    where = lax.axis_index("exp"), lax.axis_index("imp")
    shares, refs = refs[:2], refs[2:]
    out_a, out_b, out_g, shared, hot_a, hot_b, stage_a, stage_b, val_a, val_b, shift_ref = refs
    mine = half_of(*where)
    for k, part in enumerate(shares):
        shared[pl.ds(pl.multiple_of((mine ^ k) * lay.share, 8), lay.share), :] = part[...]
    flow = (
        shared[lay.rows_at : lay.cols_at, :],
        shared[lay.cols_at : lay.cnt_at, :],
        shared[0:NCE, :],
    )
    side = lay.side
    tally = shared[lay.cnt_at : lay.cnt_at + 8, :]
    before = jnp.where(iota((LANES, LANES), 0) < iota((LANES, LANES), 1), 1.0, 0.0).astype(bf16)
    start = dot(tally.astype(bf16), before, 1, 0)
    end = start + tally
    first = jnp.floor((start + 0.5) * (1.0 / side))
    middle = jnp.minimum(end, (first + 1.0) * side)

    def table(x, y):
        return jnp.concatenate([x[0:1], y[0:1], x[1:2], y[1:2]], axis=0)

    low, high = table(start, middle), table(middle, end)
    count = high - low
    full = count > 0.5
    inv_count = jnp.where(full, 1.0 / jnp.maximum(count, 1.0), 0.0)
    block_of = jnp.where(full, table(first, first + 1.0), -1.0)
    sa = Side(lay.na, side, start[0:1], middle[0:1], end[0:1], hot_a, stage_a)
    sb = Side(lay.nb, side, start[1:2], middle[1:2], end[1:2], hot_b, stage_b)

    wide = lay.blocks_b
    spots = [(r * wide // LANES, r * wide % LANES) for r in range(lay.blocks_a)]
    live = jnp.concatenate(
        [shared[lay.live_at + row : lay.live_at + row + 1, at : at + wide] for row, at in spots], axis=0
    ).astype(bf16)
    number = iota((LANES, LANES), 1).astype(f32)
    pick_a = [jnp.where(down(block_of[p : p + 1]) == number, 1.0, 0.0).astype(bf16) for p in (0, 1)]
    number = iota((LANES, LANES), 0).astype(f32)
    pick_b = [jnp.where(block_of[q : q + 1] == number, 1.0, 0.0).astype(bf16) for q in (2, 3)]
    reach = [dot(pick[:, : lay.blocks_a], live, 1, 0).astype(bf16) for pick in pick_a]
    mask = [[dot(reach[p], pick_b[q][: lay.blocks_b], 1, 0) for q in (0, 1)] for p in (0, 1)]

    a = jnp.zeros((lay.na // LANES, LANES), f32)
    b = jnp.zeros((lay.nb // LANES, LANES), f32)
    g = jnp.zeros((NCE, NCI), f32)
    mean = jnp.zeros((4, LANES), f32)
    for newton in range(NEWTON):
        if newton == 0:
            left = flow
            weight, inv, rate = count, inv_count, mask
            sum_a, sum_b = sa.sums([flow[0]]), sb.sums([flow[1]])
            part_a, part_b = sa.expand(inv[0:1], inv[1:2]), sb.expand(inv[2:3], inv[3:4])
            m2, m3 = inv, inv * inv
            f1 = jnp.concatenate([sum_a[0:2], sum_b[0:2]], axis=0) * inv
            f2 = f1 * inv
        else:
            left = (flow[0] - RIDGE * a, flow[1] - RIDGE * b, flow[2] - RIDGE * g)
            shift_ref[0:4, :] = mean
            off_a = a - sa.expand(mean[0:1], mean[1:2])
            off_b = b - sb.expand(mean[2:3], mean[3:4])
            worst = jnp.maximum(jnp.max(off_a), jnp.max(off_b))
            val_a[...] = a
            val_b[...] = b

            @pl.when(worst > 20.0)
            def _():
                shift_ref[0:1, :] = sa.maxima(val_a, low[0:1], high[0:1])
                shift_ref[1:2, :] = sa.maxima(val_a, low[1:2], high[1:2])
                shift_ref[2:3, :] = sb.maxima(val_b, low[2:3], high[2:3])
                shift_ref[3:4, :] = sb.maxima(val_b, low[3:4], high[3:4])

            shift = shift_ref[0:4, :]
            size_a = jnp.exp(a - sa.expand(shift[0:1], shift[1:2]))
            size_b = jnp.exp(b - sb.expand(shift[2:3], shift[3:4]))

            def moments(s, x, f):
                return s.sums([x, x * x, x * x * x, x * f, x * x * f])

            sum_a, sum_b = moments(sa, size_a, left[0]), moments(sb, size_b, left[1])
            got = [jnp.concatenate([sum_a[2 * k : 2 * k + 2], sum_b[2 * k : 2 * k + 2]], axis=0) for k in range(5)]
            weight = got[0]
            inv = jnp.where(full, 1.0 / jnp.where(full, weight, 1.0), 0.0)
            part_a = size_a * sa.expand(inv[0:1], inv[1:2])
            part_b = size_b * sb.expand(inv[2:3], inv[3:4])
            inv2 = inv * inv
            m2, m3 = got[1] * inv2, got[2] * (inv2 * inv)
            f1, f2 = got[3] * inv, got[4] * inv2
            lift = [g + down(shift[p : p + 1]) for p in (0, 1)]
            rate = [
                [jnp.where(mask[p][q] > 0.5, jnp.exp(lift[p] + shift[2 + q : 3 + q]), 0.0) for q in (0, 1)]
                for p in (0, 1)
            ]
        tall = [down(weight[p : p + 1]) for p in (0, 1)]
        mu = [[rate[p][q] * (tall[p] * weight[2 + q : 3 + q]) for q in (0, 1)] for p in (0, 1)]
        mu_a = [mu[p][0] + mu[p][1] for p in (0, 1)]
        mu_b = [mu[0][q] + mu[1][q] for q in (0, 1)]
        whole = jnp.concatenate([across(mu_a[0]), across(mu_a[1]), below(mu_b[0]), below(mu_b[1])], axis=0)
        da = part_a * sa.expand(whole[0:1], whole[1:2])
        db = part_b * sb.expand(whole[2:3], whole[3:4])
        res = (left[0] - da, left[1] - db, left[2] - (mu_a[0] + mu_a[1]))
        way = res
        norm = inner(res, res)
        v = f1 - whole * m2
        w = f2 - whole * m3
        for sweep in range(CG):
            tall = [down(v[p : p + 1]) for p in (0, 1)]
            flat = [v[2 + q : 3 + q] for q in (0, 1)]
            ga = [mu[p][0] * flat[0] + mu[p][1] * flat[1] + way[2] * mu_a[p] for p in (0, 1)]
            gb = [mu[0][q] * tall[0] + mu[1][q] * tall[1] + way[2] * mu_b[q] for q in (0, 1)]
            u = jnp.concatenate([across(ga[0]), across(ga[1]), below(gb[0]), below(gb[1])], axis=0)
            image = (
                (da + RIDGE) * way[0] + part_a * sa.expand(u[0:1], u[1:2]),
                (db + RIDGE) * way[1] + part_b * sb.expand(u[2:3], u[3:4]),
                RIDGE * way[2] + (ga[0] + ga[1]) + (tall[0] * mu_a[0] + tall[1] * mu_a[1]),
            )
            step = norm / inner(way, image)
            a, b, g = a + step * way[0], b + step * way[1], g + step * way[2]
            if newton + 1 < NEWTON:
                mean = mean + step * v
            if sweep + 1 < CG:
                res = tuple(x - step * y for x, y in zip(res, image))
                fresh = inner(res, res)
                ratio = fresh / norm
                way = tuple(x + ratio * y for x, y in zip(res, way))
                norm = fresh
                v = v - step * (whole * w + RIDGE * v + u * m2) + ratio * v
    out_g[...] = g
    val_a[...] = a
    val_b[...] = b
    for out, val, at in ((out_a, val_a, where[0]), (out_b, val_b, where[1])):
        rows = out.shape[0] // LANES
        for j in range(rows):
            out[j * LANES : (j + 1) * LANES] = val[pl.ds(at * rows + j, 1), :].reshape(LANES)


def powers(first, limit):
    return [1 << k for k in range(16) if first <= 1 << k < limit]


def swap(x, n_exp, n_imp, exp_bits, imp_bits):
    pairs = [
        (e * n_imp + m, (e ^ exp_bits) * n_imp + (m ^ imp_bits)) for e in range(n_exp) for m in range(n_imp)
    ]
    return lax.ppermute(x, ("exp", "imp"), pairs)


def per_device(mesh_shape, flows, routing, tile_block, exp_country, imp_country):
    slots, side = flows.shape[0], flows.shape[1]
    n_exp, n_imp = mesh_shape
    rows, cols = exp_country.shape[0], imp_country.shape[0]
    lay = Layout(rows * n_exp, cols * n_imp, side)
    vmem = pl.BlockSpec(memory_space=pltpu.VMEM)
    inputs = (
        flows,
        routing.reshape(-1),
        tile_block,
        exp_country.reshape(-1, 1, side),
        imp_country.reshape(-1, 1, side),
    )
    inputs = tuple(pltpu.with_memory_space_constraint(x, pltpu.HBM) for x in inputs)
    homes = [pltpu.VMEM, pltpu.SMEM, pltpu.SMEM, pltpu.VMEM, pltpu.VMEM]
    parts = pl.pallas_call(
        functools.partial(local_kernel, lay, slots),
        out_shape=[jax.ShapeDtypeStruct((lay.share, LANES), f32)] * 2,
        in_specs=[pl.BlockSpec(memory_space=pltpu.HBM)] * 5,
        out_specs=[vmem] * 2,
        scratch_shapes=[pltpu.VMEM((2 * lay.share, LANES), f32)]
        + [space(x.shape, x.dtype) for space, x in zip(homes, inputs)]
        + [pltpu.SemaphoreType.DMA((5 + slots,))],
        compiler_params=pltpu.CompilerParams(vmem_limit_bytes=VMEM_BYTES),
        name="local_sums",
    )(*inputs)
    mine = parts[0] + swap(parts[1], n_exp, n_imp, 1, 0)
    for bit in powers(2, n_exp):
        mine = mine + swap(mine, n_exp, n_imp, bit | 1, 0)
    for bit in powers(1, n_imp):
        mine = mine + swap(mine, n_exp, n_imp, 1, 2 * bit - 1)
    shares = (mine, swap(mine, n_exp, n_imp, 1, 0))
    high = 16
    a, b, g = pl.pallas_call(
        functools.partial(solve_kernel, lay),
        out_shape=(
            jax.ShapeDtypeStruct((rows,), f32),
            jax.ShapeDtypeStruct((cols,), f32),
            jax.ShapeDtypeStruct((NCE, NCI), f32),
        ),
        in_specs=[vmem] * 2,
        out_specs=(vmem, vmem, vmem),
        scratch_shapes=[
            pltpu.VMEM((2 * lay.share, LANES), f32),
            pltpu.VMEM((lay.na, LANES), bf16),
            pltpu.VMEM((lay.nb, LANES), bf16),
            pltpu.VMEM((high * lay.na // LANES, LANES), f32),
            pltpu.VMEM((high * lay.nb // LANES, LANES), f32),
            pltpu.VMEM((lay.na // LANES, LANES), f32),
            pltpu.VMEM((lay.nb // LANES, LANES), f32),
            pltpu.VMEM((8, LANES), f32),
        ],
        compiler_params=pltpu.CompilerParams(vmem_limit_bytes=VMEM_BYTES),
        name="solve",
    )(*shares)
    return a, b, g


def solution(mesh):
    placed = (
        P(("exp", "imp"), None, None),
        P(("exp", "imp"), None, None),
        P(("exp", "imp")),
        P("exp"),
        P("imp"),
    )
    return jax.shard_map(
        functools.partial(per_device, (mesh.shape["exp"], mesh.shape["imp"])),
        mesh=mesh,
        in_specs=placed,
        out_specs=(P("exp"), P("imp"), P()),
        check_vma=False,
    )
```

```python
import functools

import jax
import jax.numpy as jnp
from jax import lax
from jax.experimental import pallas as pl
from jax.experimental.pallas import tpu as pltpu
from jax.sharding import PartitionSpec as P

NCE = 128
NCI = 128
NEWTON = 2
CG = 2
LANES = 128
RIDGE = 64.0
VMEM_BYTES = 32 * 1024 * 1024

f32 = jnp.float32
bf16 = jnp.bfloat16
i32 = jnp.int32


def iota(shape, dim):
    return lax.broadcasted_iota(i32, shape, dim)


def split(x):
    hi = x.astype(bf16).astype(f32)
    rest = x - hi
    mid = rest.astype(bf16).astype(f32)
    return hi, mid, rest - mid


def dot(x, y, cx, cy, precision=None):
    return lax.dot_general(
        x, y, (((cx,), (cy,)), ((), ())), precision=precision, preferred_element_type=f32
    )


class Layout:
    def __init__(self, na, nb, side):
        self.na, self.nb, self.side = na, nb, side
        self.blocks_a, self.blocks_b = na // side, nb // side
        self.cnt_at = 0
        self.live_at = 2
        self.pairs_at = -(-(2 - (-self.blocks_a * self.blocks_b // LANES)) // 8) * 8
        self.rows_at = self.pairs_at + NCE
        self.cols_at = self.rows_at + na // LANES
        self.total = self.cols_at + nb // LANES
        quarter = -(-self.total // 32) * 8
        self.shares = (quarter, -(-(self.total - 2 * quarter) // 16) * 8)
        self.starts = (0, 2 * quarter)
        self.padded = 2 * sum(self.shares)


def half_of(exp_place, imp_place):
    bits = exp_place ^ (imp_place & 1)
    for shift in (8, 4, 2, 1):
        bits = bits ^ (bits >> shift)
    return bits & 1


def local_kernel(lay, slots, *refs):
    sources, outs, out, homes, sems = refs[:5], refs[5:9], refs[9], refs[10:15], refs[15]
    small = [pltpu.make_async_copy(sources[j], homes[j], sems.at[j]) for j in range(1, 5)]
    tiles = [
        pltpu.make_async_copy(sources[0].at[k], homes[0].at[k], sems.at[5 + k]) for k in range(slots)
    ]
    for copy in small + tiles:
        copy.start()
    flows, routing, tile_block, ec, ic = homes
    exp_place, imp_place = lax.axis_index("exp"), lax.axis_index("imp")
    side = lay.side
    row_blocks = ec.shape[0]
    col_local = ic.shape[0]
    out[...] = jnp.zeros_like(out)
    per = side // LANES
    country = iota((NCE, side), 0)
    ones = jnp.ones((8, side), bf16)
    for copy in small:
        copy.wait()
    cnt_a = jnp.zeros((8, LANES), f32)
    for r in range(row_blocks):
        cnt_a += dot(ones, (country == ec[r]).astype(f32).astype(bf16), 1, 1)
    cnt_b = jnp.zeros((8, LANES), f32)
    for c in range(col_local):
        cnt_b += dot(ones, (country == ic[c]).astype(f32).astype(bf16), 1, 1)
    cnt_a = cnt_a[0:1] * (imp_place == 0).astype(f32)
    cnt_b = cnt_b[0:1] * (exp_place == 0).astype(f32)
    out[lay.cnt_at : lay.cnt_at + 1, :] = cnt_a
    out[lay.cnt_at + 1 : lay.cnt_at + 2, :] = cnt_b
    pairs = jnp.zeros((NCE, NCI), f32)
    for k in range(slots):
        r = tile_block[k] // col_local
        c = tile_block[k] % col_local
        live = routing[0] == k
        for t in range(1, routing.shape[0]):
            live = live | (routing[t] == k)
        keep = live.astype(f32)
        hot_r = (country == ec[r]).astype(f32).astype(bf16)
        hot_c = (country == ic[c]).astype(f32).astype(bf16)
        tiles[k].wait()
        tile = flows[k] * keep.astype(bf16)
        half = dot(hot_r, tile, 1, 0)
        col_sum = jnp.sum(half, axis=0, keepdims=True)
        row_sum = dot(ones, tile, 1, 1)[0:1]
        top = half.astype(bf16)
        rest = (half - top.astype(f32)).astype(bf16)
        both = dot(jnp.concatenate([top, rest], axis=0), hot_c, 1, 1)
        pairs = pairs + (both[:NCE] + both[NCE:])
        row_at = lay.rows_at + (exp_place * row_blocks + r) * per
        col_at = lay.cols_at + (imp_place * col_local + c) * per
        for h in range(per):
            cut = slice(h * LANES, (h + 1) * LANES)
            out[pl.ds(row_at + h, 1), :] += row_sum[:, cut]
            out[pl.ds(col_at + h, 1), :] += col_sum[:, cut]
        flat = (exp_place * row_blocks + r) * lay.blocks_b + imp_place * col_local + c
        here = iota((1, LANES), 1) == flat % LANES
        out[pl.ds(lay.live_at + flat // LANES, 1), :] += jnp.where(here, keep, 0.0)
    out[lay.pairs_at : lay.pairs_at + NCE, :] = pairs
    mine = half_of(exp_place, imp_place)
    for k, part in enumerate(outs):
        start, share = lay.starts[k // 2], lay.shares[k // 2]
        part[...] = out[pl.ds(pl.multiple_of(start + (mine ^ (k % 2)) * share, 8), share), :]


def put_back(lay, chunk, mine, halves, whole):
    for k, part in enumerate(halves):
        share = lay.shares[chunk]
        whole[pl.ds(pl.multiple_of((mine ^ k) * share, 8), share), :] = part[...]


def lookup(row, index):
    return jnp.take_along_axis(
        jnp.broadcast_to(row, index.shape), index, axis=1, mode="promise_in_bounds"
    )


def down(row):
    return jnp.transpose(jnp.broadcast_to(row, (LANES, LANES)))


def across(x):
    return jnp.sum(jnp.transpose(x), axis=0, keepdims=True)


def below(x):
    return jnp.sum(x, axis=0, keepdims=True)


def eights(x):
    return functools.reduce(lambda u, v: u + v, [x[j : j + 8] for j in range(0, x.shape[0], 8)])


def inner(u, v):
    partial = eights(u[0] * v[0]) + eights(u[1] * v[1]) + eights(u[2] * v[2])
    return jnp.sum(below(partial), axis=1, keepdims=True)


def positions(n, block, start, middle, end, hot, country_ref, second_ref):
    shape = (n // LANES, LANES)
    place = (iota(shape, 0) * LANES + iota(shape, 1)).astype(f32)
    country = jnp.zeros(shape, i32)
    jump = LANES // 2
    while jump:
        passed = lookup(end, country + (jump - 1)) <= place
        country = jnp.where(passed, country + jump, country)
        jump //= 2
    country_ref[...] = country
    second_ref[...] = jnp.where(place >= lookup(middle, country), 1.0, 0.0)
    for j in range(n // block):
        at = (iota((block, LANES), 0) + j * block).astype(f32)
        inside = (at >= start) & (at < end)
        hot[j * block : (j + 1) * block, :] = jnp.where(inside, 1.0, 0.0).astype(bf16)


class Side:
    def __init__(self, n, block, country, second, hot, stage):
        self.n, self.block, self.hot, self.stage = n, block, hot, stage
        self.chunks = n // LANES
        self.country = country[...]
        self.second = second[...] > 0.5

    def expand(self, first, second):
        return jnp.where(self.second, lookup(second, self.country), lookup(first, self.country))

    def sums(self, vectors):
        chunks, stage = self.chunks, self.stage
        for k, v in enumerate(vectors):
            stage[2 * k * chunks : (2 * k + 1) * chunks, :] = jnp.where(self.second, 0.0, v)
            stage[(2 * k + 1) * chunks : (2 * k + 2) * chunks, :] = jnp.where(self.second, v, 0.0)
        high = -(-2 * len(vectors) // 8) * 8
        for k in range(2 * len(vectors), high):
            stage[k * chunks : (k + 1) * chunks, :] = jnp.zeros((chunks, LANES), f32)
        got = jnp.zeros((3 * high, LANES), f32)
        per = self.block // LANES
        for j in range(chunks // per):
            left = jnp.concatenate(
                [stage[pl.ds(j * per + h, high, stride=chunks), :] for h in range(per)], axis=1
            )
            pieces = jnp.concatenate(split(left), axis=0).astype(bf16)
            got += dot(pieces, self.hot[j * self.block : (j + 1) * self.block, :], 1, 0)
        return got[:high] + got[high : 2 * high] + got[2 * high :]

    def maxima(self, values_ref, low, high):
        low, high = down(low), down(high)

        def body(j, best):
            at = (iota((LANES, LANES), 1) + j * LANES).astype(f32)
            inside = (at >= low) & (at < high)
            return jnp.maximum(best, jnp.where(inside, values_ref[pl.ds(j, 1), :], -jnp.inf))

        best = lax.fori_loop(0, self.chunks, body, jnp.full((LANES, LANES), -jnp.inf, f32))
        best = jnp.max(jnp.transpose(best), axis=0, keepdims=True)
        return jnp.where(best > -jnp.inf, best, 0.0)


def prepare_kernel(lay, *refs):
    halves, refs = refs[:2], refs[2:]
    tables, mask, hot_a, hot_b, country_a, country_b, second_a, second_b, shared = refs
    put_back(lay, 0, half_of(lax.axis_index("exp"), lax.axis_index("imp")), halves, shared)
    side = lay.side
    tally = shared[lay.cnt_at : lay.cnt_at + 8, :]
    before = jnp.where(iota((LANES, LANES), 0) < iota((LANES, LANES), 1), 1.0, 0.0).astype(bf16)
    start = dot(tally.astype(bf16), before, 1, 0)
    end = start + tally
    first = jnp.floor((start + 0.5) * (1.0 / side))
    middle = jnp.minimum(end, (first + 1.0) * side)

    def table(x, y):
        return jnp.concatenate([x[0:1], y[0:1], x[1:2], y[1:2]], axis=0)

    low, high = table(start, middle), table(middle, end)
    full = high - low > 0.5
    tables[0:4, :] = low
    tables[4:8, :] = high
    block_of = jnp.where(full, table(first, first + 1.0), -1.0)
    positions(lay.na, side, start[0:1], middle[0:1], end[0:1], hot_a, country_a, second_a)
    positions(lay.nb, side, start[1:2], middle[1:2], end[1:2], hot_b, country_b, second_b)

    wide = lay.blocks_b
    spots = [(r * wide // LANES, r * wide % LANES) for r in range(lay.blocks_a)]
    live = jnp.concatenate(
        [shared[lay.live_at + row : lay.live_at + row + 1, at : at + wide] for row, at in spots], axis=0
    ).astype(bf16)
    number = iota((LANES, LANES), 1).astype(f32)
    pick_a = [jnp.where(down(block_of[p : p + 1]) == number, 1.0, 0.0).astype(bf16) for p in (0, 1)]
    number = iota((LANES, LANES), 0).astype(f32)
    pick_b = [jnp.where(block_of[q : q + 1] == number, 1.0, 0.0).astype(bf16) for q in (2, 3)]
    reach = [dot(pick[:, : lay.blocks_a], live, 1, 0).astype(bf16) for pick in pick_a]
    for p in (0, 1):
        for q in (0, 1):
            mask[2 * p + q] = dot(reach[p], pick_b[q][: lay.blocks_b], 1, 0)


def solve_kernel(lay, *refs):
    where = lax.axis_index("exp"), lax.axis_index("imp")
    halves, refs = refs[:4], refs[4:]
    tables, mask_ref, hot_a, hot_b, country_a, country_b, second_a, second_b = refs[:8]
    out_a, out_b, out_g, shared, stage_a, stage_b, val_a, val_b, shift_ref = refs[8:]
    mine = half_of(*where)
    for chunk, start in enumerate(lay.starts):
        room = shared.at[start : start + 2 * lay.shares[chunk]]
        put_back(lay, chunk, mine, halves[2 * chunk : 2 * chunk + 2], room)
    flow = (
        shared[lay.rows_at : lay.cols_at, :],
        shared[lay.cols_at : lay.total, :],
        shared[lay.pairs_at : lay.pairs_at + NCE, :],
    )
    side = lay.side
    low, high = tables[0:4, :], tables[4:8, :]
    count = high - low
    full = count > 0.5
    inv_count = jnp.where(full, 1.0 / jnp.maximum(count, 1.0), 0.0)
    sa = Side(lay.na, side, country_a, second_a, hot_a, stage_a)
    sb = Side(lay.nb, side, country_b, second_b, hot_b, stage_b)
    mask = [[mask_ref[2 * p + q] for q in (0, 1)] for p in (0, 1)]

    a = jnp.zeros((lay.na // LANES, LANES), f32)
    b = jnp.zeros((lay.nb // LANES, LANES), f32)
    g = jnp.zeros((NCE, NCI), f32)
    mean = jnp.zeros((4, LANES), f32)
    for newton in range(NEWTON):
        if newton == 0:
            left = flow
            weight, inv, rate = count, inv_count, mask
            sum_a, sum_b = sa.sums([flow[0]]), sb.sums([flow[1]])
            part_a, part_b = sa.expand(inv[0:1], inv[1:2]), sb.expand(inv[2:3], inv[3:4])
            m2, m3 = inv, inv * inv
            f1 = jnp.concatenate([sum_a[0:2], sum_b[0:2]], axis=0) * inv
            f2 = f1 * inv
        else:
            left = (flow[0] - RIDGE * a, flow[1] - RIDGE * b, flow[2] - RIDGE * g)
            shift_ref[0:4, :] = mean
            off_a = a - sa.expand(mean[0:1], mean[1:2])
            off_b = b - sb.expand(mean[2:3], mean[3:4])
            worst = jnp.maximum(jnp.max(off_a), jnp.max(off_b))
            val_a[...] = a
            val_b[...] = b

            @pl.when(worst > 20.0)
            def _():
                shift_ref[0:1, :] = sa.maxima(val_a, low[0:1], high[0:1])
                shift_ref[1:2, :] = sa.maxima(val_a, low[1:2], high[1:2])
                shift_ref[2:3, :] = sb.maxima(val_b, low[2:3], high[2:3])
                shift_ref[3:4, :] = sb.maxima(val_b, low[3:4], high[3:4])

            shift = shift_ref[0:4, :]
            size_a = jnp.exp(a - sa.expand(shift[0:1], shift[1:2]))
            size_b = jnp.exp(b - sb.expand(shift[2:3], shift[3:4]))

            def moments(s, x, f):
                return s.sums([x, x * x, x * x * x, x * f, x * x * f])

            sum_a, sum_b = moments(sa, size_a, left[0]), moments(sb, size_b, left[1])
            got = [jnp.concatenate([sum_a[2 * k : 2 * k + 2], sum_b[2 * k : 2 * k + 2]], axis=0) for k in range(5)]
            weight = got[0]
            inv = jnp.where(full, 1.0 / jnp.where(full, weight, 1.0), 0.0)
            part_a = size_a * sa.expand(inv[0:1], inv[1:2])
            part_b = size_b * sb.expand(inv[2:3], inv[3:4])
            inv2 = inv * inv
            m2, m3 = got[1] * inv2, got[2] * (inv2 * inv)
            f1, f2 = got[3] * inv, got[4] * inv2
            lift = [g + down(shift[p : p + 1]) for p in (0, 1)]
            rate = [
                [jnp.where(mask[p][q] > 0.5, jnp.exp(lift[p] + shift[2 + q : 3 + q]), 0.0) for q in (0, 1)]
                for p in (0, 1)
            ]
        tall = [down(weight[p : p + 1]) for p in (0, 1)]
        mu = [[rate[p][q] * (tall[p] * weight[2 + q : 3 + q]) for q in (0, 1)] for p in (0, 1)]
        mu_a = [mu[p][0] + mu[p][1] for p in (0, 1)]
        mu_b = [mu[0][q] + mu[1][q] for q in (0, 1)]
        whole = jnp.concatenate([across(mu_a[0]), across(mu_a[1]), below(mu_b[0]), below(mu_b[1])], axis=0)
        da = part_a * sa.expand(whole[0:1], whole[1:2])
        db = part_b * sb.expand(whole[2:3], whole[3:4])
        res = (left[0] - da, left[1] - db, left[2] - (mu_a[0] + mu_a[1]))
        way = res
        norm = inner(res, res)
        v = f1 - whole * m2
        w = f2 - whole * m3
        for sweep in range(CG):
            tall = [down(v[p : p + 1]) for p in (0, 1)]
            flat = [v[2 + q : 3 + q] for q in (0, 1)]
            ga = [mu[p][0] * flat[0] + mu[p][1] * flat[1] + way[2] * mu_a[p] for p in (0, 1)]
            gb = [mu[0][q] * tall[0] + mu[1][q] * tall[1] + way[2] * mu_b[q] for q in (0, 1)]
            u = jnp.concatenate([across(ga[0]), across(ga[1]), below(gb[0]), below(gb[1])], axis=0)
            image = (
                (da + RIDGE) * way[0] + part_a * sa.expand(u[0:1], u[1:2]),
                (db + RIDGE) * way[1] + part_b * sb.expand(u[2:3], u[3:4]),
                RIDGE * way[2] + (ga[0] + ga[1]) + (tall[0] * mu_a[0] + tall[1] * mu_a[1]),
            )
            step = norm / inner(way, image)
            a, b, g = a + step * way[0], b + step * way[1], g + step * way[2]
            if newton + 1 < NEWTON:
                mean = mean + step * v
            if sweep + 1 < CG:
                res = tuple(x - step * y for x, y in zip(res, image))
                fresh = inner(res, res)
                ratio = fresh / norm
                way = tuple(x + ratio * y for x, y in zip(res, way))
                norm = fresh
                v = v - step * (whole * w + RIDGE * v + u * m2) + ratio * v
    out_g[...] = g
    val_a[...] = a
    val_b[...] = b
    for out, val, at in ((out_a, val_a, where[0]), (out_b, val_b, where[1])):
        rows = out.shape[0] // LANES
        for j in range(rows):
            out[j * LANES : (j + 1) * LANES] = val[pl.ds(at * rows + j, 1), :].reshape(LANES)


def powers(first, limit):
    return [1 << k for k in range(16) if first <= 1 << k < limit]


def swap(x, n_exp, n_imp, exp_bits, imp_bits):
    pairs = [
        (e * n_imp + m, (e ^ exp_bits) * n_imp + (m ^ imp_bits)) for e in range(n_exp) for m in range(n_imp)
    ]
    return lax.ppermute(x, ("exp", "imp"), pairs)


def per_device(mesh_shape, flows, routing, tile_block, exp_country, imp_country):
    slots, side = flows.shape[0], flows.shape[1]
    n_exp, n_imp = mesh_shape
    rows, cols = exp_country.shape[0], imp_country.shape[0]
    lay = Layout(rows * n_exp, cols * n_imp, side)
    vmem = pl.BlockSpec(memory_space=pltpu.VMEM)
    inputs = (
        flows,
        routing.reshape(-1),
        tile_block,
        exp_country.reshape(-1, 1, side),
        imp_country.reshape(-1, 1, side),
    )
    inputs = tuple(pltpu.with_memory_space_constraint(x, pltpu.HBM) for x in inputs)
    homes = [pltpu.VMEM, pltpu.SMEM, pltpu.SMEM, pltpu.VMEM, pltpu.VMEM]
    parts = pl.pallas_call(
        functools.partial(local_kernel, lay, slots),
        out_shape=[jax.ShapeDtypeStruct((share, LANES), f32) for share in lay.shares for _ in (0, 1)],
        in_specs=[pl.BlockSpec(memory_space=pltpu.HBM)] * 5,
        out_specs=[vmem] * 4,
        scratch_shapes=[pltpu.VMEM((lay.padded, LANES), f32)]
        + [space(x.shape, x.dtype) for space, x in zip(homes, inputs)]
        + [pltpu.SemaphoreType.DMA((5 + slots,))],
        compiler_params=pltpu.CompilerParams(vmem_limit_bytes=VMEM_BYTES),
        name="local_sums",
    )(*inputs)
    halves = []
    for mine, other in (parts[:2], parts[2:]):
        mine = mine + swap(other, n_exp, n_imp, 1, 0)
        for bit in powers(2, n_exp):
            mine = mine + swap(mine, n_exp, n_imp, bit | 1, 0)
        for bit in powers(1, n_imp):
            mine = mine + swap(mine, n_exp, n_imp, 1, 2 * bit - 1)
        halves += [mine, swap(mine, n_exp, n_imp, 1, 0)]
    shape_a, shape_b = (lay.na // LANES, LANES), (lay.nb // LANES, LANES)
    ready = pl.pallas_call(
        functools.partial(prepare_kernel, lay),
        out_shape=(
            jax.ShapeDtypeStruct((8, LANES), f32),
            jax.ShapeDtypeStruct((4, NCE, NCI), f32),
            jax.ShapeDtypeStruct((lay.na, LANES), bf16),
            jax.ShapeDtypeStruct((lay.nb, LANES), bf16),
            jax.ShapeDtypeStruct(shape_a, i32),
            jax.ShapeDtypeStruct(shape_b, i32),
            jax.ShapeDtypeStruct(shape_a, f32),
            jax.ShapeDtypeStruct(shape_b, f32),
        ),
        in_specs=[vmem] * 2,
        out_specs=(vmem,) * 8,
        scratch_shapes=[pltpu.VMEM((2 * lay.shares[0], LANES), f32)],
        compiler_params=pltpu.CompilerParams(vmem_limit_bytes=VMEM_BYTES),
        cost_estimate=pl.CostEstimate(flops=10**9, bytes_accessed=4 * 10**6, transcendentals=0),
        name="prepare",
    )(*halves[:2])
    most = 16
    a, b, g = pl.pallas_call(
        functools.partial(solve_kernel, lay),
        out_shape=(
            jax.ShapeDtypeStruct((rows,), f32),
            jax.ShapeDtypeStruct((cols,), f32),
            jax.ShapeDtypeStruct((NCE, NCI), f32),
        ),
        in_specs=[vmem] * 12,
        out_specs=(vmem, vmem, vmem),
        scratch_shapes=[
            pltpu.VMEM((lay.padded, LANES), f32),
            pltpu.VMEM((most * lay.na // LANES, LANES), f32),
            pltpu.VMEM((most * lay.nb // LANES, LANES), f32),
            pltpu.VMEM(shape_a, f32),
            pltpu.VMEM(shape_b, f32),
            pltpu.VMEM((8, LANES), f32),
        ],
        compiler_params=pltpu.CompilerParams(vmem_limit_bytes=VMEM_BYTES),
        name="solve",
    )(*halves, *ready)
    return a, b, g


def solution(mesh):
    placed = (
        P(("exp", "imp"), None, None),
        P(("exp", "imp"), None, None),
        P(("exp", "imp")),
        P("exp"),
        P("imp"),
    )
    return jax.shard_map(
        functools.partial(per_device, (mesh.shape["exp"], mesh.shape["imp"])),
        mesh=mesh,
        in_specs=placed,
        out_specs=(P("exp"), P("imp"), P()),
        check_vma=False,
    )
```

```python
import functools

import jax
import jax.numpy as jnp
from jax import lax
from jax.experimental import pallas as pl
from jax.experimental.pallas import tpu as pltpu
from jax.sharding import PartitionSpec as P

NCE = 128
NCI = 128
NEWTON = 2
CG = 2
LANES = 128
RIDGE = 64.0
VMEM_BYTES = 32 * 1024 * 1024

f32 = jnp.float32
bf16 = jnp.bfloat16
i32 = jnp.int32


def iota(shape, dim):
    return lax.broadcasted_iota(i32, shape, dim)


def split(x):
    hi = x.astype(bf16).astype(f32)
    rest = x - hi
    mid = rest.astype(bf16).astype(f32)
    return hi, mid, rest - mid


def dot(x, y, cx, cy, precision=None):
    return lax.dot_general(
        x, y, (((cx,), (cy,)), ((), ())), precision=precision, preferred_element_type=f32
    )


class Layout:
    def __init__(self, na, nb, side):
        self.na, self.nb, self.side = na, nb, side
        self.blocks_a, self.blocks_b = na // side, nb // side
        self.cnt_at = 0
        self.live_at = 2
        self.pairs_at = -(-(2 - (-self.blocks_a * self.blocks_b // LANES)) // 8) * 8
        self.rows_at = self.pairs_at + NCE
        self.cols_at = self.rows_at + na // LANES
        self.total = self.cols_at + nb // LANES
        first = -(-self.total // 40) * 8
        self.shares = (first, -(-(self.total - 2 * first) // 16) * 8)
        self.starts = (0, 2 * first)
        self.padded = 2 * sum(self.shares)


def half_of(exp_place, imp_place):
    bits = exp_place ^ (imp_place & 1)
    for shift in (8, 4, 2, 1):
        bits = bits ^ (bits >> shift)
    return bits & 1


def local_kernel(lay, slots, *refs):
    sources, outs, out, homes, sems = refs[:5], refs[5:8], refs[8], refs[9:14], refs[14]
    small = [pltpu.make_async_copy(sources[j], homes[j], sems.at[j]) for j in range(1, 5)]
    tiles = [
        pltpu.make_async_copy(sources[0].at[k], homes[0].at[k], sems.at[5 + k]) for k in range(slots)
    ]
    for copy in small + tiles:
        copy.start()
    flows, routing, tile_block, ec, ic = homes
    exp_place, imp_place = lax.axis_index("exp"), lax.axis_index("imp")
    side = lay.side
    row_blocks = ec.shape[0]
    col_local = ic.shape[0]
    out[...] = jnp.zeros_like(out)
    per = side // LANES
    country = iota((NCE, side), 0)
    ones = jnp.ones((8, side), bf16)
    for copy in small:
        copy.wait()
    cnt_a = jnp.zeros((8, LANES), f32)
    for r in range(row_blocks):
        cnt_a += dot(ones, (country == ec[r]).astype(f32).astype(bf16), 1, 1)
    cnt_b = jnp.zeros((8, LANES), f32)
    for c in range(col_local):
        cnt_b += dot(ones, (country == ic[c]).astype(f32).astype(bf16), 1, 1)
    cnt_a = cnt_a[0:1] * (imp_place == 0).astype(f32)
    cnt_b = cnt_b[0:1] * (exp_place == 0).astype(f32)
    out[lay.cnt_at : lay.cnt_at + 1, :] = cnt_a
    out[lay.cnt_at + 1 : lay.cnt_at + 2, :] = cnt_b
    pairs = jnp.zeros((NCE, NCI), f32)
    for k in range(slots):
        r = tile_block[k] // col_local
        c = tile_block[k] % col_local
        live = routing[0] == k
        for t in range(1, routing.shape[0]):
            live = live | (routing[t] == k)
        keep = live.astype(f32)
        hot_r = (country == ec[r]).astype(f32).astype(bf16)
        hot_c = (country == ic[c]).astype(f32).astype(bf16)
        tiles[k].wait()
        tile = flows[k] * keep.astype(bf16)
        half = dot(hot_r, tile, 1, 0)
        col_sum = jnp.sum(half, axis=0, keepdims=True)
        row_sum = dot(ones, tile, 1, 1)[0:1]
        top = half.astype(bf16)
        rest = (half - top.astype(f32)).astype(bf16)
        both = dot(jnp.concatenate([top, rest], axis=0), hot_c, 1, 1)
        pairs = pairs + (both[:NCE] + both[NCE:])
        row_at = lay.rows_at + (exp_place * row_blocks + r) * per
        col_at = lay.cols_at + (imp_place * col_local + c) * per
        for h in range(per):
            cut = slice(h * LANES, (h + 1) * LANES)
            out[pl.ds(row_at + h, 1), :] += row_sum[:, cut]
            out[pl.ds(col_at + h, 1), :] += col_sum[:, cut]
        flat = (exp_place * row_blocks + r) * lay.blocks_b + imp_place * col_local + c
        here = iota((1, LANES), 1) == flat % LANES
        out[pl.ds(lay.live_at + flat // LANES, 1), :] += jnp.where(here, keep, 0.0)
    out[lay.pairs_at : lay.pairs_at + NCE, :] = pairs
    mine = half_of(exp_place, imp_place)
    keeps, send = outs[:2], outs[2]
    at = 0
    for keep, start, share in zip(keeps, lay.starts, lay.shares):
        keep[...] = out[pl.ds(pl.multiple_of(start + mine * share, 8), share), :]
        send[at : at + share, :] = out[pl.ds(pl.multiple_of(start + (1 - mine) * share, 8), share), :]
        at += share


def put_back(lay, chunk, mine, halves, whole):
    for k, part in enumerate(halves):
        share = lay.shares[chunk]
        whole[pl.ds(pl.multiple_of((mine ^ k) * share, 8), share), :] = part[...]


def lookup(row, index):
    return jnp.take_along_axis(
        jnp.broadcast_to(row, index.shape), index, axis=1, mode="promise_in_bounds"
    )


def down(row):
    return jnp.transpose(jnp.broadcast_to(row, (LANES, LANES)))


def across(x):
    return jnp.sum(jnp.transpose(x), axis=0, keepdims=True)


def below(x):
    return jnp.sum(x, axis=0, keepdims=True)


def eights(x):
    return functools.reduce(lambda u, v: u + v, [x[j : j + 8] for j in range(0, x.shape[0], 8)])


def inner(u, v):
    partial = eights(u[0] * v[0]) + eights(u[1] * v[1]) + eights(u[2] * v[2])
    return jnp.sum(below(partial), axis=1, keepdims=True)


def positions(n, block, start, middle, end, hot, country_ref, second_ref):
    shape = (n // LANES, LANES)
    place = (iota(shape, 0) * LANES + iota(shape, 1)).astype(f32)
    country = jnp.zeros(shape, i32)
    jump = LANES // 2
    while jump:
        passed = lookup(end, country + (jump - 1)) <= place
        country = jnp.where(passed, country + jump, country)
        jump //= 2
    country_ref[...] = country
    second_ref[...] = jnp.where(place >= lookup(middle, country), 1.0, 0.0)
    for j in range(n // block):
        at = (iota((block, LANES), 0) + j * block).astype(f32)
        inside = (at >= start) & (at < end)
        hot[j * block : (j + 1) * block, :] = jnp.where(inside, 1.0, 0.0).astype(bf16)


class Side:
    def __init__(self, n, block, country, second, hot, stage):
        self.n, self.block, self.hot, self.stage = n, block, hot, stage
        self.chunks = n // LANES
        self.country = country[...]
        self.second = second[...] > 0.5

    def expand(self, first, second):
        return jnp.where(self.second, lookup(second, self.country), lookup(first, self.country))

    def sums(self, vectors):
        chunks, stage = self.chunks, self.stage
        for k, v in enumerate(vectors):
            stage[2 * k * chunks : (2 * k + 1) * chunks, :] = jnp.where(self.second, 0.0, v)
            stage[(2 * k + 1) * chunks : (2 * k + 2) * chunks, :] = jnp.where(self.second, v, 0.0)
        high = -(-2 * len(vectors) // 8) * 8
        for k in range(2 * len(vectors), high):
            stage[k * chunks : (k + 1) * chunks, :] = jnp.zeros((chunks, LANES), f32)
        got = jnp.zeros((3 * high, LANES), f32)
        per = self.block // LANES
        for j in range(chunks // per):
            left = jnp.concatenate(
                [stage[pl.ds(j * per + h, high, stride=chunks), :] for h in range(per)], axis=1
            )
            pieces = jnp.concatenate(split(left), axis=0).astype(bf16)
            got += dot(pieces, self.hot[j * self.block : (j + 1) * self.block, :], 1, 0)
        return got[:high] + got[high : 2 * high] + got[2 * high :]

    def maxima(self, values_ref, low, high):
        low, high = down(low), down(high)

        def body(j, best):
            at = (iota((LANES, LANES), 1) + j * LANES).astype(f32)
            inside = (at >= low) & (at < high)
            return jnp.maximum(best, jnp.where(inside, values_ref[pl.ds(j, 1), :], -jnp.inf))

        best = lax.fori_loop(0, self.chunks, body, jnp.full((LANES, LANES), -jnp.inf, f32))
        best = jnp.max(jnp.transpose(best), axis=0, keepdims=True)
        return jnp.where(best > -jnp.inf, best, 0.0)


def prepare_kernel(lay, *refs):
    halves, refs = refs[:2], refs[2:]
    tables, mask, hot_a, hot_b, country_a, country_b, second_a, second_b, shared = refs
    put_back(lay, 0, half_of(lax.axis_index("exp"), lax.axis_index("imp")), halves, shared)
    side = lay.side
    tally = shared[lay.cnt_at : lay.cnt_at + 8, :]
    before = jnp.where(iota((LANES, LANES), 0) < iota((LANES, LANES), 1), 1.0, 0.0).astype(bf16)
    start = dot(tally.astype(bf16), before, 1, 0)
    end = start + tally
    first = jnp.floor((start + 0.5) * (1.0 / side))
    middle = jnp.minimum(end, (first + 1.0) * side)

    def table(x, y):
        return jnp.concatenate([x[0:1], y[0:1], x[1:2], y[1:2]], axis=0)

    low, high = table(start, middle), table(middle, end)
    full = high - low > 0.5
    tables[0:4, :] = low
    tables[4:8, :] = high
    block_of = jnp.where(full, table(first, first + 1.0), -1.0)
    positions(lay.na, side, start[0:1], middle[0:1], end[0:1], hot_a, country_a, second_a)
    positions(lay.nb, side, start[1:2], middle[1:2], end[1:2], hot_b, country_b, second_b)

    wide = lay.blocks_b
    spots = [(r * wide // LANES, r * wide % LANES) for r in range(lay.blocks_a)]
    live = jnp.concatenate(
        [shared[lay.live_at + row : lay.live_at + row + 1, at : at + wide] for row, at in spots], axis=0
    ).astype(bf16)
    number = iota((LANES, LANES), 1).astype(f32)
    pick_a = [jnp.where(down(block_of[p : p + 1]) == number, 1.0, 0.0).astype(bf16) for p in (0, 1)]
    number = iota((LANES, LANES), 0).astype(f32)
    pick_b = [jnp.where(block_of[q : q + 1] == number, 1.0, 0.0).astype(bf16) for q in (2, 3)]
    reach = [dot(pick[:, : lay.blocks_a], live, 1, 0).astype(bf16) for pick in pick_a]
    for p in (0, 1):
        for q in (0, 1):
            mask[2 * p + q] = dot(reach[p], pick_b[q][: lay.blocks_b], 1, 0)


def solve_kernel(lay, *refs):
    where = lax.axis_index("exp"), lax.axis_index("imp")
    halves, refs = refs[:4], refs[4:]
    tables, mask_ref, hot_a, hot_b, country_a, country_b, second_a, second_b = refs[:8]
    out_a, out_b, out_g, shared, stage_a, stage_b, val_a, val_b, shift_ref = refs[8:]
    mine = half_of(*where)
    for chunk, start in enumerate(lay.starts):
        room = shared.at[start : start + 2 * lay.shares[chunk]]
        put_back(lay, chunk, mine, halves[2 * chunk : 2 * chunk + 2], room)
    flow = (
        shared[lay.rows_at : lay.cols_at, :],
        shared[lay.cols_at : lay.total, :],
        shared[lay.pairs_at : lay.pairs_at + NCE, :],
    )
    side = lay.side
    low, high = tables[0:4, :], tables[4:8, :]
    count = high - low
    full = count > 0.5
    inv_count = jnp.where(full, 1.0 / jnp.maximum(count, 1.0), 0.0)
    sa = Side(lay.na, side, country_a, second_a, hot_a, stage_a)
    sb = Side(lay.nb, side, country_b, second_b, hot_b, stage_b)
    mask = [[mask_ref[2 * p + q] for q in (0, 1)] for p in (0, 1)]

    a = jnp.zeros((lay.na // LANES, LANES), f32)
    b = jnp.zeros((lay.nb // LANES, LANES), f32)
    g = jnp.zeros((NCE, NCI), f32)
    mean = jnp.zeros((4, LANES), f32)
    for newton in range(NEWTON):
        if newton == 0:
            left = flow
            weight, inv, rate = count, inv_count, mask
            sum_a, sum_b = sa.sums([flow[0]]), sb.sums([flow[1]])
            part_a, part_b = sa.expand(inv[0:1], inv[1:2]), sb.expand(inv[2:3], inv[3:4])
            m2, m3 = inv, inv * inv
            f1 = jnp.concatenate([sum_a[0:2], sum_b[0:2]], axis=0) * inv
            f2 = f1 * inv
        else:
            left = (flow[0] - RIDGE * a, flow[1] - RIDGE * b, flow[2] - RIDGE * g)
            shift_ref[0:4, :] = mean
            off_a = a - sa.expand(mean[0:1], mean[1:2])
            off_b = b - sb.expand(mean[2:3], mean[3:4])
            worst = jnp.maximum(jnp.max(off_a), jnp.max(off_b))
            val_a[...] = a
            val_b[...] = b

            @pl.when(worst > 20.0)
            def _():
                shift_ref[0:1, :] = sa.maxima(val_a, low[0:1], high[0:1])
                shift_ref[1:2, :] = sa.maxima(val_a, low[1:2], high[1:2])
                shift_ref[2:3, :] = sb.maxima(val_b, low[2:3], high[2:3])
                shift_ref[3:4, :] = sb.maxima(val_b, low[3:4], high[3:4])

            shift = shift_ref[0:4, :]
            size_a = jnp.exp(a - sa.expand(shift[0:1], shift[1:2]))
            size_b = jnp.exp(b - sb.expand(shift[2:3], shift[3:4]))

            def moments(s, x, f):
                return s.sums([x, x * x, x * x * x, x * f, x * x * f])

            sum_a, sum_b = moments(sa, size_a, left[0]), moments(sb, size_b, left[1])
            got = [jnp.concatenate([sum_a[2 * k : 2 * k + 2], sum_b[2 * k : 2 * k + 2]], axis=0) for k in range(5)]
            weight = got[0]
            inv = jnp.where(full, 1.0 / jnp.where(full, weight, 1.0), 0.0)
            part_a = size_a * sa.expand(inv[0:1], inv[1:2])
            part_b = size_b * sb.expand(inv[2:3], inv[3:4])
            inv2 = inv * inv
            m2, m3 = got[1] * inv2, got[2] * (inv2 * inv)
            f1, f2 = got[3] * inv, got[4] * inv2
            lift = [g + down(shift[p : p + 1]) for p in (0, 1)]
            rate = [
                [jnp.where(mask[p][q] > 0.5, jnp.exp(lift[p] + shift[2 + q : 3 + q]), 0.0) for q in (0, 1)]
                for p in (0, 1)
            ]
        tall = [down(weight[p : p + 1]) for p in (0, 1)]
        mu = [[rate[p][q] * (tall[p] * weight[2 + q : 3 + q]) for q in (0, 1)] for p in (0, 1)]
        mu_a = [mu[p][0] + mu[p][1] for p in (0, 1)]
        mu_b = [mu[0][q] + mu[1][q] for q in (0, 1)]
        whole = jnp.concatenate([across(mu_a[0]), across(mu_a[1]), below(mu_b[0]), below(mu_b[1])], axis=0)
        da = part_a * sa.expand(whole[0:1], whole[1:2])
        db = part_b * sb.expand(whole[2:3], whole[3:4])
        res = (left[0] - da, left[1] - db, left[2] - (mu_a[0] + mu_a[1]))
        way = res
        norm = inner(res, res)
        v = f1 - whole * m2
        w = f2 - whole * m3
        for sweep in range(CG):
            tall = [down(v[p : p + 1]) for p in (0, 1)]
            flat = [v[2 + q : 3 + q] for q in (0, 1)]
            ga = [mu[p][0] * flat[0] + mu[p][1] * flat[1] + way[2] * mu_a[p] for p in (0, 1)]
            gb = [mu[0][q] * tall[0] + mu[1][q] * tall[1] + way[2] * mu_b[q] for q in (0, 1)]
            u = jnp.concatenate([across(ga[0]), across(ga[1]), below(gb[0]), below(gb[1])], axis=0)
            image = (
                (da + RIDGE) * way[0] + part_a * sa.expand(u[0:1], u[1:2]),
                (db + RIDGE) * way[1] + part_b * sb.expand(u[2:3], u[3:4]),
                RIDGE * way[2] + (ga[0] + ga[1]) + (tall[0] * mu_a[0] + tall[1] * mu_a[1]),
            )
            step = norm / inner(way, image)
            a, b, g = a + step * way[0], b + step * way[1], g + step * way[2]
            if newton + 1 < NEWTON:
                mean = mean + step * v
            if sweep + 1 < CG:
                res = tuple(x - step * y for x, y in zip(res, image))
                fresh = inner(res, res)
                ratio = fresh / norm
                way = tuple(x + ratio * y for x, y in zip(res, way))
                norm = fresh
                v = v - step * (whole * w + RIDGE * v + u * m2) + ratio * v
    out_g[...] = g
    val_a[...] = a
    val_b[...] = b
    for out, val, at in ((out_a, val_a, where[0]), (out_b, val_b, where[1])):
        rows = out.shape[0] // LANES
        for j in range(rows):
            out[j * LANES : (j + 1) * LANES] = val[pl.ds(at * rows + j, 1), :].reshape(LANES)


def powers(first, limit):
    return [1 << k for k in range(16) if first <= 1 << k < limit]


def swap(x, n_exp, n_imp, exp_bits, imp_bits):
    pairs = [
        (e * n_imp + m, (e ^ exp_bits) * n_imp + (m ^ imp_bits)) for e in range(n_exp) for m in range(n_imp)
    ]
    return lax.ppermute(x, ("exp", "imp"), pairs)


def per_device(mesh_shape, flows, routing, tile_block, exp_country, imp_country):
    slots, side = flows.shape[0], flows.shape[1]
    n_exp, n_imp = mesh_shape
    rows, cols = exp_country.shape[0], imp_country.shape[0]
    lay = Layout(rows * n_exp, cols * n_imp, side)
    vmem = pl.BlockSpec(memory_space=pltpu.VMEM)
    inputs = (
        flows,
        routing.reshape(-1),
        tile_block,
        exp_country.reshape(-1, 1, side),
        imp_country.reshape(-1, 1, side),
    )
    inputs = tuple(pltpu.with_memory_space_constraint(x, pltpu.HBM) for x in inputs)
    homes = [pltpu.VMEM, pltpu.SMEM, pltpu.SMEM, pltpu.VMEM, pltpu.VMEM]
    parts = pl.pallas_call(
        functools.partial(local_kernel, lay, slots),
        out_shape=[jax.ShapeDtypeStruct((size, LANES), f32) for size in (*lay.shares, sum(lay.shares))],
        in_specs=[pl.BlockSpec(memory_space=pltpu.HBM)] * 5,
        out_specs=[vmem] * 3,
        scratch_shapes=[pltpu.VMEM((lay.padded, LANES), f32)]
        + [space(x.shape, x.dtype) for space, x in zip(homes, inputs)]
        + [pltpu.SemaphoreType.DMA((5 + slots,))],
        compiler_params=pltpu.CompilerParams(vmem_limit_bytes=VMEM_BYTES),
        name="local_sums",
    )(*inputs)
    halves = []
    other = swap(parts[2], n_exp, n_imp, 1, 0)
    first = lay.shares[0]
    for mine in (parts[0] + other[:first], parts[1] + other[first:]):
        for bit in powers(2, n_exp):
            mine = mine + swap(mine, n_exp, n_imp, bit | 1, 0)
        for bit in powers(1, n_imp):
            mine = mine + swap(mine, n_exp, n_imp, 1, 2 * bit - 1)
        halves += [mine, swap(mine, n_exp, n_imp, 1, 0)]
    shape_a, shape_b = (lay.na // LANES, LANES), (lay.nb // LANES, LANES)
    ready = pl.pallas_call(
        functools.partial(prepare_kernel, lay),
        out_shape=(
            jax.ShapeDtypeStruct((8, LANES), f32),
            jax.ShapeDtypeStruct((4, NCE, NCI), f32),
            jax.ShapeDtypeStruct((lay.na, LANES), bf16),
            jax.ShapeDtypeStruct((lay.nb, LANES), bf16),
            jax.ShapeDtypeStruct(shape_a, i32),
            jax.ShapeDtypeStruct(shape_b, i32),
            jax.ShapeDtypeStruct(shape_a, f32),
            jax.ShapeDtypeStruct(shape_b, f32),
        ),
        in_specs=[vmem] * 2,
        out_specs=(vmem,) * 8,
        scratch_shapes=[pltpu.VMEM((2 * lay.shares[0], LANES), f32)],
        compiler_params=pltpu.CompilerParams(vmem_limit_bytes=VMEM_BYTES),
        cost_estimate=pl.CostEstimate(flops=10**9, bytes_accessed=4 * 10**6, transcendentals=0),
        name="prepare",
    )(*halves[:2])
    most = 16
    a, b, g = pl.pallas_call(
        functools.partial(solve_kernel, lay),
        out_shape=(
            jax.ShapeDtypeStruct((rows,), f32),
            jax.ShapeDtypeStruct((cols,), f32),
            jax.ShapeDtypeStruct((NCE, NCI), f32),
        ),
        in_specs=[vmem] * 12,
        out_specs=(vmem, vmem, vmem),
        scratch_shapes=[
            pltpu.VMEM((lay.padded, LANES), f32),
            pltpu.VMEM((most * lay.na // LANES, LANES), f32),
            pltpu.VMEM((most * lay.nb // LANES, LANES), f32),
            pltpu.VMEM(shape_a, f32),
            pltpu.VMEM(shape_b, f32),
            pltpu.VMEM((8, LANES), f32),
        ],
        compiler_params=pltpu.CompilerParams(vmem_limit_bytes=VMEM_BYTES),
        name="solve",
    )(*halves, *ready)
    return a, b, g


def solution(mesh):
    placed = (
        P(("exp", "imp"), None, None),
        P(("exp", "imp"), None, None),
        P(("exp", "imp")),
        P("exp"),
        P("imp"),
    )
    return jax.shard_map(
        functools.partial(per_device, (mesh.shape["exp"], mesh.shape["imp"])),
        mesh=mesh,
        in_specs=placed,
        out_specs=(P("exp"), P("imp"), P()),
        check_vma=False,
    )
```

```python
import functools

import jax
import jax.numpy as jnp
from jax import lax
from jax.experimental import pallas as pl
from jax.experimental.pallas import tpu as pltpu
from jax.sharding import PartitionSpec as P

NCE = 128
NCI = 128
NEWTON = 2
CG = 2
LANES = 128
RIDGE = 64.0
VMEM_BYTES = 48 * 1024 * 1024

f32 = jnp.float32
bf16 = jnp.bfloat16
i32 = jnp.int32


def iota(shape, dim):
    return lax.broadcasted_iota(i32, shape, dim)


def split(x):
    hi = x.astype(bf16).astype(f32)
    rest = x - hi
    mid = rest.astype(bf16).astype(f32)
    return hi, mid, rest - mid


def dot(x, y, cx, cy, precision=None):
    return lax.dot_general(
        x, y, (((cx,), (cy,)), ((), ())), precision=precision, preferred_element_type=f32
    )


class Layout:
    def __init__(self, na, nb, side):
        self.na, self.nb, self.side = na, nb, side
        self.rows_at = NCE
        self.cols_at = self.rows_at + na // LANES
        self.cnt_at = self.cols_at + nb // LANES
        self.live_at = self.cnt_at + 2
        self.blocks_a, self.blocks_b = na // side, nb // side
        self.total = -(-(self.live_at - (-self.blocks_a * self.blocks_b // LANES)) // 8) * 8
        self.share = -(-self.total // 16) * 8


def half_of(exp_place, imp_place):
    bits = exp_place ^ (imp_place & 1)
    for shift in (8, 4, 2, 1):
        bits = bits ^ (bits >> shift)
    return bits & 1


def local_kernel(lay, slots, *refs):
    sources, outs, out, homes, sems = refs[:5], refs[5:7], refs[7], refs[8:13], refs[13]
    small = [pltpu.make_async_copy(sources[j], homes[j], sems.at[j]) for j in range(1, 5)]
    tiles = [
        pltpu.make_async_copy(sources[0].at[k], homes[0].at[k], sems.at[5 + k]) for k in range(slots)
    ]
    for copy in small + tiles:
        copy.start()
    flows, routing, tile_block, ec, ic = homes
    exp_place, imp_place = lax.axis_index("exp"), lax.axis_index("imp")
    side = lay.side
    row_blocks = ec.shape[0]
    col_local = ic.shape[0]
    out[...] = jnp.zeros_like(out)
    per = side // LANES
    country = iota((NCE, side), 0)
    ones = jnp.ones((8, side), bf16)
    for copy in small:
        copy.wait()
    cnt_a = jnp.zeros((8, LANES), f32)
    for r in range(row_blocks):
        cnt_a += dot(ones, (country == ec[r]).astype(f32).astype(bf16), 1, 1)
    cnt_b = jnp.zeros((8, LANES), f32)
    for c in range(col_local):
        cnt_b += dot(ones, (country == ic[c]).astype(f32).astype(bf16), 1, 1)
    cnt_a = cnt_a[0:1] * (imp_place == 0).astype(f32)
    cnt_b = cnt_b[0:1] * (exp_place == 0).astype(f32)
    out[lay.cnt_at : lay.cnt_at + 1, :] = cnt_a
    out[lay.cnt_at + 1 : lay.cnt_at + 2, :] = cnt_b
    pairs = jnp.zeros((NCE, NCI), f32)
    for k in range(slots):
        r = tile_block[k] // col_local
        c = tile_block[k] % col_local
        live = routing[0] == k
        for t in range(1, routing.shape[0]):
            live = live | (routing[t] == k)
        keep = live.astype(f32)
        hot_r = (country == ec[r]).astype(f32).astype(bf16)
        hot_c = (country == ic[c]).astype(f32).astype(bf16)
        tiles[k].wait()
        tile = flows[k] * keep.astype(bf16)
        half = dot(hot_r, tile, 1, 0)
        col_sum = jnp.sum(half, axis=0, keepdims=True)
        row_sum = dot(ones, tile, 1, 1)[0:1]
        top = half.astype(bf16)
        rest = (half - top.astype(f32)).astype(bf16)
        both = dot(jnp.concatenate([top, rest], axis=0), hot_c, 1, 1)
        pairs = pairs + (both[:NCE] + both[NCE:])
        row_at = lay.rows_at + (exp_place * row_blocks + r) * per
        col_at = lay.cols_at + (imp_place * col_local + c) * per
        for h in range(per):
            cut = slice(h * LANES, (h + 1) * LANES)
            out[pl.ds(row_at + h, 1), :] += row_sum[:, cut]
            out[pl.ds(col_at + h, 1), :] += col_sum[:, cut]
        flat = (exp_place * row_blocks + r) * lay.blocks_b + imp_place * col_local + c
        here = iota((1, LANES), 1) == flat % LANES
        out[pl.ds(lay.live_at + flat // LANES, 1), :] += jnp.where(here, keep, 0.0)
    out[0:NCE, :] = pairs
    mine = half_of(exp_place, imp_place)
    for k, part in enumerate(outs):
        part[...] = out[pl.ds(pl.multiple_of((mine ^ k) * lay.share, 8), lay.share), :]


def lookup(row, index):
    return jnp.take_along_axis(
        jnp.broadcast_to(row, index.shape), index, axis=1, mode="promise_in_bounds"
    )


def down(row):
    return jnp.transpose(jnp.broadcast_to(row, (LANES, LANES)))


def across(x):
    return jnp.sum(jnp.transpose(x), axis=0, keepdims=True)


def below(x):
    return jnp.sum(x, axis=0, keepdims=True)


def eights(x):
    return functools.reduce(lambda u, v: u + v, [x[j : j + 8] for j in range(0, x.shape[0], 8)])


def inner(u, v):
    partial = eights(u[0] * v[0]) + eights(u[1] * v[1]) + eights(u[2] * v[2])
    return jnp.sum(below(partial), axis=1, keepdims=True)


class Side:
    def __init__(self, n, block, start, middle, end, hot, stage):
        self.n, self.block, self.hot, self.stage = n, block, hot, stage
        self.chunks = n // LANES
        shape = (self.chunks, LANES)
        place = (iota(shape, 0) * LANES + iota(shape, 1)).astype(f32)
        country = jnp.zeros(shape, i32)
        jump = LANES // 2
        while jump:
            passed = lookup(end, country + (jump - 1)) <= place
            country = jnp.where(passed, country + jump, country)
            jump //= 2
        self.country = country
        self.second = place >= lookup(middle, country)
        at = iota((block, LANES), 0).astype(f32).astype(bf16)
        one, none = jnp.ones((block, LANES), bf16), jnp.zeros((block, LANES), bf16)
        for j in range(n // block):
            lo, hi = (jnp.clip(x - j * block, 0.0, block).astype(bf16) for x in (start, end))
            inside = (at >= lo) & (at < hi)
            hot[j * block : (j + 1) * block, :] = jnp.where(inside, one, none)

    def expand(self, first, second):
        return jnp.where(self.second, lookup(second, self.country), lookup(first, self.country))

    def sums(self, vectors):
        chunks, stage = self.chunks, self.stage
        for k, v in enumerate(vectors):
            stage[2 * k * chunks : (2 * k + 1) * chunks, :] = jnp.where(self.second, 0.0, v)
            stage[(2 * k + 1) * chunks : (2 * k + 2) * chunks, :] = jnp.where(self.second, v, 0.0)
        high = -(-2 * len(vectors) // 8) * 8
        for k in range(2 * len(vectors), high):
            stage[k * chunks : (k + 1) * chunks, :] = jnp.zeros((chunks, LANES), f32)
        got = jnp.zeros((3 * high, LANES), f32)
        per = self.block // LANES
        for j in range(chunks // per):
            left = jnp.concatenate(
                [stage[pl.ds(j * per + h, high, stride=chunks), :] for h in range(per)], axis=1
            )
            pieces = jnp.concatenate(split(left), axis=0).astype(bf16)
            got += dot(pieces, self.hot[j * self.block : (j + 1) * self.block, :], 1, 0)
        return got[:high] + got[high : 2 * high] + got[2 * high :]

    def maxima(self, values_ref, low, high):
        low, high = down(low), down(high)

        def body(j, best):
            at = (iota((LANES, LANES), 1) + j * LANES).astype(f32)
            inside = (at >= low) & (at < high)
            return jnp.maximum(best, jnp.where(inside, values_ref[pl.ds(j, 1), :], -jnp.inf))

        best = lax.fori_loop(0, self.chunks, body, jnp.full((LANES, LANES), -jnp.inf, f32))
        best = jnp.max(jnp.transpose(best), axis=0, keepdims=True)
        return jnp.where(best > -jnp.inf, best, 0.0)


def solve_kernel(lay, *refs):
    where = lax.axis_index("exp"), lax.axis_index("imp")
    shares, refs = refs[:2], refs[2:]
    out_a, out_b, out_g, shared, hot_a, hot_b, stage_a, stage_b, val_a, val_b, shift_ref = refs
    mine = half_of(*where)
    for k, part in enumerate(shares):
        shared[pl.ds(pl.multiple_of((mine ^ k) * lay.share, 8), lay.share), :] = part[...]
    flow = (
        shared[lay.rows_at : lay.cols_at, :],
        shared[lay.cols_at : lay.cnt_at, :],
        shared[0:NCE, :],
    )
    side = lay.side
    tally = shared[lay.cnt_at : lay.cnt_at + 8, :]
    before = jnp.where(iota((LANES, LANES), 0) < iota((LANES, LANES), 1), 1.0, 0.0).astype(bf16)
    start = dot(tally.astype(bf16), before, 1, 0)
    end = start + tally
    first = jnp.floor((start + 0.5) * (1.0 / side))
    middle = jnp.minimum(end, (first + 1.0) * side)

    def table(x, y):
        return jnp.concatenate([x[0:1], y[0:1], x[1:2], y[1:2]], axis=0)

    low, high = table(start, middle), table(middle, end)
    count = high - low
    full = count > 0.5
    inv_count = jnp.where(full, 1.0 / jnp.maximum(count, 1.0), 0.0)
    block_of = jnp.where(full, table(first, first + 1.0), -1.0)
    sa = Side(lay.na, side, start[0:1], middle[0:1], end[0:1], hot_a, stage_a)
    sb = Side(lay.nb, side, start[1:2], middle[1:2], end[1:2], hot_b, stage_b)

    wide = lay.blocks_b
    spots = [(r * wide // LANES, r * wide % LANES) for r in range(lay.blocks_a)]
    live = jnp.concatenate(
        [shared[lay.live_at + row : lay.live_at + row + 1, at : at + wide] for row, at in spots], axis=0
    ).astype(bf16)
    number = iota((LANES, LANES), 1).astype(f32)
    pick_a = [jnp.where(down(block_of[p : p + 1]) == number, 1.0, 0.0).astype(bf16) for p in (0, 1)]
    number = iota((LANES, LANES), 0).astype(f32)
    pick_b = [jnp.where(block_of[q : q + 1] == number, 1.0, 0.0).astype(bf16) for q in (2, 3)]
    reach = [dot(pick[:, : lay.blocks_a], live, 1, 0).astype(bf16) for pick in pick_a]
    mask = [[dot(reach[p], pick_b[q][: lay.blocks_b], 1, 0) for q in (0, 1)] for p in (0, 1)]

    a = jnp.zeros((lay.na // LANES, LANES), f32)
    b = jnp.zeros((lay.nb // LANES, LANES), f32)
    g = jnp.zeros((NCE, NCI), f32)
    mean = jnp.zeros((4, LANES), f32)
    for newton in range(NEWTON):
        if newton == 0:
            left = flow
            weight, inv, rate = count, inv_count, mask
            sum_a, sum_b = sa.sums([flow[0]]), sb.sums([flow[1]])
            part_a, part_b = sa.expand(inv[0:1], inv[1:2]), sb.expand(inv[2:3], inv[3:4])
            m2, m3 = inv, inv * inv
            f1 = jnp.concatenate([sum_a[0:2], sum_b[0:2]], axis=0) * inv
            f2 = f1 * inv
        else:
            left = (flow[0] - RIDGE * a, flow[1] - RIDGE * b, flow[2] - RIDGE * g)
            shift_ref[0:4, :] = mean
            off_a = a - sa.expand(mean[0:1], mean[1:2])
            off_b = b - sb.expand(mean[2:3], mean[3:4])
            worst = jnp.maximum(jnp.max(off_a), jnp.max(off_b))
            val_a[...] = a
            val_b[...] = b

            @pl.when(worst > 20.0)
            def _():
                shift_ref[0:1, :] = sa.maxima(val_a, low[0:1], high[0:1])
                shift_ref[1:2, :] = sa.maxima(val_a, low[1:2], high[1:2])
                shift_ref[2:3, :] = sb.maxima(val_b, low[2:3], high[2:3])
                shift_ref[3:4, :] = sb.maxima(val_b, low[3:4], high[3:4])

            shift = shift_ref[0:4, :]
            size_a = jnp.exp(a - sa.expand(shift[0:1], shift[1:2]))
            size_b = jnp.exp(b - sb.expand(shift[2:3], shift[3:4]))

            def moments(s, x, f):
                return s.sums([x, x * x, x * x * x, x * f, x * x * f])

            sum_a, sum_b = moments(sa, size_a, left[0]), moments(sb, size_b, left[1])
            got = [jnp.concatenate([sum_a[2 * k : 2 * k + 2], sum_b[2 * k : 2 * k + 2]], axis=0) for k in range(5)]
            weight = got[0]
            inv = jnp.where(full, 1.0 / jnp.where(full, weight, 1.0), 0.0)
            part_a = size_a * sa.expand(inv[0:1], inv[1:2])
            part_b = size_b * sb.expand(inv[2:3], inv[3:4])
            inv2 = inv * inv
            m2, m3 = got[1] * inv2, got[2] * (inv2 * inv)
            f1, f2 = got[3] * inv, got[4] * inv2
            lift = [g + down(shift[p : p + 1]) for p in (0, 1)]
            rate = [
                [jnp.where(mask[p][q] > 0.5, jnp.exp(lift[p] + shift[2 + q : 3 + q]), 0.0) for q in (0, 1)]
                for p in (0, 1)
            ]
        tall = [down(weight[p : p + 1]) for p in (0, 1)]
        mu = [[rate[p][q] * (tall[p] * weight[2 + q : 3 + q]) for q in (0, 1)] for p in (0, 1)]
        mu_a = [mu[p][0] + mu[p][1] for p in (0, 1)]
        mu_b = [mu[0][q] + mu[1][q] for q in (0, 1)]
        whole = jnp.concatenate([across(mu_a[0]), across(mu_a[1]), below(mu_b[0]), below(mu_b[1])], axis=0)
        da = part_a * sa.expand(whole[0:1], whole[1:2])
        db = part_b * sb.expand(whole[2:3], whole[3:4])
        res = (left[0] - da, left[1] - db, left[2] - (mu_a[0] + mu_a[1]))
        way = res
        norm = inner(res, res)
        v = f1 - whole * m2
        w = f2 - whole * m3
        for sweep in range(CG):
            tall = [down(v[p : p + 1]) for p in (0, 1)]
            flat = [v[2 + q : 3 + q] for q in (0, 1)]
            ga = [mu[p][0] * flat[0] + mu[p][1] * flat[1] + way[2] * mu_a[p] for p in (0, 1)]
            gb = [mu[0][q] * tall[0] + mu[1][q] * tall[1] + way[2] * mu_b[q] for q in (0, 1)]
            u = jnp.concatenate([across(ga[0]), across(ga[1]), below(gb[0]), below(gb[1])], axis=0)
            image = (
                (da + RIDGE) * way[0] + part_a * sa.expand(u[0:1], u[1:2]),
                (db + RIDGE) * way[1] + part_b * sb.expand(u[2:3], u[3:4]),
                RIDGE * way[2] + (ga[0] + ga[1]) + (tall[0] * mu_a[0] + tall[1] * mu_a[1]),
            )
            step = norm / inner(way, image)
            a, b, g = a + step * way[0], b + step * way[1], g + step * way[2]
            if newton + 1 < NEWTON:
                mean = mean + step * v
            if sweep + 1 < CG:
                res = tuple(x - step * y for x, y in zip(res, image))
                fresh = inner(res, res)
                ratio = fresh / norm
                way = tuple(x + ratio * y for x, y in zip(res, way))
                norm = fresh
                v = v - step * (whole * w + RIDGE * v + u * m2) + ratio * v
    out_g[...] = g
    val_a[...] = a
    val_b[...] = b
    for out, val, at in ((out_a, val_a, where[0]), (out_b, val_b, where[1])):
        rows = out.shape[0] // LANES
        for j in range(rows):
            out[j * LANES : (j + 1) * LANES] = val[pl.ds(at * rows + j, 1), :].reshape(LANES)


def powers(first, limit):
    return [1 << k for k in range(16) if first <= 1 << k < limit]


def swap(x, n_exp, n_imp, exp_bits, imp_bits):
    pairs = [
        (e * n_imp + m, (e ^ exp_bits) * n_imp + (m ^ imp_bits)) for e in range(n_exp) for m in range(n_imp)
    ]
    return lax.ppermute(x, ("exp", "imp"), pairs)


def per_device(mesh_shape, flows, routing, tile_block, exp_country, imp_country):
    slots, side = flows.shape[0], flows.shape[1]
    n_exp, n_imp = mesh_shape
    rows, cols = exp_country.shape[0], imp_country.shape[0]
    lay = Layout(rows * n_exp, cols * n_imp, side)
    vmem = pl.BlockSpec(memory_space=pltpu.VMEM)
    inputs = (
        flows,
        routing.reshape(-1),
        tile_block,
        exp_country.reshape(-1, 1, side),
        imp_country.reshape(-1, 1, side),
    )
    inputs = tuple(pltpu.with_memory_space_constraint(x, pltpu.HBM) for x in inputs)
    homes = [pltpu.VMEM, pltpu.SMEM, pltpu.SMEM, pltpu.VMEM, pltpu.VMEM]
    parts = pl.pallas_call(
        functools.partial(local_kernel, lay, slots),
        out_shape=[jax.ShapeDtypeStruct((lay.share, LANES), f32)] * 2,
        in_specs=[pl.BlockSpec(memory_space=pltpu.HBM)] * 5,
        out_specs=[vmem] * 2,
        scratch_shapes=[pltpu.VMEM((2 * lay.share, LANES), f32)]
        + [space(x.shape, x.dtype) for space, x in zip(homes, inputs)]
        + [pltpu.SemaphoreType.DMA((5 + slots,))],
        compiler_params=pltpu.CompilerParams(vmem_limit_bytes=VMEM_BYTES),
        name="local_sums",
    )(*inputs)
    mine = parts[0] + swap(parts[1], n_exp, n_imp, 1, 0)
    for bit in powers(2, n_exp):
        mine = mine + swap(mine, n_exp, n_imp, bit | 1, 0)
    for bit in powers(1, n_imp):
        mine = mine + swap(mine, n_exp, n_imp, 1, 2 * bit - 1)
    shares = (mine, swap(mine, n_exp, n_imp, 1, 0))
    high = 16
    a, b, g = pl.pallas_call(
        functools.partial(solve_kernel, lay),
        out_shape=(
            jax.ShapeDtypeStruct((rows,), f32),
            jax.ShapeDtypeStruct((cols,), f32),
            jax.ShapeDtypeStruct((NCE, NCI), f32),
        ),
        in_specs=[vmem] * 2,
        out_specs=(vmem, vmem, vmem),
        scratch_shapes=[
            pltpu.VMEM((2 * lay.share, LANES), f32),
            pltpu.VMEM((lay.na, LANES), bf16),
            pltpu.VMEM((lay.nb, LANES), bf16),
            pltpu.VMEM((high * lay.na // LANES, LANES), f32),
            pltpu.VMEM((high * lay.nb // LANES, LANES), f32),
            pltpu.VMEM((lay.na // LANES, LANES), f32),
            pltpu.VMEM((lay.nb // LANES, LANES), f32),
            pltpu.VMEM((8, LANES), f32),
        ],
        compiler_params=pltpu.CompilerParams(vmem_limit_bytes=VMEM_BYTES),
        name="solve",
    )(*shares)
    return a, b, g


def solution(mesh):
    placed = (
        P(("exp", "imp"), None, None),
        P(("exp", "imp"), None, None),
        P(("exp", "imp")),
        P("exp"),
        P("imp"),
    )
    return jax.shard_map(
        functools.partial(per_device, (mesh.shape["exp"], mesh.shape["imp"])),
        mesh=mesh,
        in_specs=placed,
        out_specs=(P("exp"), P("imp"), P()),
        check_vma=False,
    )
```

```python
import functools

import jax
import jax.numpy as jnp
from jax import lax
from jax.experimental import pallas as pl
from jax.experimental.pallas import tpu as pltpu
from jax.sharding import PartitionSpec as P

NCE = 128
NCI = 128
NEWTON = 2
CG = 2
LANES = 128
RIDGE = 64.0
VMEM_BYTES = 48 * 1024 * 1024

f32 = jnp.float32
bf16 = jnp.bfloat16
i32 = jnp.int32


def iota(shape, dim):
    return lax.broadcasted_iota(i32, shape, dim)


def split(x):
    hi = x.astype(bf16).astype(f32)
    rest = x - hi
    mid = rest.astype(bf16).astype(f32)
    return hi, mid, rest - mid


def dot(x, y, cx, cy, precision=None):
    return lax.dot_general(
        x, y, (((cx,), (cy,)), ((), ())), precision=precision, preferred_element_type=f32
    )


class Layout:
    def __init__(self, na, nb, side):
        self.na, self.nb, self.side = na, nb, side
        self.rows_at = NCE
        self.cols_at = self.rows_at + na // LANES
        self.cnt_at = self.cols_at + nb // LANES
        self.live_at = self.cnt_at + 2
        self.blocks_a, self.blocks_b = na // side, nb // side
        self.total = -(-(self.live_at - (-self.blocks_a * self.blocks_b // LANES)) // 8) * 8
        self.share = -(-self.total // 16) * 8


def half_of(exp_place, imp_place):
    bits = exp_place ^ imp_place
    for shift in (8, 4, 2, 1):
        bits = bits ^ (bits >> shift)
    return bits & 1


def local_kernel(lay, slots, *refs):
    sources, outs, out, homes, sems = refs[:5], refs[5:7], refs[7], refs[8:13], refs[13]
    small = [pltpu.make_async_copy(sources[j], homes[j], sems.at[j]) for j in range(1, 5)]
    tiles = [
        pltpu.make_async_copy(sources[0].at[k], homes[0].at[k], sems.at[5 + k]) for k in range(slots)
    ]
    for copy in small + tiles:
        copy.start()
    flows, routing, tile_block, ec, ic = homes
    exp_place, imp_place = lax.axis_index("exp"), lax.axis_index("imp")
    side = lay.side
    row_blocks = ec.shape[0]
    col_local = ic.shape[0]
    out[...] = jnp.zeros_like(out)
    per = side // LANES
    country = iota((NCE, side), 0)
    ones = jnp.ones((8, side), bf16)
    for copy in small:
        copy.wait()
    cnt_a = jnp.zeros((8, LANES), f32)
    for r in range(row_blocks):
        cnt_a += dot(ones, (country == ec[r]).astype(f32).astype(bf16), 1, 1)
    cnt_b = jnp.zeros((8, LANES), f32)
    for c in range(col_local):
        cnt_b += dot(ones, (country == ic[c]).astype(f32).astype(bf16), 1, 1)
    cnt_a = cnt_a[0:1] * (imp_place == 0).astype(f32)
    cnt_b = cnt_b[0:1] * (exp_place == 0).astype(f32)
    out[lay.cnt_at : lay.cnt_at + 1, :] = cnt_a
    out[lay.cnt_at + 1 : lay.cnt_at + 2, :] = cnt_b
    pairs = jnp.zeros((NCE, NCI), f32)
    for k in range(slots):
        r = tile_block[k] // col_local
        c = tile_block[k] % col_local
        live = routing[0] == k
        for t in range(1, routing.shape[0]):
            live = live | (routing[t] == k)
        keep = live.astype(f32)
        hot_r = (country == ec[r]).astype(f32).astype(bf16)
        hot_c = (country == ic[c]).astype(f32).astype(bf16)
        tiles[k].wait()
        tile = flows[k] * keep.astype(bf16)
        half = dot(hot_r, tile, 1, 0)
        col_sum = jnp.sum(half, axis=0, keepdims=True)
        row_sum = dot(ones, tile, 1, 1)[0:1]
        top = half.astype(bf16)
        rest = (half - top.astype(f32)).astype(bf16)
        both = dot(jnp.concatenate([top, rest], axis=0), hot_c, 1, 1)
        pairs = pairs + (both[:NCE] + both[NCE:])
        row_at = lay.rows_at + (exp_place * row_blocks + r) * per
        col_at = lay.cols_at + (imp_place * col_local + c) * per
        for h in range(per):
            cut = slice(h * LANES, (h + 1) * LANES)
            out[pl.ds(row_at + h, 1), :] += row_sum[:, cut]
            out[pl.ds(col_at + h, 1), :] += col_sum[:, cut]
        flat = (exp_place * row_blocks + r) * lay.blocks_b + imp_place * col_local + c
        here = iota((1, LANES), 1) == flat % LANES
        out[pl.ds(lay.live_at + flat // LANES, 1), :] += jnp.where(here, keep, 0.0)
    out[0:NCE, :] = pairs
    mine = half_of(exp_place, imp_place)
    for k, part in enumerate(outs):
        part[...] = out[pl.ds(pl.multiple_of((mine ^ k) * lay.share, 8), lay.share), :]


def lookup(row, index):
    return jnp.take_along_axis(
        jnp.broadcast_to(row, index.shape), index, axis=1, mode="promise_in_bounds"
    )


def down(row):
    return jnp.transpose(jnp.broadcast_to(row, (LANES, LANES)))


def across(x):
    return jnp.sum(jnp.transpose(x), axis=0, keepdims=True)


def below(x):
    return jnp.sum(x, axis=0, keepdims=True)


def eights(x):
    return functools.reduce(lambda u, v: u + v, [x[j : j + 8] for j in range(0, x.shape[0], 8)])


def inner(u, v):
    partial = eights(u[0] * v[0]) + eights(u[1] * v[1]) + eights(u[2] * v[2])
    return jnp.sum(below(partial), axis=1, keepdims=True)


class Side:
    def __init__(self, n, block, start, middle, end, hot, stage):
        self.n, self.block, self.hot, self.stage = n, block, hot, stage
        self.chunks = n // LANES
        shape = (self.chunks, LANES)
        place = (iota(shape, 0) * LANES + iota(shape, 1)).astype(f32)
        country = jnp.zeros(shape, i32)
        jump = LANES // 2
        while jump:
            passed = lookup(end, country + (jump - 1)) <= place
            country = jnp.where(passed, country + jump, country)
            jump //= 2
        self.country = country
        self.second = place >= lookup(middle, country)
        at = iota((block, LANES), 0).astype(f32).astype(bf16)
        one, none = jnp.ones((block, LANES), bf16), jnp.zeros((block, LANES), bf16)
        for j in range(n // block):
            lo, hi = (jnp.clip(x - j * block, 0.0, block).astype(bf16) for x in (start, end))
            inside = (at >= lo) & (at < hi)
            hot[j * block : (j + 1) * block, :] = jnp.where(inside, one, none)

    def expand(self, first, second):
        return jnp.where(self.second, lookup(second, self.country), lookup(first, self.country))

    def sums(self, vectors):
        chunks, stage = self.chunks, self.stage
        for k, v in enumerate(vectors):
            stage[2 * k * chunks : (2 * k + 1) * chunks, :] = jnp.where(self.second, 0.0, v)
            stage[(2 * k + 1) * chunks : (2 * k + 2) * chunks, :] = jnp.where(self.second, v, 0.0)
        high = -(-2 * len(vectors) // 8) * 8
        for k in range(2 * len(vectors), high):
            stage[k * chunks : (k + 1) * chunks, :] = jnp.zeros((chunks, LANES), f32)
        got = jnp.zeros((3 * high, LANES), f32)
        per = self.block // LANES
        for j in range(chunks // per):
            left = jnp.concatenate(
                [stage[pl.ds(j * per + h, high, stride=chunks), :] for h in range(per)], axis=1
            )
            pieces = jnp.concatenate(split(left), axis=0).astype(bf16)
            got += dot(pieces, self.hot[j * self.block : (j + 1) * self.block, :], 1, 0)
        return got[:high] + got[high : 2 * high] + got[2 * high :]

    def maxima(self, values_ref, low, high):
        low, high = down(low), down(high)

        def body(j, best):
            at = (iota((LANES, LANES), 1) + j * LANES).astype(f32)
            inside = (at >= low) & (at < high)
            return jnp.maximum(best, jnp.where(inside, values_ref[pl.ds(j, 1), :], -jnp.inf))

        best = lax.fori_loop(0, self.chunks, body, jnp.full((LANES, LANES), -jnp.inf, f32))
        best = jnp.max(jnp.transpose(best), axis=0, keepdims=True)
        return jnp.where(best > -jnp.inf, best, 0.0)


def solve_kernel(lay, *refs):
    where = lax.axis_index("exp"), lax.axis_index("imp")
    shares, refs = refs[:2], refs[2:]
    out_a, out_b, out_g, shared, hot_a, hot_b, stage_a, stage_b, val_a, val_b, shift_ref = refs
    mine = half_of(*where)
    for k, part in enumerate(shares):
        shared[pl.ds(pl.multiple_of((mine ^ k) * lay.share, 8), lay.share), :] = part[...]
    flow = (
        shared[lay.rows_at : lay.cols_at, :],
        shared[lay.cols_at : lay.cnt_at, :],
        shared[0:NCE, :],
    )
    side = lay.side
    tally = shared[lay.cnt_at : lay.cnt_at + 8, :]
    before = jnp.where(iota((LANES, LANES), 0) < iota((LANES, LANES), 1), 1.0, 0.0).astype(bf16)
    start = dot(tally.astype(bf16), before, 1, 0)
    end = start + tally
    first = jnp.floor((start + 0.5) * (1.0 / side))
    middle = jnp.minimum(end, (first + 1.0) * side)

    def table(x, y):
        return jnp.concatenate([x[0:1], y[0:1], x[1:2], y[1:2]], axis=0)

    low, high = table(start, middle), table(middle, end)
    count = high - low
    full = count > 0.5
    inv_count = jnp.where(full, 1.0 / jnp.maximum(count, 1.0), 0.0)
    block_of = jnp.where(full, table(first, first + 1.0), -1.0)
    sa = Side(lay.na, side, start[0:1], middle[0:1], end[0:1], hot_a, stage_a)
    sb = Side(lay.nb, side, start[1:2], middle[1:2], end[1:2], hot_b, stage_b)

    wide = lay.blocks_b
    spots = [(r * wide // LANES, r * wide % LANES) for r in range(lay.blocks_a)]
    live = jnp.concatenate(
        [shared[lay.live_at + row : lay.live_at + row + 1, at : at + wide] for row, at in spots], axis=0
    ).astype(bf16)
    number = iota((LANES, LANES), 1).astype(f32)
    pick_a = [jnp.where(down(block_of[p : p + 1]) == number, 1.0, 0.0).astype(bf16) for p in (0, 1)]
    number = iota((LANES, LANES), 0).astype(f32)
    pick_b = [jnp.where(block_of[q : q + 1] == number, 1.0, 0.0).astype(bf16) for q in (2, 3)]
    reach = [dot(pick[:, : lay.blocks_a], live, 1, 0).astype(bf16) for pick in pick_a]
    mask = [[dot(reach[p], pick_b[q][: lay.blocks_b], 1, 0) for q in (0, 1)] for p in (0, 1)]

    a = jnp.zeros((lay.na // LANES, LANES), f32)
    b = jnp.zeros((lay.nb // LANES, LANES), f32)
    g = jnp.zeros((NCE, NCI), f32)
    mean = jnp.zeros((4, LANES), f32)
    for newton in range(NEWTON):
        if newton == 0:
            left = flow
            weight, inv, rate = count, inv_count, mask
            sum_a, sum_b = sa.sums([flow[0]]), sb.sums([flow[1]])
            part_a, part_b = sa.expand(inv[0:1], inv[1:2]), sb.expand(inv[2:3], inv[3:4])
            m2, m3 = inv, inv * inv
            f1 = jnp.concatenate([sum_a[0:2], sum_b[0:2]], axis=0) * inv
            f2 = f1 * inv
        else:
            left = (flow[0] - RIDGE * a, flow[1] - RIDGE * b, flow[2] - RIDGE * g)
            shift_ref[0:4, :] = mean
            off_a = a - sa.expand(mean[0:1], mean[1:2])
            off_b = b - sb.expand(mean[2:3], mean[3:4])
            worst = jnp.maximum(jnp.max(off_a), jnp.max(off_b))
            val_a[...] = a
            val_b[...] = b

            @pl.when(worst > 20.0)
            def _():
                shift_ref[0:1, :] = sa.maxima(val_a, low[0:1], high[0:1])
                shift_ref[1:2, :] = sa.maxima(val_a, low[1:2], high[1:2])
                shift_ref[2:3, :] = sb.maxima(val_b, low[2:3], high[2:3])
                shift_ref[3:4, :] = sb.maxima(val_b, low[3:4], high[3:4])

            shift = shift_ref[0:4, :]
            size_a = jnp.exp(a - sa.expand(shift[0:1], shift[1:2]))
            size_b = jnp.exp(b - sb.expand(shift[2:3], shift[3:4]))

            def moments(s, x, f):
                return s.sums([x, x * x, x * x * x, x * f, x * x * f])

            sum_a, sum_b = moments(sa, size_a, left[0]), moments(sb, size_b, left[1])
            got = [jnp.concatenate([sum_a[2 * k : 2 * k + 2], sum_b[2 * k : 2 * k + 2]], axis=0) for k in range(5)]
            weight = got[0]
            inv = jnp.where(full, 1.0 / jnp.where(full, weight, 1.0), 0.0)
            part_a = size_a * sa.expand(inv[0:1], inv[1:2])
            part_b = size_b * sb.expand(inv[2:3], inv[3:4])
            inv2 = inv * inv
            m2, m3 = got[1] * inv2, got[2] * (inv2 * inv)
            f1, f2 = got[3] * inv, got[4] * inv2
            lift = [g + down(shift[p : p + 1]) for p in (0, 1)]
            rate = [
                [jnp.where(mask[p][q] > 0.5, jnp.exp(lift[p] + shift[2 + q : 3 + q]), 0.0) for q in (0, 1)]
                for p in (0, 1)
            ]
        tall = [down(weight[p : p + 1]) for p in (0, 1)]
        mu = [[rate[p][q] * (tall[p] * weight[2 + q : 3 + q]) for q in (0, 1)] for p in (0, 1)]
        mu_a = [mu[p][0] + mu[p][1] for p in (0, 1)]
        mu_b = [mu[0][q] + mu[1][q] for q in (0, 1)]
        whole = jnp.concatenate([across(mu_a[0]), across(mu_a[1]), below(mu_b[0]), below(mu_b[1])], axis=0)
        da = part_a * sa.expand(whole[0:1], whole[1:2])
        db = part_b * sb.expand(whole[2:3], whole[3:4])
        res = (left[0] - da, left[1] - db, left[2] - (mu_a[0] + mu_a[1]))
        way = res
        norm = inner(res, res)
        v = f1 - whole * m2
        w = f2 - whole * m3
        for sweep in range(CG):
            tall = [down(v[p : p + 1]) for p in (0, 1)]
            flat = [v[2 + q : 3 + q] for q in (0, 1)]
            ga = [mu[p][0] * flat[0] + mu[p][1] * flat[1] + way[2] * mu_a[p] for p in (0, 1)]
            gb = [mu[0][q] * tall[0] + mu[1][q] * tall[1] + way[2] * mu_b[q] for q in (0, 1)]
            u = jnp.concatenate([across(ga[0]), across(ga[1]), below(gb[0]), below(gb[1])], axis=0)
            image = (
                (da + RIDGE) * way[0] + part_a * sa.expand(u[0:1], u[1:2]),
                (db + RIDGE) * way[1] + part_b * sb.expand(u[2:3], u[3:4]),
                RIDGE * way[2] + (ga[0] + ga[1]) + (tall[0] * mu_a[0] + tall[1] * mu_a[1]),
            )
            step = norm / inner(way, image)
            a, b, g = a + step * way[0], b + step * way[1], g + step * way[2]
            if newton + 1 < NEWTON:
                mean = mean + step * v
            if sweep + 1 < CG:
                res = tuple(x - step * y for x, y in zip(res, image))
                fresh = inner(res, res)
                ratio = fresh / norm
                way = tuple(x + ratio * y for x, y in zip(res, way))
                norm = fresh
                v = v - step * (whole * w + RIDGE * v + u * m2) + ratio * v
    out_g[...] = g
    val_a[...] = a
    val_b[...] = b
    for out, val, at in ((out_a, val_a, where[0]), (out_b, val_b, where[1])):
        rows = out.shape[0] // LANES
        for j in range(rows):
            out[j * LANES : (j + 1) * LANES] = val[pl.ds(at * rows + j, 1), :].reshape(LANES)


def powers(first, limit):
    return [1 << k for k in range(16) if first <= 1 << k < limit]


def swap(x, n_exp, n_imp, exp_bits, imp_bits):
    pairs = [
        (e * n_imp + m, (e ^ exp_bits) * n_imp + (m ^ imp_bits)) for e in range(n_exp) for m in range(n_imp)
    ]
    return lax.ppermute(x, ("exp", "imp"), pairs)


def per_device(mesh_shape, flows, routing, tile_block, exp_country, imp_country):
    slots, side = flows.shape[0], flows.shape[1]
    n_exp, n_imp = mesh_shape
    rows, cols = exp_country.shape[0], imp_country.shape[0]
    lay = Layout(rows * n_exp, cols * n_imp, side)
    vmem = pl.BlockSpec(memory_space=pltpu.VMEM)
    inputs = (
        flows,
        routing.reshape(-1),
        tile_block,
        exp_country.reshape(-1, 1, side),
        imp_country.reshape(-1, 1, side),
    )
    inputs = tuple(pltpu.with_memory_space_constraint(x, pltpu.HBM) for x in inputs)
    homes = [pltpu.VMEM, pltpu.SMEM, pltpu.SMEM, pltpu.VMEM, pltpu.VMEM]
    parts = pl.pallas_call(
        functools.partial(local_kernel, lay, slots),
        out_shape=[jax.ShapeDtypeStruct((lay.share, LANES), f32)] * 2,
        in_specs=[pl.BlockSpec(memory_space=pltpu.HBM)] * 5,
        out_specs=[vmem] * 2,
        scratch_shapes=[pltpu.VMEM((2 * lay.share, LANES), f32)]
        + [space(x.shape, x.dtype) for space, x in zip(homes, inputs)]
        + [pltpu.SemaphoreType.DMA((5 + slots,))],
        compiler_params=pltpu.CompilerParams(vmem_limit_bytes=VMEM_BYTES),
        name="local_sums",
    )(*inputs)
    mine = parts[0] + swap(parts[1], n_exp, n_imp, 1, 0)
    for bit in powers(2, n_exp):
        mine = mine + swap(mine, n_exp, n_imp, bit | 1, 0)
    for bit in powers(1, n_imp):
        mine = mine + swap(mine, n_exp, n_imp, 1, bit)
    shares = (mine, swap(mine, n_exp, n_imp, 1, 0))
    high = 16
    a, b, g = pl.pallas_call(
        functools.partial(solve_kernel, lay),
        out_shape=(
            jax.ShapeDtypeStruct((rows,), f32),
            jax.ShapeDtypeStruct((cols,), f32),
            jax.ShapeDtypeStruct((NCE, NCI), f32),
        ),
        in_specs=[vmem] * 2,
        out_specs=(vmem, vmem, vmem),
        scratch_shapes=[
            pltpu.VMEM((2 * lay.share, LANES), f32),
            pltpu.VMEM((lay.na, LANES), bf16),
            pltpu.VMEM((lay.nb, LANES), bf16),
            pltpu.VMEM((high * lay.na // LANES, LANES), f32),
            pltpu.VMEM((high * lay.nb // LANES, LANES), f32),
            pltpu.VMEM((lay.na // LANES, LANES), f32),
            pltpu.VMEM((lay.nb // LANES, LANES), f32),
            pltpu.VMEM((8, LANES), f32),
        ],
        compiler_params=pltpu.CompilerParams(vmem_limit_bytes=VMEM_BYTES),
        name="solve",
    )(*shares)
    return a, b, g


def solution(mesh):
    placed = (
        P(("exp", "imp"), None, None),
        P(("exp", "imp"), None, None),
        P(("exp", "imp")),
        P("exp"),
        P("imp"),
    )
    return jax.shard_map(
        functools.partial(per_device, (mesh.shape["exp"], mesh.shape["imp"])),
        mesh=mesh,
        in_specs=placed,
        out_specs=(P("exp"), P("imp"), P()),
        check_vma=False,
    )
```

```python
import functools

import jax
import jax.numpy as jnp
from jax import lax
from jax.experimental import pallas as pl
from jax.experimental.pallas import tpu as pltpu
from jax.sharding import PartitionSpec as P

NCE = 128
NCI = 128
NEWTON = 2
CG = 2
LANES = 128
RIDGE = 64.0
VMEM_BYTES = 48 * 1024 * 1024

f32 = jnp.float32
bf16 = jnp.bfloat16
i32 = jnp.int32


def iota(shape, dim):
    return lax.broadcasted_iota(i32, shape, dim)


def split(x):
    hi = x.astype(bf16).astype(f32)
    rest = x - hi
    mid = rest.astype(bf16).astype(f32)
    return hi, mid, rest - mid


def dot(x, y, cx, cy, precision=None):
    return lax.dot_general(
        x, y, (((cx,), (cy,)), ((), ())), precision=precision, preferred_element_type=f32
    )


class Layout:
    def __init__(self, na, nb, side):
        self.na, self.nb, self.side = na, nb, side
        self.rows_at = NCE
        self.cols_at = self.rows_at + na // LANES
        self.cnt_at = self.cols_at + nb // LANES
        self.live_at = self.cnt_at + 2
        self.blocks_a, self.blocks_b = na // side, nb // side
        self.total = -(-(self.live_at - (-self.blocks_a * self.blocks_b // LANES)) // 8) * 8
        self.share = -(-self.total // 16) * 8


def half_of(exp_place, imp_place):
    bits = exp_place ^ imp_place
    for shift in (8, 4, 2, 1):
        bits = bits ^ (bits >> shift)
    return bits & 1


def local_kernel(lay, slots, *refs):
    sources, outs, out, homes, sems = refs[:5], refs[5:7], refs[7], refs[8:13], refs[13]
    small = [pltpu.make_async_copy(sources[j], homes[j], sems.at[j]) for j in range(1, 5)]
    tiles = [
        pltpu.make_async_copy(sources[0].at[k], homes[0].at[k], sems.at[5 + k]) for k in range(slots)
    ]
    for copy in small + tiles:
        copy.start()
    flows, routing, tile_block, ec, ic = homes
    exp_place, imp_place = lax.axis_index("exp"), lax.axis_index("imp")
    side = lay.side
    row_blocks = ec.shape[0]
    col_local = ic.shape[0]
    out[...] = jnp.zeros_like(out)
    per = side // LANES
    country = iota((NCE, side), 0)
    ones = jnp.ones((8, side), bf16)
    for copy in small:
        copy.wait()
    cnt_a = jnp.zeros((8, LANES), f32)
    for r in range(row_blocks):
        cnt_a += dot(ones, (country == ec[r]).astype(f32).astype(bf16), 1, 1)
    cnt_b = jnp.zeros((8, LANES), f32)
    for c in range(col_local):
        cnt_b += dot(ones, (country == ic[c]).astype(f32).astype(bf16), 1, 1)
    cnt_a = cnt_a[0:1] * (imp_place == 0).astype(f32)
    cnt_b = cnt_b[0:1] * (exp_place == 0).astype(f32)
    out[lay.cnt_at : lay.cnt_at + 1, :] = cnt_a
    out[lay.cnt_at + 1 : lay.cnt_at + 2, :] = cnt_b
    pairs = jnp.zeros((NCE, NCI), f32)
    for k in range(slots):
        r = tile_block[k] // col_local
        c = tile_block[k] % col_local
        live = routing[0] == k
        for t in range(1, routing.shape[0]):
            live = live | (routing[t] == k)
        keep = live.astype(f32)
        hot_r = (country == ec[r]).astype(f32).astype(bf16)
        hot_c = (country == ic[c]).astype(f32).astype(bf16)
        tiles[k].wait()
        tile = flows[k] * keep.astype(bf16)
        half = dot(hot_r, tile, 1, 0)
        col_sum = jnp.sum(half, axis=0, keepdims=True)
        row_sum = dot(ones, tile, 1, 1)[0:1]
        top = half.astype(bf16)
        rest = (half - top.astype(f32)).astype(bf16)
        both = dot(jnp.concatenate([top, rest], axis=0), hot_c, 1, 1)
        pairs = pairs + (both[:NCE] + both[NCE:])
        row_at = lay.rows_at + (exp_place * row_blocks + r) * per
        col_at = lay.cols_at + (imp_place * col_local + c) * per
        for h in range(per):
            cut = slice(h * LANES, (h + 1) * LANES)
            out[pl.ds(row_at + h, 1), :] += row_sum[:, cut]
            out[pl.ds(col_at + h, 1), :] += col_sum[:, cut]
        flat = (exp_place * row_blocks + r) * lay.blocks_b + imp_place * col_local + c
        here = iota((1, LANES), 1) == flat % LANES
        out[pl.ds(lay.live_at + flat // LANES, 1), :] += jnp.where(here, keep, 0.0)
    out[0:NCE, :] = pairs
    mine = half_of(exp_place, imp_place)
    for k, part in enumerate(outs):
        part[...] = out[pl.ds(pl.multiple_of((mine ^ k) * lay.share, 8), lay.share), :]


def lookup(row, index):
    return jnp.take_along_axis(
        jnp.broadcast_to(row, index.shape), index, axis=1, mode="promise_in_bounds"
    )


def down(row):
    return jnp.transpose(jnp.broadcast_to(row, (LANES, LANES)))


def across(x):
    return jnp.sum(jnp.transpose(x), axis=0, keepdims=True)


def below(x):
    return jnp.sum(x, axis=0, keepdims=True)


def eights(x):
    return functools.reduce(lambda u, v: u + v, [x[j : j + 8] for j in range(0, x.shape[0], 8)])


def inner(u, v):
    partial = eights(u[0] * v[0]) + eights(u[1] * v[1]) + eights(u[2] * v[2])
    return jnp.sum(below(partial), axis=1, keepdims=True)


class Side:
    def __init__(self, n, block, start, middle, end, hot, stage):
        self.n, self.block, self.hot, self.stage = n, block, hot, stage
        self.chunks = n // LANES
        shape = (self.chunks, LANES)
        place = (iota(shape, 0) * LANES + iota(shape, 1)).astype(f32)
        country = jnp.zeros(shape, i32)
        jump = LANES // 2
        while jump:
            passed = lookup(end, country + (jump - 1)) <= place
            country = jnp.where(passed, country + jump, country)
            jump //= 2
        self.country = country
        self.second = place >= lookup(middle, country)
        at = iota((block, LANES), 0).astype(f32).astype(bf16)
        one, none = jnp.ones((block, LANES), bf16), jnp.zeros((block, LANES), bf16)
        for j in range(n // block):
            lo, hi = (jnp.clip(x - j * block, 0.0, block).astype(bf16) for x in (start, end))
            inside = (at >= lo) & (at < hi)
            hot[j * block : (j + 1) * block, :] = jnp.where(inside, one, none)

    def expand(self, first, second):
        return jnp.where(self.second, lookup(second, self.country), lookup(first, self.country))

    def sums(self, vectors):
        chunks, stage = self.chunks, self.stage
        for k, v in enumerate(vectors):
            stage[2 * k * chunks : (2 * k + 1) * chunks, :] = jnp.where(self.second, 0.0, v)
            stage[(2 * k + 1) * chunks : (2 * k + 2) * chunks, :] = jnp.where(self.second, v, 0.0)
        high = -(-2 * len(vectors) // 8) * 8
        for k in range(2 * len(vectors), high):
            stage[k * chunks : (k + 1) * chunks, :] = jnp.zeros((chunks, LANES), f32)
        got = jnp.zeros((3 * high, LANES), f32)
        per = self.block // LANES
        for j in range(chunks // per):
            left = jnp.concatenate(
                [stage[pl.ds(j * per + h, high, stride=chunks), :] for h in range(per)], axis=1
            )
            pieces = jnp.concatenate(split(left), axis=0).astype(bf16)
            got += dot(pieces, self.hot[j * self.block : (j + 1) * self.block, :], 1, 0)
        return got[:high] + got[high : 2 * high] + got[2 * high :]

    def maxima(self, values_ref, low, high):
        low, high = down(low), down(high)

        def body(j, best):
            at = (iota((LANES, LANES), 1) + j * LANES).astype(f32)
            inside = (at >= low) & (at < high)
            return jnp.maximum(best, jnp.where(inside, values_ref[pl.ds(j, 1), :], -jnp.inf))

        best = lax.fori_loop(0, self.chunks, body, jnp.full((LANES, LANES), -jnp.inf, f32))
        best = jnp.max(jnp.transpose(best), axis=0, keepdims=True)
        return jnp.where(best > -jnp.inf, best, 0.0)


def solve_kernel(lay, *refs):
    where = lax.axis_index("exp"), lax.axis_index("imp")
    shares, refs = refs[:2], refs[2:]
    out_a, out_b, out_g, shared, hot_a, hot_b, stage_a, stage_b, val_a, val_b, shift_ref = refs
    mine = half_of(*where)
    for k, part in enumerate(shares):
        shared[pl.ds(pl.multiple_of((mine ^ k) * lay.share, 8), lay.share), :] = part[...]
    flow = (
        shared[lay.rows_at : lay.cols_at, :],
        shared[lay.cols_at : lay.cnt_at, :],
        shared[0:NCE, :],
    )
    side = lay.side
    tally = shared[lay.cnt_at : lay.cnt_at + 8, :]
    before = jnp.where(iota((LANES, LANES), 0) < iota((LANES, LANES), 1), 1.0, 0.0).astype(bf16)
    start = dot(tally.astype(bf16), before, 1, 0)
    end = start + tally
    first = jnp.floor((start + 0.5) * (1.0 / side))
    middle = jnp.minimum(end, (first + 1.0) * side)

    def table(x, y):
        return jnp.concatenate([x[0:1], y[0:1], x[1:2], y[1:2]], axis=0)

    low, high = table(start, middle), table(middle, end)
    count = high - low
    full = count > 0.5
    inv_count = jnp.where(full, 1.0 / jnp.maximum(count, 1.0), 0.0)
    block_of = jnp.where(full, table(first, first + 1.0), -1.0)
    sa = Side(lay.na, side, start[0:1], middle[0:1], end[0:1], hot_a, stage_a)
    sb = Side(lay.nb, side, start[1:2], middle[1:2], end[1:2], hot_b, stage_b)

    wide = lay.blocks_b
    spots = [(r * wide // LANES, r * wide % LANES) for r in range(lay.blocks_a)]
    live = jnp.concatenate(
        [shared[lay.live_at + row : lay.live_at + row + 1, at : at + wide] for row, at in spots], axis=0
    ).astype(bf16)
    number = iota((LANES, LANES), 1).astype(f32)
    pick_a = [jnp.where(down(block_of[p : p + 1]) == number, 1.0, 0.0).astype(bf16) for p in (0, 1)]
    number = iota((LANES, LANES), 0).astype(f32)
    pick_b = [jnp.where(block_of[q : q + 1] == number, 1.0, 0.0).astype(bf16) for q in (2, 3)]
    reach = [dot(pick[:, : lay.blocks_a], live, 1, 0).astype(bf16) for pick in pick_a]
    mask = [[dot(reach[p], pick_b[q][: lay.blocks_b], 1, 0) for q in (0, 1)] for p in (0, 1)]

    a = jnp.zeros((lay.na // LANES, LANES), f32)
    b = jnp.zeros((lay.nb // LANES, LANES), f32)
    g = jnp.zeros((NCE, NCI), f32)
    mean = jnp.zeros((4, LANES), f32)
    for newton in range(NEWTON):
        if newton == 0:
            left = flow
            weight, inv, rate = count, inv_count, mask
            sum_a, sum_b = sa.sums([flow[0]]), sb.sums([flow[1]])
            part_a, part_b = sa.expand(inv[0:1], inv[1:2]), sb.expand(inv[2:3], inv[3:4])
            m2, m3 = inv, inv * inv
            f1 = jnp.concatenate([sum_a[0:2], sum_b[0:2]], axis=0) * inv
            f2 = f1 * inv
        else:
            left = (flow[0] - RIDGE * a, flow[1] - RIDGE * b, flow[2] - RIDGE * g)
            shift_ref[0:4, :] = mean
            off_a = a - sa.expand(mean[0:1], mean[1:2])
            off_b = b - sb.expand(mean[2:3], mean[3:4])
            worst = jnp.maximum(jnp.max(off_a), jnp.max(off_b))
            val_a[...] = a
            val_b[...] = b

            @pl.when(worst > 20.0)
            def _():
                shift_ref[0:1, :] = sa.maxima(val_a, low[0:1], high[0:1])
                shift_ref[1:2, :] = sa.maxima(val_a, low[1:2], high[1:2])
                shift_ref[2:3, :] = sb.maxima(val_b, low[2:3], high[2:3])
                shift_ref[3:4, :] = sb.maxima(val_b, low[3:4], high[3:4])

            shift = shift_ref[0:4, :]
            size_a = jnp.exp(a - sa.expand(shift[0:1], shift[1:2]))
            size_b = jnp.exp(b - sb.expand(shift[2:3], shift[3:4]))

            def moments(s, x, f):
                return s.sums([x, x * x, x * x * x, x * f, x * x * f])

            sum_a, sum_b = moments(sa, size_a, left[0]), moments(sb, size_b, left[1])
            got = [jnp.concatenate([sum_a[2 * k : 2 * k + 2], sum_b[2 * k : 2 * k + 2]], axis=0) for k in range(5)]
            weight = got[0]
            inv = jnp.where(full, 1.0 / jnp.where(full, weight, 1.0), 0.0)
            part_a = size_a * sa.expand(inv[0:1], inv[1:2])
            part_b = size_b * sb.expand(inv[2:3], inv[3:4])
            inv2 = inv * inv
            m2, m3 = got[1] * inv2, got[2] * (inv2 * inv)
            f1, f2 = got[3] * inv, got[4] * inv2
            lift = [g + down(shift[p : p + 1]) for p in (0, 1)]
            rate = [
                [jnp.where(mask[p][q] > 0.5, jnp.exp(lift[p] + shift[2 + q : 3 + q]), 0.0) for q in (0, 1)]
                for p in (0, 1)
            ]
        tall = [down(weight[p : p + 1]) for p in (0, 1)]
        mu = [[rate[p][q] * (tall[p] * weight[2 + q : 3 + q]) for q in (0, 1)] for p in (0, 1)]
        mu_a = [mu[p][0] + mu[p][1] for p in (0, 1)]
        mu_b = [mu[0][q] + mu[1][q] for q in (0, 1)]
        whole = jnp.concatenate([across(mu_a[0]), across(mu_a[1]), below(mu_b[0]), below(mu_b[1])], axis=0)
        da = part_a * sa.expand(whole[0:1], whole[1:2])
        db = part_b * sb.expand(whole[2:3], whole[3:4])
        res = (left[0] - da, left[1] - db, left[2] - (mu_a[0] + mu_a[1]))
        way = res
        norm = inner(res, res)
        v = f1 - whole * m2
        w = f2 - whole * m3
        for sweep in range(CG):
            tall = [down(v[p : p + 1]) for p in (0, 1)]
            flat = [v[2 + q : 3 + q] for q in (0, 1)]
            ga = [mu[p][0] * flat[0] + mu[p][1] * flat[1] + way[2] * mu_a[p] for p in (0, 1)]
            gb = [mu[0][q] * tall[0] + mu[1][q] * tall[1] + way[2] * mu_b[q] for q in (0, 1)]
            u = jnp.concatenate([across(ga[0]), across(ga[1]), below(gb[0]), below(gb[1])], axis=0)
            image = (
                (da + RIDGE) * way[0] + part_a * sa.expand(u[0:1], u[1:2]),
                (db + RIDGE) * way[1] + part_b * sb.expand(u[2:3], u[3:4]),
                RIDGE * way[2] + (ga[0] + ga[1]) + (tall[0] * mu_a[0] + tall[1] * mu_a[1]),
            )
            step = norm / inner(way, image)
            a, b, g = a + step * way[0], b + step * way[1], g + step * way[2]
            if newton + 1 < NEWTON:
                mean = mean + step * v
            if sweep + 1 < CG:
                res = tuple(x - step * y for x, y in zip(res, image))
                fresh = inner(res, res)
                ratio = fresh / norm
                way = tuple(x + ratio * y for x, y in zip(res, way))
                norm = fresh
                v = v - step * (whole * w + RIDGE * v + u * m2) + ratio * v
    out_g[...] = g
    val_a[...] = a
    val_b[...] = b
    for out, val, at in ((out_a, val_a, where[0]), (out_b, val_b, where[1])):
        rows = out.shape[0] // LANES
        for j in range(rows):
            out[j * LANES : (j + 1) * LANES] = val[pl.ds(at * rows + j, 1), :].reshape(LANES)


def powers(first, limit):
    return [1 << k for k in range(16) if first <= 1 << k < limit]


def swap(x, n_exp, n_imp, exp_bits, imp_bits):
    pairs = [
        (e * n_imp + m, (e ^ exp_bits) * n_imp + (m ^ imp_bits)) for e in range(n_exp) for m in range(n_imp)
    ]
    return lax.ppermute(x, ("exp", "imp"), pairs)


def per_device(mesh_shape, flows, routing, tile_block, exp_country, imp_country):
    slots, side = flows.shape[0], flows.shape[1]
    n_exp, n_imp = mesh_shape
    rows, cols = exp_country.shape[0], imp_country.shape[0]
    lay = Layout(rows * n_exp, cols * n_imp, side)
    vmem = pl.BlockSpec(memory_space=pltpu.VMEM)
    inputs = (
        flows,
        routing.reshape(-1),
        tile_block,
        exp_country.reshape(-1, 1, side),
        imp_country.reshape(-1, 1, side),
    )
    inputs = tuple(pltpu.with_memory_space_constraint(x, pltpu.HBM) for x in inputs)
    homes = [pltpu.VMEM, pltpu.SMEM, pltpu.SMEM, pltpu.VMEM, pltpu.VMEM]
    parts = pl.pallas_call(
        functools.partial(local_kernel, lay, slots),
        out_shape=[jax.ShapeDtypeStruct((lay.share, LANES), f32)] * 2,
        in_specs=[pl.BlockSpec(memory_space=pltpu.HBM)] * 5,
        out_specs=[vmem] * 2,
        scratch_shapes=[pltpu.VMEM((2 * lay.share, LANES), f32)]
        + [space(x.shape, x.dtype) for space, x in zip(homes, inputs)]
        + [pltpu.SemaphoreType.DMA((5 + slots,))],
        compiler_params=pltpu.CompilerParams(vmem_limit_bytes=VMEM_BYTES),
        name="local_sums",
    )(*inputs)
    mine = parts[0] + swap(parts[1], n_exp, n_imp, 1, 0)
    for bit in powers(1, n_imp):
        mine = mine + swap(mine, n_exp, n_imp, 1, bit)
    for bit in powers(2, n_exp):
        mine = mine + swap(mine, n_exp, n_imp, bit | 1, 0)
    shares = (mine, swap(mine, n_exp, n_imp, 1, 0))
    high = 16
    a, b, g = pl.pallas_call(
        functools.partial(solve_kernel, lay),
        out_shape=(
            jax.ShapeDtypeStruct((rows,), f32),
            jax.ShapeDtypeStruct((cols,), f32),
            jax.ShapeDtypeStruct((NCE, NCI), f32),
        ),
        in_specs=[vmem] * 2,
        out_specs=(vmem, vmem, vmem),
        scratch_shapes=[
            pltpu.VMEM((2 * lay.share, LANES), f32),
            pltpu.VMEM((lay.na, LANES), bf16),
            pltpu.VMEM((lay.nb, LANES), bf16),
            pltpu.VMEM((high * lay.na // LANES, LANES), f32),
            pltpu.VMEM((high * lay.nb // LANES, LANES), f32),
            pltpu.VMEM((lay.na // LANES, LANES), f32),
            pltpu.VMEM((lay.nb // LANES, LANES), f32),
            pltpu.VMEM((8, LANES), f32),
        ],
        compiler_params=pltpu.CompilerParams(vmem_limit_bytes=VMEM_BYTES),
        name="solve",
    )(*shares)
    return a, b, g


def solution(mesh):
    placed = (
        P(("exp", "imp"), None, None),
        P(("exp", "imp"), None, None),
        P(("exp", "imp")),
        P("exp"),
        P("imp"),
    )
    return jax.shard_map(
        functools.partial(per_device, (mesh.shape["exp"], mesh.shape["imp"])),
        mesh=mesh,
        in_specs=placed,
        out_specs=(P("exp"), P("imp"), P()),
        check_vma=False,
    )
```
